128 devices in a mesh: row: 16 (over x, z), col: 8 (over y, core).
Axes of the slice: x: 4, y: 4, z: 4, core: 2. Of those that a mesh axis runs over, the one named last changes fastest.
Arguments:
- pair_repr: bfloat16 [1536, 1536, 128], P('row', 'col'), may hold values from -6 to 6
- pair_gain: float32 [128], replicated, may hold values from 0.1 to 1.9
- proj_weight: bfloat16 [128, 16], replicated, may hold values from -0.5 to 0.5
- query_weight: bfloat16 [128, 16], replicated, may hold values from -0.5 to 0.5
- key_weight: bfloat16 [128, 16], replicated, may hold values from -0.5 to 0.5
- mlp_first: bfloat16 [16, 16], replicated, may hold values from -1.5 to 1.5
- mlp_second: bfloat16 [16, 16], replicated, may hold values from -1.5 to 1.5
- mlp_third: bfloat16 [16, 16], replicated, may hold values from -1.5 to 1.5
- atom_feats: bfloat16 [32768, 128], P(('row', 'col')), may hold values from -6 to 6
- token_counts: int32 [16, 96], P('row'), may hold values from 1 to 23, 2048 in all within a row
- key_start: int32 [1024], P(('row', 'col')), may hold values from -96 to 0, as said below
- pair_cotangent: bfloat16 [32768, 2048], P(('row', 'col')), may hold values from -6 to 6
Outputs:
- pair_grad: bfloat16 [1536, 1536, 128], P('row', 'col')
- atom_grad: bfloat16 [32768, 128], P(('row', 'col'))
- proj_grad: float32 [128, 16], replicated
The draws below stay inside these ranges and needn't reach their ends.
Inputs may be any that keep to these rules, and one draw needn't show every extreme that they name: `token_counts`: each row of counts sums to 2048; each row's largest count is 23. `key_start`: every query block lies inside its key window.
All inputs are finite; a program needn't handle non-finite values.
Results may differ from the reference program's by a relative error of at most 0.0038.
Values may be sent and summed in bfloat16 or wider, within the bound.
A program may use at most 128 MiB of HBM per device.

```python
import math
import jax
import jax.numpy as jnp
import numpy as np
from jax import lax

CP = 128
CA = 16
CATOM = 128
QBLK = 32
KWIN = 128
MOST = 23
TOK_ROW = 96
ATOM_DEV = 256
TOKENS = 1536
ROW_BLOCKS = 16
ROW_ATOMS = 2048
NATOM = 32768
NBLK = 1024
N_ROW = 16
N_COL = 8


def draw_key_start(key, part):
    key = jax.random.fold_in(key, 11)
    first_key, second_key = jax.random.split(key)
    starts = jax.random.randint(first_key, (NBLK,), QBLK - KWIN, 1)
    picks = jax.random.permutation(second_key, NBLK)
    starts = starts.at[picks[0]].set(QBLK - KWIN)
    starts = starts.at[picks[1]].set(0)
    return starts.astype(jnp.int32)


def steps_of(own_key, dims, pieces, least, largest):
    def one(axis_at, parts):
        draws = jax.random.uniform(jax.random.fold_in(jax.random.fold_in(own_key, 6), axis_at), (parts,), jnp.float32, least / len(pieces), largest / len(pieces))
        return jnp.repeat(jnp.exp(draws), dims[axis_at] // parts).reshape((-1,) + (1,) * (len(dims) - axis_at - 1))

    level = one(*pieces[0])
    for cut in pieces[1:]:
        level = level * one(*cut)
    return level


def split_up(number_of, total, bound, slope):
    portions = [(1 << 20) // math.isqrt(rank ** slope) + 1 for rank in range(2, number_of + 1)]
    spare, holding = total - bound - (number_of - 1), [1] * (number_of - 1)
    while spare > 0:
        free = [i for i in range(number_of - 1) if holding[i] < bound]
        pool, budget = sum([portions[i] for i in free]), spare
        for i in free:
            addition = min(bound - holding[i], max(1, budget * portions[i] // pool), spare)
            holding[i] = holding[i] + addition
            spare = spare - addition
    return np.array([bound] + holding)


def uneven(rng, amount, total, bound, skew):
    if amount == 2:
        one = jax.random.randint(rng, (), max(1, total - bound), min(bound, total - 1) + 1)
        return jnp.stack([one, total - one])
    sizes = jnp.asarray(split_up(amount, total, bound, skew), jnp.int32)
    pairs = (amount - 1) // 2
    donor, taker = sizes[1:1 + 2 * pairs:2], sizes[2:2 + 2 * pairs:2]
    room = jnp.minimum(donor - 1, bound - taker)
    moved = jax.random.randint(jax.random.fold_in(rng, 1), (pairs,), 0, 1 << 20) % (room + 1)
    sizes = sizes.at[1:1 + 2 * pairs:2].set(donor - moved).at[2:2 + 2 * pairs:2].set(taker + moved)
    return sizes[jax.random.permutation(jax.random.fold_in(rng, 2), amount)]


def gaussian(stream_key, shape, scale, reach, cuts=(), kind=jnp.bfloat16):
    values = scale * jax.random.normal(stream_key, shape, jnp.float32)
    if cuts:
        values = values * steps_of(stream_key, shape, cuts, -0.22, 0.18)
    return jnp.clip(values, -reach, reach).astype(kind)


def setup_inputs(seed: int = 0) -> dict:
    key_of = jax.random.split(jax.random.key(seed), 13)
    pair_repr = gaussian(key_of[0], (TOKENS, TOKENS, CP), 1.0, 6.0, ((0, 16), (1, 8)))
    pair_gain = jnp.clip(1.0 + 0.18 * jax.random.normal(key_of[1], (CP,), jnp.float32), 0.1, 1.9)
    proj_weight = gaussian(key_of[2], (CP, CA), CP ** -0.5, 0.5)
    query_weight = gaussian(key_of[3], (CATOM, CA), CATOM ** -0.5, 0.5)
    key_weight = gaussian(key_of[4], (CATOM, CA), CATOM ** -0.5, 0.5)
    mlp_first = gaussian(key_of[5], (CA, CA), CA ** -0.5, 1.5)
    mlp_second = gaussian(key_of[6], (CA, CA), CA ** -0.5, 1.5)
    mlp_third = gaussian(key_of[7], (CA, CA), CA ** -0.5, 1.5)
    atom_feats = gaussian(key_of[8], (NATOM, CATOM), 1.0, 6.0, ((0, 128),))
    token_counts = jax.vmap(lambda own: uneven(own, TOK_ROW, ROW_ATOMS, MOST, 2))(jax.random.split(key_of[9], ROW_BLOCKS)).reshape((ROW_BLOCKS, TOK_ROW)).astype(jnp.int32)
    key_start = draw_key_start(jax.random.fold_in(key_of[12], 71), 0)
    pair_cotangent = gaussian(key_of[11], (NATOM, KWIN * CA), 1.0, 6.0, ((0, 128),))
    return dict(pair_repr=pair_repr, pair_gain=pair_gain, proj_weight=proj_weight, query_weight=query_weight, key_weight=key_weight, mlp_first=mlp_first, mlp_second=mlp_second, mlp_third=mlp_third, atom_feats=atom_feats, token_counts=token_counts, key_start=key_start, pair_cotangent=pair_cotangent)


def silu_slope(values):
    sigma = jax.nn.sigmoid(values)
    return sigma * (1.0 + values * (1.0 - sigma))

def norm_rows(values, gain_vec):
    floats = values.astype(jnp.float32)
    centre = floats - lax.optimization_barrier(jnp.mean(floats, axis=-1, keepdims=True))
    spread = lax.optimization_barrier(jnp.mean(centre * centre, axis=-1, keepdims=True))
    inv_scale = lax.rsqrt(spread + 1e-05)
    hatted = centre * inv_scale
    normed = (hatted * gain_vec).astype(jnp.bfloat16)
    return (hatted, inv_scale, normed)

def norm_back(grad_normed, hatted, inv_scale, gain_vec):
    scaled = grad_normed * gain_vec
    first_mean = lax.optimization_barrier(jnp.mean(scaled, axis=-1, keepdims=True))
    second_mean = lax.optimization_barrier(jnp.mean(scaled * hatted, axis=-1, keepdims=True))
    return (inv_scale * (scaled - first_mean - hatted * second_mean)).astype(jnp.bfloat16)

def pair_backward(start, cotangent, first_w, second_w, third_w):
    top = lax.Precision.HIGHEST
    hidden_one = jnp.einsum('qkc,cd->qkd', jax.nn.silu(start), first_w, precision=top)
    hidden_two = jnp.einsum('qkc,cd->qkd', jax.nn.silu(hidden_one), second_w, precision=top)
    back_two = jnp.einsum('qkd,cd->qkc', cotangent, third_w, precision=top) * silu_slope(hidden_two)
    back_one = jnp.einsum('qkd,cd->qkc', back_two, second_w, precision=top) * silu_slope(hidden_one)
    back_zero = jnp.einsum('qkd,cd->qkc', back_one, first_w, precision=top) * silu_slope(start)
    return cotangent + back_zero

def band_slab(pair_repr, row_block):
    tok_rows = TOK_ROW
    slab_rows = pair_repr[row_block * tok_rows:(row_block + 1) * tok_rows]
    padded = jnp.pad(slab_rows, ((0, 0), (tok_rows, tok_rows), (0, 0)))
    return padded[:, row_block * tok_rows:row_block * tok_rows + 3 * tok_rows]

def reference(pair_repr, pair_gain, proj_weight, query_weight, key_weight, mlp_first, mlp_second, mlp_third, atom_feats, token_counts, key_start, pair_cotangent):
    top = lax.Precision.HIGHEST
    tok_rows = TOK_ROW
    band_width = 3 * tok_rows
    channels = CP
    pair_width = CA
    row_atoms = ATOM_DEV * N_COL
    projections = []
    for row_block in range(N_ROW):
        slab = band_slab(pair_repr, row_block)
        hatted, inv_scale, normed = norm_rows(slab, pair_gain)
        projected = jnp.dot(normed.reshape(-1, channels), proj_weight, preferred_element_type=jnp.float32)
        projections.append(projected.astype(jnp.bfloat16))
    band_proj = jnp.stack(projections).reshape(-1, pair_width)
    ends = jnp.cumsum(token_counts, axis=1)
    local_atoms = jnp.arange(row_atoms, dtype=jnp.int32)
    tok_local = lax.optimization_barrier(jnp.sum((ends[:, None, :] <= local_atoms[None, :, None]).astype(jnp.int32), axis=2))
    tok_global = (tok_local + jnp.arange(N_ROW, dtype=jnp.int32)[:, None] * tok_rows).reshape(-1)
    atom_index = jnp.arange(NATOM, dtype=jnp.int32)
    block_of = atom_index // QBLK
    key_atom = (block_of * QBLK + key_start[block_of])[:, None] + jnp.arange(KWIN, dtype=jnp.int32)[None, :]
    key_valid = (key_atom >= 0) & (key_atom < NATOM)
    key_clip = jnp.clip(key_atom, 0, NATOM - 1).astype(jnp.int32)
    row_of = atom_index // row_atoms
    query_tok = tok_global - row_of * tok_rows
    key_tok = jnp.clip(tok_global[key_clip] - (row_of[:, None] - 1) * tok_rows, 0, band_width - 1)
    pair_slot = ((row_of * tok_rows + query_tok)[:, None] * band_width + key_tok).astype(jnp.int32)
    zp_pairs = band_proj[pair_slot.reshape(-1)].astype(jnp.float32).reshape(NATOM, KWIN, pair_width)
    activated = jax.nn.silu(atom_feats.astype(jnp.float32)).astype(jnp.bfloat16)
    query_terms = jnp.dot(activated, query_weight, preferred_element_type=jnp.float32)
    key_terms = jnp.dot(activated, key_weight, preferred_element_type=jnp.float32)
    start = zp_pairs + query_terms[:, None, :] + key_terms[key_clip]
    cotangent = pair_cotangent.reshape(NATOM, KWIN, pair_width).astype(jnp.float32) * key_valid[:, :, None].astype(jnp.float32)
    back = pair_backward(start, cotangent, mlp_first.astype(jnp.float32), mlp_second.astype(jnp.float32), mlp_third.astype(jnp.float32))
    flat_back = back.reshape(-1, pair_width)
    band_grad = jax.ops.segment_sum(flat_back, pair_slot.reshape(-1), num_segments=N_ROW * tok_rows * band_width)
    band_grad = band_grad.reshape(N_ROW, tok_rows, band_width, pair_width)
    query_grad = lax.optimization_barrier(jnp.sum(back, axis=1))
    key_grad = jax.ops.segment_sum(flat_back, key_clip.reshape(-1), num_segments=NATOM)
    atom_sum = jnp.dot(query_grad, query_weight.astype(jnp.float32).T, precision=top) + jnp.dot(key_grad, key_weight.astype(jnp.float32).T, precision=top)
    atom_grad = (atom_sum * silu_slope(atom_feats.astype(jnp.float32))).astype(jnp.bfloat16)
    proj_grad = jnp.zeros((channels, pair_width), jnp.float32)
    row_outputs = []
    for row_block in range(N_ROW):
        slab = band_slab(pair_repr, row_block)
        hatted, inv_scale, normed = norm_rows(slab, pair_gain)
        block_grad = band_grad[row_block]
        grad_normed = jnp.einsum('ijc,dc->ijd', block_grad, proj_weight.astype(jnp.float32), precision=top)
        slab_grad = norm_back(grad_normed, hatted, inv_scale, pair_gain)
        whole_row = jnp.zeros((tok_rows, TOKENS + 2 * tok_rows, channels), jnp.bfloat16)
        whole_row = whole_row.at[:, row_block * tok_rows:row_block * tok_rows + band_width].set(slab_grad)
        row_outputs.append(whole_row[:, tok_rows:tok_rows + TOKENS])
        proj_grad = proj_grad + jnp.dot(normed.reshape(-1, channels).T, block_grad.reshape(-1, pair_width), precision=top)
    pair_grad = jnp.concatenate(row_outputs, axis=0)
    return (pair_grad, atom_grad, proj_grad)
```

```python
import jax
import jax.numpy as jnp
from jax import lax
from jax.experimental import pallas as pl
from jax.experimental.pallas import tpu as pltpu
from jax.sharding import PartitionSpec as P

F32 = jnp.float32
BF16 = jnp.bfloat16
MESH = pl.DeviceIdType.MESH

N_ROW = 16
N_COL = 8
TOK = 96
COLS = 192
CP = 128
CA = 16
QBLK = 32
KWIN = 128
MOST = 23
ATOMS = 256
ROW_ATOMS = 2048
SLACK = TOK * MOST - ROW_ATOMS
HALO = KWIN - QBLK
EXT = ATOMS + 2 * HALO
NBLK = ATOMS // QBLK
LANES = QBLK * CA
KEYS = 48
QTOK = 32
GROUPS = TOK // 8
VMEM_LIMIT = 56 * 1024 * 1024


def key_base(col):
    return 16 * ((11 * col - 5 + 16) // 16) - 16


def query_base(col):
    return jnp.minimum(8 * ((11 * col) // 8), TOK - QTOK)


def query_base_static(col):
    return min(8 * ((11 * col) // 8), TOK - QTOK)


def iota(shape, dim):
    return lax.broadcasted_iota(jnp.int32, shape, dim)


def dot(a, b):
    return jnp.dot(a, b, preferred_element_type=F32)


def dot_nt(a, b):
    return lax.dot_general(a, b, (((1,), (1,)), ((), ())), preferred_element_type=F32)


def dot_tn(a, b):
    return lax.dot_general(a, b, (((0,), (0,)), ((), ())), preferred_element_type=F32)


def split(x):
    high = x.astype(BF16)
    low = (x - high.astype(F32)).astype(BF16)
    return high, low


def dot_split(x, w):
    high, low = split(x)
    return dot(high, w) + dot(low, w)


def sigmoid(x):
    return 0.5 * jnp.tanh(0.5 * x) + 0.5


def mesh_place():
    row = lax.axis_index("row")
    col = lax.axis_index("col")
    return row, col


def normalise(block):
    floats = block.astype(F32)
    centre = floats - jnp.mean(floats, axis=-1, keepdims=True)
    spread = jnp.mean(centre * centre, axis=-1, keepdims=True)
    inv_scale = lax.rsqrt(spread + 1e-05)
    return centre * inv_scale, inv_scale


def channel_eye(rows):
    return ((iota((rows, CA), 0) & (CA - 1)) == iota((rows, CA), 1)).astype(F32).astype(BF16)


def spread_projection(proj):
    eye = channel_eye(CP)
    wide = dot_nt(proj, eye)
    lane = iota((CP, CP), 1) // CA
    return jnp.concatenate(
        [jnp.where(lane == i, wide, 0.0).astype(BF16) for i in range(8)], axis=0
    )


def spread_projection_t(proj):
    eye = channel_eye(CP)
    tall = dot_nt(eye, proj)
    row = iota((CP, CP), 0) // CA
    return jnp.concatenate(
        [jnp.where(row == i, tall, 0.0).astype(BF16) for i in range(8)], axis=1
    )


def window_column(group, odd):
    first = 16 * ((8 * group - 13 + 16) // 16) - 16
    return jnp.clip(first + TOK * odd, 0, COLS - KEYS)


def corner_place(odd):
    return 80 * odd, 176 * (1 - odd)


def owners(row, col):
    odd = row % 2
    half = row // 2
    is_main = col == half
    is_corner = jnp.where(odd == 0, col == half - 1, col == half + 1)
    return odd, is_main, is_corner


def project_kernel(pair_ref, gain_ref, proj_ref, zrow_ref, corner_ref, band, cband, sems, csem):
    row, col = mesh_place()
    odd, is_main, is_corner = owners(row, col)

    def window_copy(group):
        first = pl.multiple_of(window_column(group, odd), 16)
        return pltpu.make_async_copy(
            pair_ref.at[pl.ds(8 * group, 8), pl.ds(first, KEYS)], band.at[group], sems.at[group]
        )

    @pl.when(is_main)
    def _():
        for group in range(GROUPS):
            window_copy(group).start()
        zrow_ref[...] = jnp.zeros_like(zrow_ref)
        spread_w = spread_projection(proj_ref[...])
        gain = gain_ref[...]
        for group in range(GROUPS):
            window_copy(group).wait()
            hatted, _ = normalise(band[group])
            normed = (hatted * gain).astype(BF16)
            flat = jnp.concatenate([normed[i] for i in range(8)], axis=1)
            at = pl.multiple_of(window_column(group, odd) - TOK * odd + 16, 16)
            zrow_ref[pl.ds(at, KEYS), 128 * group : 128 * group + 128] = dot(
                flat, spread_w
            ).astype(BF16)

    @pl.when(is_corner)
    def _():
        first_row, first_col = corner_place(odd)
        copy = pltpu.make_async_copy(
            pair_ref.at[pl.ds(first_row, 16), pl.ds(pl.multiple_of(first_col, 16), 16)],
            cband,
            csem,
        )
        copy.start()
        spread_w = spread_projection(proj_ref[...])
        copy.wait()
        hatted, _ = normalise(cband[...])
        normed = (hatted * gain_ref[...]).astype(BF16)
        for part in range(2):
            flat = jnp.concatenate([normed[8 * part + i] for i in range(8)], axis=1)
            corner_ref[:, 128 * part : 128 * part + 128] = dot(flat, spread_w).astype(BF16)


def project_band(pair_repr, gain, proj):
    return pl.pallas_call(
        project_kernel,
        out_shape=(
            jax.ShapeDtypeStruct((128, TOK * CA), BF16),
            jax.ShapeDtypeStruct((16, 256), BF16),
        ),
        in_specs=[
            pl.BlockSpec(memory_space=pl.ANY),
            pl.BlockSpec(memory_space=pltpu.VMEM),
            pl.BlockSpec(memory_space=pltpu.VMEM),
        ],
        out_specs=(
            pl.BlockSpec(memory_space=pltpu.VMEM),
            pl.BlockSpec(memory_space=pltpu.VMEM),
        ),
        scratch_shapes=[
            pltpu.VMEM((GROUPS, 8, KEYS, CP), BF16),
            pltpu.VMEM((16, 16, CP), BF16),
            pltpu.SemaphoreType.DMA((GROUPS,)),
            pltpu.SemaphoreType.DMA,
        ],
        compiler_params=pltpu.CompilerParams(vmem_limit_bytes=VMEM_LIMIT),
        name="project_band",
    )(pair_repr, gain, proj)


def neighbours(row, col):
    ahead = (
        jnp.where(col == N_COL - 1, lax.rem(row + 1, N_ROW), row),
        lax.rem(col + 1, N_COL),
    )
    behind = (
        jnp.where(col == 0, lax.rem(row + N_ROW - 1, N_ROW), row),
        lax.rem(col + N_COL - 1, N_COL),
    )
    return ahead, behind


def greet_row_and_neighbours(row, col):
    barrier = pltpu.get_barrier_semaphore()
    ahead, behind = neighbours(row, col)
    for step in range(1, N_COL):
        pl.semaphore_signal(
            barrier, inc=1, device_id=(row, lax.rem(col + step, N_COL)), device_id_type=MESH
        )

    @pl.when(col == 0)
    def _():
        pl.semaphore_signal(barrier, inc=1, device_id=behind, device_id_type=MESH)

    @pl.when(col == N_COL - 1)
    def _():
        pl.semaphore_signal(barrier, inc=1, device_id=ahead, device_id_type=MESH)

    extra = jnp.where(col == 0, 1, 0) + jnp.where(col == N_COL - 1, 1, 0)
    pl.semaphore_wait(barrier, N_COL - 1 + extra)
    return ahead, behind


def scatter_kernel(
    zrow_ref,
    corner_ref,
    feats_ref,
    counts_ref,
    patch_ref,
    patch_corner_ref,
    feats_before_ref,
    feats_after_ref,
    counts_before_ref,
    counts_after_ref,
    send_z,
    recv_z,
    send_c,
    recv_c,
    send_h,
    recv_h,
    local_sem,
):
    row, col = mesh_place()
    odd, is_main, is_corner = owners(row, col)
    half = row // 2
    ahead, behind = greet_row_and_neighbours(row, col)

    def z_part(target):
        base = key_base(target)
        return zrow_ref.at[
            pl.ds(base + 16, KEYS),
            pl.ds(query_base_static(target) * CA, QTOK * CA),
        ]

    def z_copy(target):
        return pltpu.make_async_remote_copy(
            src_ref=z_part(target),
            dst_ref=patch_ref,
            send_sem=send_z.at[target],
            recv_sem=recv_z,
            device_id=(row, target),
            device_id_type=MESH,
        )

    def z_local(target):
        return pltpu.make_async_copy(z_part(target), patch_ref, local_sem.at[0])

    corner_target = jnp.where(odd == 0, 0, N_COL - 1)

    def corner_copy():
        return pltpu.make_async_remote_copy(
            src_ref=corner_ref,
            dst_ref=patch_corner_ref,
            send_sem=send_c,
            recv_sem=recv_c,
            device_id=(row, corner_target),
            device_id_type=MESH,
        )

    corner_local = pltpu.make_async_copy(corner_ref, patch_corner_ref, local_sem.at[1])

    @pl.when(is_main)
    def _():
        for target in range(N_COL):

            @pl.when(col != target)
            def _():
                z_copy(target).start()

            @pl.when(col == target)
            def _():
                z_local(target).start()

    @pl.when(is_corner & (col != corner_target))
    def _():
        corner_copy().start()

    @pl.when(is_corner & (col == corner_target))
    def _():
        corner_local.start()

    halos = []
    for at, (src, dst, device) in enumerate(
        (
            (feats_ref.at[pl.ds(ATOMS - HALO, HALO)], feats_before_ref, ahead),
            (feats_ref.at[pl.ds(0, HALO)], feats_after_ref, behind),
            (counts_ref, counts_before_ref, ahead),
            (counts_ref, counts_after_ref, behind),
        )
    ):
        copy = pltpu.make_async_remote_copy(
            src_ref=src,
            dst_ref=dst,
            send_sem=send_h.at[at],
            recv_sem=recv_h.at[at],
            device_id=device,
            device_id_type=MESH,
        )
        copy.start()
        halos.append(copy)

    for copy in halos:
        copy.wait()

    @pl.when(is_main)
    def _():
        for target in range(N_COL):

            @pl.when(col != target)
            def _():
                z_copy(target).wait_send()

            @pl.when(col == target)
            def _():
                z_local(target).wait()

    @pl.when(jnp.logical_not(is_main))
    def _():
        z_copy(0).wait_recv()

    @pl.when(is_corner & (col != corner_target))
    def _():
        corner_copy().wait_send()

    @pl.when(is_corner & (col == corner_target))
    def _():
        corner_local.wait()

    owner = jnp.where(odd == 0, half - 1, half + 1)
    has_corner = (owner >= 0) & (owner < N_COL) & (owner != corner_target)

    @pl.when((col == corner_target) & has_corner)
    def _():
        corner_copy().wait_recv()


def scatter_band(zrow, corner, feats, counts):
    any_spec = pl.BlockSpec(memory_space=pl.ANY)
    return pl.pallas_call(
        scatter_kernel,
        out_shape=(
            jax.ShapeDtypeStruct((KEYS, QTOK * CA), BF16),
            jax.ShapeDtypeStruct((16, 256), BF16),
            jax.ShapeDtypeStruct((HALO, CP), BF16),
            jax.ShapeDtypeStruct((HALO, CP), BF16),
            jax.ShapeDtypeStruct((1, TOK), jnp.int32),
            jax.ShapeDtypeStruct((1, TOK), jnp.int32),
        ),
        in_specs=[any_spec] * 4,
        out_specs=(any_spec,) * 6,
        scratch_shapes=[
            pltpu.SemaphoreType.DMA((N_COL,)),
            pltpu.SemaphoreType.DMA,
            pltpu.SemaphoreType.DMA,
            pltpu.SemaphoreType.DMA,
            pltpu.SemaphoreType.DMA((4,)),
            pltpu.SemaphoreType.DMA((4,)),
            pltpu.SemaphoreType.DMA((2,)),
        ],
        compiler_params=pltpu.CompilerParams(
            collective_id=0, has_side_effects=True, vmem_limit_bytes=VMEM_LIMIT
        ),
        name="scatter_band",
    )(zrow, corner, feats, counts)


def swap_atoms(block):
    row = iota((8, 128), 0)
    lane = iota((8, 128), 1)
    turn = (lane + CA * row) % 128
    pick = (row + 8 - lane // CA) % 8
    pieces = []
    for at in range(block.shape[0] // 8):
        piece = jnp.take_along_axis(block[8 * at : 8 * at + 8], turn, axis=1)
        piece = jnp.take_along_axis(piece, pick, axis=0)
        pieces.append(jnp.take_along_axis(piece, turn, axis=1))
    return pieces


def pair_kernel(
    start_ref,
    cot_ref,
    feats_ref,
    feats_before_ref,
    feats_after_ref,
    counts_ref,
    counts_before_ref,
    counts_after_ref,
    patch_ref,
    patch_corner_ref,
    query_w_ref,
    key_w_ref,
    first_w_ref,
    second_w_ref,
    third_w_ref,
    key_out_ref,
    query_out_ref,
    token_out_ref,
    blank_ref,
    act_ext,
    lhs,
    rhs,
    query_high,
    query_low,
    cot,
    state,
    mixers,
    key_tiled,
    query_tiled,
    slot_from,
    slot_to,
    hot_ref,
    zeros,
    zero_sem,
):
    row, col = mesh_place()
    odd = row % 2
    zeros[...] = jnp.zeros_like(zeros)
    fills = [
        pltpu.make_async_copy(zeros, blank_ref.at[pl.ds(8 * g, 8)], zero_sem.at[g])
        for g in range(GROUPS)
    ]
    for fill in fills:
        fill.start()

    eye = channel_eye(LANES)
    eye16 = eye[:256]
    same = (iota((256, 256), 0) // CA) == (iota((256, 256), 1) // CA)

    def mixer(weight, flip):
        left = dot_nt(eye16, weight) if flip else dot(eye16, weight)
        wide = dot_nt(left.astype(BF16), eye16)
        return jnp.where(same, wide, 0.0).astype(BF16)

    mixers[0] = mixer(first_w_ref[...], False)
    mixers[1] = mixer(second_w_ref[...], False)
    mixers[2] = mixer(third_w_ref[...], True)
    mixers[3] = mixer(second_w_ref[...], True)
    mixers[4] = mixer(first_w_ref[...], True)
    key_tiled[...] = dot_nt(eye, key_w_ref[...]).astype(BF16)
    query_tiled[...] = dot_nt(eye, query_w_ref[...]).astype(BF16)
    rhs[128:256, :] = dot_nt(key_w_ref[...], eye).astype(BF16)
    rhs[112:128, :] = jnp.zeros((16, LANES), BF16)

    def activate(feats):
        floats = feats.astype(F32)
        return floats * jax.nn.sigmoid(floats)

    own_act = activate(feats_ref[...]).astype(BF16)
    act_ext[0:HALO] = activate(feats_before_ref[...])
    act_ext[HALO : HALO + ATOMS] = activate(feats_ref[...])
    act_ext[HALO + ATOMS : EXT] = activate(feats_after_ref[...])

    lane_index = iota((QBLK, LANES), 1)
    lane_atom = 8 * (lane_index // 128) + ((8 - (lane_index % 128) // CA) % 8)
    lane_is_row = lane_atom == iota((QBLK, LANES), 0)
    query_wide = dot_nt(query_w_ref[...], eye).astype(BF16)
    for block in range(NBLK):
        terms = dot(own_act[QBLK * block : QBLK * block + QBLK], query_wide)
        high, low = split(jnp.where(lane_is_row, terms, 0.0))
        query_high[QBLK * block : QBLK * block + QBLK] = high
        query_low[QBLK * block : QBLK * block + QBLK] = low

    base = key_base(col)
    own = counts_ref[...].astype(F32)
    before = counts_before_ref[...].astype(F32)
    after = counts_after_ref[...].astype(F32)

    def rows_of(counts, rows):
        return jnp.broadcast_to(counts, (rows, TOK)).astype(BF16)

    def as_mask(flag):
        return jnp.where(flag, 1.0, 0.0).astype(BF16)

    def lane_bounds(offset):
        token = iota((TOK, 128), 1) + (base + offset)
        index = iota((TOK, 128), 0)
        total = dot(rows_of(own, 8), as_mask(index < token))
        total += dot(rows_of(after, 8), as_mask(index + TOK < token))
        return total - dot(rows_of(before, 8), as_mask(index - TOK >= token))

    def column_bounds(offset):
        token = iota((KEYS, TOK), 0) + (base + offset)
        index = iota((KEYS, TOK), 1)
        total = dot_nt(as_mask(index < token), rows_of(own, 128))
        total += dot_nt(as_mask(index + TOK < token), rows_of(after, 128))
        return total - dot_nt(as_mask(index - TOK >= token), rows_of(before, 128))

    lane = iota((8, 128), 1)
    far = 1.0e6
    lane_from = jnp.where(lane < 48, lane_bounds(0), jnp.where(lane < 112, -far, far))[0:1]
    lane_to = jnp.where(lane < 48, lane_bounds(1), jnp.where(lane < 112, far, -far))[0:1]
    column_from = column_bounds(0)
    column_to = column_bounds(1)

    first_query = query_base(col)
    slot = iota((LANES, TOK), 0) // CA + first_query
    slot_index = iota((LANES, TOK), 1)
    own_rows = rows_of(own, 128)
    slot_from[...] = dot_nt(as_mask(slot_index < slot), own_rows)
    slot_to[...] = dot_nt(as_mask(slot_index < slot + 1), own_rows)

    def swap_step(chunk, carry):
        at = pl.multiple_of(128 * chunk, 128)
        turned = swap_atoms(cot_ref[:, pl.ds(at, 128)].astype(F32))
        for block in range(NBLK):
            to = pl.multiple_of(128 * block + 8 * chunk, 8)
            for part in range(4):
                cot[pl.ds(to, 8), 128 * part : 128 * part + 128] = turned[4 * block + part]
        return carry

    lax.fori_loop(0, ATOMS * 8 // 128, swap_step, 0)

    has_before = (col == 0) & (odd == 0) & (row > 0)
    has_after = (col == N_COL - 1) & (odd == 1) & (row < N_ROW - 1)
    patch = patch_ref[...]
    corner = patch_corner_ref[...]
    head = jnp.where(has_before, corner, patch[0:16, 0:256])
    tail = jnp.where(has_after, corner, patch[32:48, 256:512])
    patch_ref[0:16, 0:256] = head
    patch_ref[32:48, 256:512] = tail

    lane_atom_row = (
        8 * (iota((1, LANES), 1) // 128) + ((8 - (iota((1, LANES), 1) % 128) // CA) % 8)
    ).astype(F32)
    channel_match = (iota((256, 128), 0) % CA) == (iota((256, 128), 1) % CA)

    def block_place(block):
        first = col * ATOMS + block * QBLK
        token = 8 * (first // (8 * MOST)) - first_query
        return first, pl.multiple_of(token * CA, 128)

    def query_hot(block):
        first, at = block_place(block)
        low = slot_from[pl.ds(at, 256), :]
        high = slot_to[pl.ds(at, 256), :]
        parts = []
        for part in range(4):
            atom = lane_atom_row[:, 128 * part : 128 * part + 128] + first.astype(F32)
            hot = (low <= atom) & (atom < high) & channel_match
            parts.append(jnp.where(hot, 1.0, 0.0).astype(BF16))
        return jnp.concatenate(parts, axis=1)

    def key_first(block):
        return col * ATOMS + block * QBLK + start_ref[block]

    def start_step(block, carry):
        _, at = block_place(block)
        hot = query_hot(block)
        hot_ref[block] = hot
        window = start_ref[block] + block * QBLK + HALO
        atom = (iota((KWIN, 128), 0) + key_first(block)).astype(F32)
        lhs[:, 0:128] = as_mask((lane_from <= atom) & (atom < lane_to))
        lhs[:, 128:256] = act_ext[pl.ds(window, KWIN), :].astype(BF16)
        rhs[0:48, :] = dot(patch_ref[:, pl.ds(at, 256)], hot).astype(BF16)
        mine = pl.multiple_of(block * QBLK, QBLK)
        rhs[48:80, :] = query_high[pl.ds(mine, QBLK), :]
        rhs[80:112, :] = query_low[pl.ds(mine, QBLK), :]
        state[pl.ds(pl.multiple_of(block * KWIN, KWIN), KWIN), :] = dot(lhs[...], rhs[...])
        return carry

    lax.fori_loop(0, NBLK, start_step, 0)

    atom_low = jnp.where(row == 0, 0, -ROW_ATOMS)
    atom_high = jnp.where(row == N_ROW - 1, ROW_ATOMS, 2 * ROW_ATOMS)

    def slope(value, sigma, act):
        return sigma + act - act * sigma

    def mlp_step(step, carry):
        pair = step // 2
        at = pl.multiple_of(256 * pair, 256)
        place = pl.ds(at, 256), pl.ds(pl.multiple_of(256 * (step % 2), 256), 256)
        value = state[place]
        index = iota((256, 256), 0)
        begin = jnp.where(index < KWIN, key_first(2 * pair), key_first(2 * pair + 1) - KWIN)
        atom = index + begin
        grad = jnp.where((atom >= atom_low) & (atom < atom_high), cot[place], 0.0)
        sig_0 = sigmoid(value)
        act_0 = value * sig_0
        one = dot_split(act_0, mixers[0])
        sig_1 = sigmoid(one)
        act_1 = one * sig_1
        two = dot_split(act_1, mixers[1])
        sig_2 = sigmoid(two)
        back = dot(grad.astype(BF16), mixers[2]) * slope(two, sig_2, two * sig_2)
        back = dot_split(back, mixers[3]) * slope(one, sig_1, act_1)
        back = dot_split(back, mixers[4]) * slope(value, sig_0, act_0)
        state[place] = grad + back
        return carry

    lax.fori_loop(0, 8, mlp_step, 0)

    key_out_ref[...] = jnp.zeros_like(key_out_ref)
    token_out_ref[...] = jnp.zeros_like(token_out_ref)

    def sum_step(block, carry):
        _, at = block_place(block)
        window = start_ref[block] + block * QBLK + HALO
        back = state[pl.ds(pl.multiple_of(block * KWIN, KWIN), KWIN), :]
        high, low = split(back)
        key_out_ref[pl.ds(window, KWIN), :] += dot(high, key_tiled[...]) + dot(
            low, key_tiled[...]
        )
        over_keys = jnp.sum(back, axis=0, keepdims=True)
        over_keys = jnp.where(lane_is_row, over_keys, 0.0)
        mine = pl.multiple_of(block * QBLK, QBLK)
        query_out_ref[pl.ds(mine, QBLK), :] = dot_split(over_keys, query_tiled[...])
        atom = (iota((KEYS, 128), 1) + key_first(block)).astype(F32)
        key_hot = as_mask((column_from <= atom) & (atom < column_to))
        by_token = dot(key_hot, high) + dot(key_hot, low)
        high, low = split(by_token)
        hot = hot_ref[block]
        token_out_ref[:, pl.ds(at, 256)] += dot_nt(high, hot) + dot_nt(low, hot)
        return carry

    lax.fori_loop(0, NBLK, sum_step, 0)
    for fill in fills:
        fill.wait()


def atom_pairs(key_start, cot, feats, halo_feats, counts, halo_counts, patch, corner, weights):
    vmem = pl.BlockSpec(memory_space=pltpu.VMEM)
    return pl.pallas_call(
        pair_kernel,
        out_shape=(
            jax.ShapeDtypeStruct((EXT, CP), F32),
            jax.ShapeDtypeStruct((ATOMS, CP), F32),
            jax.ShapeDtypeStruct((KEYS, QTOK * CA), F32),
            jax.ShapeDtypeStruct((TOK, COLS, CP), BF16),
        ),
        in_specs=[pl.BlockSpec(memory_space=pltpu.SMEM)] + [vmem] * 14,
        out_specs=(vmem, vmem, vmem, pl.BlockSpec(memory_space=pl.ANY)),
        scratch_shapes=[
            pltpu.VMEM((EXT, CP), F32),
            pltpu.VMEM((KWIN, 256), BF16),
            pltpu.VMEM((256, LANES), BF16),
            pltpu.VMEM((ATOMS, LANES), BF16),
            pltpu.VMEM((ATOMS, LANES), BF16),
            pltpu.VMEM((NBLK * KWIN, LANES), F32),
            pltpu.VMEM((NBLK * KWIN, LANES), F32),
            pltpu.VMEM((5, 256, 256), BF16),
            pltpu.VMEM((LANES, CP), BF16),
            pltpu.VMEM((LANES, CP), BF16),
            pltpu.VMEM((LANES, 128), F32),
            pltpu.VMEM((LANES, 128), F32),
            pltpu.VMEM((NBLK, 256, LANES), BF16),
            pltpu.VMEM((8, COLS, CP), BF16),
            pltpu.SemaphoreType.DMA((GROUPS,)),
        ],
        compiler_params=pltpu.CompilerParams(vmem_limit_bytes=VMEM_LIMIT),
        name="atom_pairs",
    )(key_start, cot, feats, *halo_feats, counts, *halo_counts, patch, corner, *weights)


def gather_kernel(
    key_ref,
    token_ref,
    from_before_ref,
    from_after_ref,
    patches_ref,
    corner_ref,
    send_t,
    recv_t,
    send_c,
    recv_c,
    send_h,
    recv_h,
    local_sem,
):
    row, col = mesh_place()
    odd, is_main, is_corner = owners(row, col)
    half = row // 2
    ahead, behind = greet_row_and_neighbours(row, col)

    def token_copy(source):
        return pltpu.make_async_remote_copy(
            src_ref=token_ref,
            dst_ref=patches_ref.at[source],
            send_sem=send_t,
            recv_sem=recv_t.at[source],
            device_id=(row, half),
            device_id_type=MESH,
        )

    token_local = pltpu.make_async_copy(token_ref, patches_ref.at[col], local_sem.at[0])

    @pl.when(jnp.logical_not(is_main))
    def _():
        token_copy(col).start()

    @pl.when(is_main)
    def _():
        token_local.start()

    corner_source = jnp.where(odd == 0, 0, N_COL - 1)
    corner_owner = jnp.where(odd == 0, half - 1, half + 1)
    corner_exists = (corner_owner >= 0) & (corner_owner < N_COL)
    corner_part = token_ref.at[
        pl.ds(pl.multiple_of(32 * odd, 16), 16), pl.ds(pl.multiple_of(256 * odd, 256), 256)
    ]
    corner_copy = pltpu.make_async_remote_copy(
        src_ref=corner_part,
        dst_ref=corner_ref,
        send_sem=send_c,
        recv_sem=recv_c,
        device_id=(row, jnp.clip(corner_owner, 0, N_COL - 1)),
        device_id_type=MESH,
    )
    corner_local = pltpu.make_async_copy(corner_part, corner_ref, local_sem.at[1])
    corner_here = (col == corner_source) & corner_exists

    @pl.when(corner_here & (corner_owner != col))
    def _():
        corner_copy.start()

    @pl.when(corner_here & (corner_owner == col))
    def _():
        corner_local.start()

    halos = []
    for at, (src, dst, device) in enumerate(
        (
            (key_ref.at[pl.ds(HALO + ATOMS, HALO)], from_before_ref, ahead),
            (key_ref.at[pl.ds(0, HALO)], from_after_ref, behind),
        )
    ):
        copy = pltpu.make_async_remote_copy(
            src_ref=src,
            dst_ref=dst,
            send_sem=send_h.at[at],
            recv_sem=recv_h.at[at],
            device_id=device,
            device_id_type=MESH,
        )
        copy.start()
        halos.append(copy)
    for copy in halos:
        copy.wait()

    @pl.when(jnp.logical_not(is_main))
    def _():
        token_copy(col).wait_send()

    @pl.when(is_main)
    def _():
        token_local.wait()
        for source in range(N_COL):

            @pl.when(col != source)
            def _():
                token_copy(source).wait_recv()

    @pl.when(corner_here & (corner_owner != col))
    def _():
        corner_copy.wait_send()

    @pl.when(corner_here & (corner_owner == col))
    def _():
        corner_local.wait()

    @pl.when(is_corner & (col != corner_source))
    def _():
        corner_copy.wait_recv()


def gather_gradients(key_sums, token_sums):
    any_spec = pl.BlockSpec(memory_space=pl.ANY)
    return pl.pallas_call(
        gather_kernel,
        out_shape=(
            jax.ShapeDtypeStruct((HALO, CP), F32),
            jax.ShapeDtypeStruct((HALO, CP), F32),
            jax.ShapeDtypeStruct((N_COL, KEYS, QTOK * CA), F32),
            jax.ShapeDtypeStruct((16, 256), F32),
        ),
        in_specs=[any_spec] * 2,
        out_specs=(any_spec,) * 4,
        scratch_shapes=[
            pltpu.SemaphoreType.DMA,
            pltpu.SemaphoreType.DMA((N_COL,)),
            pltpu.SemaphoreType.DMA,
            pltpu.SemaphoreType.DMA,
            pltpu.SemaphoreType.DMA((2,)),
            pltpu.SemaphoreType.DMA((2,)),
            pltpu.SemaphoreType.DMA((2,)),
        ],
        compiler_params=pltpu.CompilerParams(
            collective_id=1, has_side_effects=True, vmem_limit_bytes=VMEM_LIMIT
        ),
        name="gather_gradients",
    )(key_sums, token_sums)


def finish_kernel(
    pair_ref,
    gain_ref,
    proj_ref,
    patches_ref,
    corner_ref,
    blank_ref,
    key_ref,
    from_before_ref,
    from_after_ref,
    query_ref,
    feats_ref,
    pair_grad_ref,
    atom_grad_ref,
    proj_grad_ref,
    band,
    grads,
    patches,
    tokens,
    weight_sum,
    sems,
    out_sems,
    patch_sems,
):
    row, col = mesh_place()
    odd, is_main, is_corner = owners(row, col)

    def in_place(group):
        first = pl.multiple_of(window_column(group, odd), 16)
        return pl.ds(8 * group, 8), pl.ds(first, KEYS)

    def window_copy(group):
        return pltpu.make_async_copy(
            pair_ref.at[in_place(group)], band.at[group], sems.at[group]
        )

    def out_copy(group):
        return pltpu.make_async_copy(
            grads.at[group], pair_grad_ref.at[in_place(group)], out_sems.at[group]
        )

    def patch_copy(source):
        return pltpu.make_async_copy(
            patches_ref.at[source], patches.at[source], patch_sems.at[source]
        )

    first_row, first_col = corner_place(odd)
    corner_at = pl.ds(first_row, 16), pl.ds(pl.multiple_of(first_col, 16), 16)
    half_band = band.at[0, :, pl.ds(0, 32)]

    @pl.when(is_main)
    def _():
        for group in range(GROUPS):
            window_copy(group).start()
        for source in range(N_COL):
            patch_copy(source).start()

    total = query_ref[...] + key_ref[HALO : HALO + ATOMS]
    lead = total[:HALO] + from_before_ref[...]
    trail = total[ATOMS - HALO :] + from_after_ref[...]
    total = jnp.concatenate([lead, total[HALO : ATOMS - HALO], trail], axis=0)
    floats = feats_ref[...].astype(F32)
    sigma = jax.nn.sigmoid(floats)
    atom_grad_ref[...] = (total * (sigma * (1.0 + floats * (1.0 - sigma)))).astype(BF16)

    weight_sum[...] = jnp.zeros_like(weight_sum)

    def gradient(normed_rows, hatted, inv_scale, token_part, spread_w, gain):
        high, low = split(token_part)
        wide = dot(high, spread_w) + dot(low, spread_w)
        scaled = jnp.stack([wide[:, 128 * i : 128 * i + 128] for i in range(8)]) * gain
        first_mean = jnp.mean(scaled, axis=-1, keepdims=True)
        second_mean = jnp.mean(scaled * hatted, axis=-1, keepdims=True)
        flat = jnp.concatenate([normed_rows[i] for i in range(8)], axis=1)
        weight_sum[...] += dot_tn(high, flat) + dot_tn(low, flat)
        return (inv_scale * (scaled - first_mean - hatted * second_mean)).astype(BF16)

    @pl.when(is_main)
    def _():
        spread_w = spread_projection_t(proj_ref[...])
        gain = gain_ref[...]
        tokens[...] = jnp.zeros_like(tokens)
        for source in range(N_COL):
            patch_copy(source).wait()
            at = key_base(source) + 16
            lanes = query_base_static(source) * CA
            tokens[at : at + KEYS, lanes : lanes + QTOK * CA] += patches[source]
        for group in range(GROUPS):
            window_copy(group).wait()
            hatted, inv_scale = normalise(band[group])
            normed = (hatted * gain).astype(BF16)
            at = pl.multiple_of(window_column(group, odd) - TOK * odd + 16, 16)
            part = tokens[pl.ds(at, KEYS), 128 * group : 128 * group + 128]
            grads[group] = gradient(normed, hatted, inv_scale, part, spread_w, gain)
            out_copy(group).start()
        for group in range(GROUPS):
            out_copy(group).wait()

    @pl.when(is_corner)
    def _():
        loads = [
            pltpu.make_async_copy(
                pair_ref.at[
                    pl.ds(first_row + 8 * part, 8), pl.ds(pl.multiple_of(first_col, 16), 16)
                ],
                band.at[part, :, pl.ds(0, 16)],
                sems.at[part],
            )
            for part in range(2)
        ]
        loads.append(
            pltpu.make_async_copy(
                corner_ref, tokens.at[pl.ds(0, 16), pl.ds(0, 256)], patch_sems.at[0]
            )
        )
        for load in loads:
            load.start()
        for load in loads:
            load.wait()
        spread_w = spread_projection_t(proj_ref[...])
        gain = gain_ref[...]
        stores = []
        for part in range(2):
            hatted, inv_scale = normalise(band[part, :, 0:16])
            normed = (hatted * gain).astype(BF16)
            tokens_part = tokens[0:16, 128 * part : 128 * part + 128]
            grads[part, :, 0:16] = gradient(
                normed, hatted, inv_scale, tokens_part, spread_w, gain
            )
            store = pltpu.make_async_copy(
                grads.at[part, :, pl.ds(0, 16)],
                pair_grad_ref.at[
                    pl.ds(first_row + 8 * part, 8), pl.ds(pl.multiple_of(first_col, 16), 16)
                ],
                out_sems.at[part],
            )
            store.start()
            stores.append(store)
        for store in stores:
            store.wait()

    result = jnp.zeros((CA, CP), F32)
    for i in range(8):
        result += weight_sum[CA * i : CA * i + CA, 128 * i : 128 * i + 128]
    proj_grad_ref[...] = result


def finish(pair_repr, gain, proj, patches, corner, blank, key_sums, halos, query_sums, feats):
    vmem = pl.BlockSpec(memory_space=pltpu.VMEM)
    any_spec = pl.BlockSpec(memory_space=pl.ANY)
    return pl.pallas_call(
        finish_kernel,
        out_shape=(
            jax.ShapeDtypeStruct((TOK, COLS, CP), BF16),
            jax.ShapeDtypeStruct((ATOMS, CP), BF16),
            jax.ShapeDtypeStruct((CA, CP), F32),
        ),
        in_specs=[any_spec, vmem, vmem, any_spec, any_spec, any_spec] + [vmem] * 5,
        out_specs=(any_spec, vmem, vmem),
        input_output_aliases={5: 0},
        scratch_shapes=[
            pltpu.VMEM((GROUPS, 8, KEYS, CP), BF16),
            pltpu.VMEM((GROUPS, 8, KEYS, CP), BF16),
            pltpu.VMEM((N_COL, KEYS, QTOK * CA), F32),
            pltpu.VMEM((128, TOK * CA), F32),
            pltpu.VMEM((128, 8 * CP), F32),
            pltpu.SemaphoreType.DMA((GROUPS,)),
            pltpu.SemaphoreType.DMA((GROUPS,)),
            pltpu.SemaphoreType.DMA((N_COL,)),
        ],
        compiler_params=pltpu.CompilerParams(vmem_limit_bytes=VMEM_LIMIT),
        name="finish",
    )(pair_repr, gain, proj, patches, corner, blank, key_sums, *halos, query_sums, feats)


def total_kernel(part_ref, out_ref, held, sub, wide, send_1, recv_1, send_2, recv_2):
    row, col = mesh_place()
    barrier = pltpu.get_barrier_semaphore()
    row_partners = [(row, lax.rem(col + s, N_COL)) for s in range(1, N_COL)]
    col_partners = [(lax.rem(row + s, N_ROW), col) for s in range(1, N_ROW)]
    for device in row_partners + col_partners:
        pl.semaphore_signal(barrier, inc=1, device_id=device, device_id_type=MESH)
    pl.semaphore_wait(barrier, N_COL + N_ROW - 2)

    def copies(src, dst, devices, send, recv):
        return [
            pltpu.make_async_remote_copy(
                src_ref=src,
                dst_ref=dst.at[at],
                send_sem=send.at[at],
                recv_sem=recv.at[at],
                device_id=device,
                device_id_type=MESH,
            )
            for at, device in enumerate(devices)
        ]

    first = copies(part_ref, held, row_partners, send_1, recv_1)
    for copy in first:
        copy.start()
    total = part_ref[...]
    for at, copy in enumerate(first):
        copy.wait_recv()
        total += held[at]
    sub[...] = total
    second = copies(sub, wide, col_partners, send_2, recv_2)
    for copy in second:
        copy.start()
    for at, copy in enumerate(second):
        copy.wait_recv()
        total += wide[at]
    out_ref[...] = total
    for copy in first + second:
        copy.wait_send()


def total_everywhere(part):
    vmem = pl.BlockSpec(memory_space=pltpu.VMEM)
    return pl.pallas_call(
        total_kernel,
        out_shape=jax.ShapeDtypeStruct((CA, CP), F32),
        in_specs=[vmem],
        out_specs=vmem,
        scratch_shapes=[
            pltpu.VMEM((N_COL - 1, CA, CP), F32),
            pltpu.VMEM((CA, CP), F32),
            pltpu.VMEM((N_ROW - 1, CA, CP), F32),
            pltpu.SemaphoreType.DMA((N_COL - 1,)),
            pltpu.SemaphoreType.DMA((N_COL - 1,)),
            pltpu.SemaphoreType.DMA((N_ROW - 1,)),
            pltpu.SemaphoreType.DMA((N_ROW - 1,)),
        ],
        compiler_params=pltpu.CompilerParams(
            collective_id=2, has_side_effects=True, vmem_limit_bytes=VMEM_LIMIT
        ),
        name="total_everywhere",
    )(part)


def shards(
    pair_repr,
    pair_gain,
    proj_weight,
    query_weight,
    key_weight,
    mlp_first,
    mlp_second,
    mlp_third,
    atom_feats,
    token_counts,
    key_start,
    pair_cotangent,
):
    gain = pair_gain.reshape(1, CP)
    zrow, corner = project_band(pair_repr, gain, proj_weight)
    patch, patch_corner, *halo = scatter_band(zrow, corner, atom_feats, token_counts)
    key_sums, query_sums, token_sums, blank = atom_pairs(
        key_start,
        pair_cotangent,
        atom_feats,
        halo[:2],
        token_counts,
        halo[2:],
        patch,
        patch_corner,
        (query_weight, key_weight, mlp_first, mlp_second, mlp_third),
    )
    from_before, from_after, patches, corner_sums = gather_gradients(key_sums, token_sums)
    pair_grad, atom_grad, part = finish(
        pair_repr,
        gain,
        proj_weight,
        patches,
        corner_sums,
        blank,
        key_sums,
        (from_before, from_after),
        query_sums,
        atom_feats,
    )
    proj_grad = total_everywhere(part).T
    return pair_grad, atom_grad, proj_grad


def solution(mesh):
    placed = (
        P("row", "col", None),
        P(),
        P(),
        P(),
        P(),
        P(),
        P(),
        P(),
        P(("row", "col"), None),
        P("row", None),
        P(("row", "col")),
        P(("row", "col"), None),
    )
    return jax.shard_map(
        shards,
        mesh=mesh,
        in_specs=placed,
        out_specs=(P("row", "col", None), P(("row", "col"), None), P()),
        check_vma=False,
    )
```

```python
import jax
import jax.numpy as jnp
from jax import lax
from jax.experimental import pallas as pl
from jax.experimental.pallas import tpu as pltpu
from jax.sharding import PartitionSpec as P

F32 = jnp.float32
BF16 = jnp.bfloat16
MESH = pl.DeviceIdType.MESH

N_ROW = 16
N_COL = 8
TOK = 96
COLS = 192
CP = 128
CA = 16
QBLK = 32
KWIN = 128
MOST = 23
ATOMS = 256
ROW_ATOMS = 2048
SLACK = TOK * MOST - ROW_ATOMS
HALO = KWIN - QBLK
EXT = ATOMS + 2 * HALO
NBLK = ATOMS // QBLK
LANES = QBLK * CA
KEYS = 48
QTOK = 32
GROUPS = TOK // 8
VMEM_LIMIT = 56 * 1024 * 1024


def key_base(col):
    return 16 * ((11 * col - 5 + 16) // 16) - 16


def query_base(col):
    return jnp.minimum(8 * ((11 * col) // 8), TOK - QTOK)


def query_base_static(col):
    return min(8 * ((11 * col) // 8), TOK - QTOK)


def iota(shape, dim):
    return lax.broadcasted_iota(jnp.int32, shape, dim)


def dot(a, b):
    return jnp.dot(a, b, preferred_element_type=F32)


def dot_nt(a, b):
    return lax.dot_general(a, b, (((1,), (1,)), ((), ())), preferred_element_type=F32)


def dot_tn(a, b):
    return lax.dot_general(a, b, (((0,), (0,)), ((), ())), preferred_element_type=F32)


def split(x):
    high = x.astype(BF16)
    low = (x - high.astype(F32)).astype(BF16)
    return high, low


def dot_split(x, w):
    high, low = split(x)
    return dot(high, w) + dot(low, w)


def sigmoid(x):
    return 0.5 * jnp.tanh(0.5 * x) + 0.5


def mesh_place():
    row = lax.axis_index("row")
    col = lax.axis_index("col")
    return row, col


def normalise(block):
    floats = block.astype(F32)
    centre = floats - jnp.mean(floats, axis=-1, keepdims=True)
    spread = jnp.mean(centre * centre, axis=-1, keepdims=True)
    inv_scale = lax.rsqrt(spread + 1e-05)
    return centre * inv_scale, inv_scale


def channel_eye(rows):
    return ((iota((rows, CA), 0) & (CA - 1)) == iota((rows, CA), 1)).astype(F32).astype(BF16)


def channel_eye_t(lanes):
    return ((iota((CA, lanes), 1) & (CA - 1)) == iota((CA, lanes), 0)).astype(F32).astype(BF16)


def spread_projection(proj):
    eye_t = channel_eye_t(CP)
    wide = dot_tn(proj, eye_t)
    lane = iota((CP, CP), 1) // CA
    return jnp.concatenate(
        [jnp.where(lane == i, wide, 0.0).astype(BF16) for i in range(8)], axis=0
    )


def spread_projection_t(proj):
    eye = channel_eye(CP)
    tall = dot(eye, proj)
    row = iota((CP, CP), 0) // CA
    return jnp.concatenate(
        [jnp.where(row == i, tall, 0.0).astype(BF16) for i in range(8)], axis=1
    )


def window_column(group, odd):
    first = 16 * ((8 * group - 13 + 16) // 16) - 16
    return jnp.clip(first + TOK * odd, 0, COLS - KEYS)


def corner_place(odd):
    return 80 * odd, 176 * (1 - odd)


def swap_groups(pieces, group):
    for bit in (1, 2, 4):
        take = (group & bit) != 0
        swapped = list(pieces)
        for at in range(8):
            if at & bit == 0:
                one, two = pieces[at], pieces[at | bit]
                swapped[at] = jnp.where(take, pltpu.roll(two, CA * bit, 1), one)
                swapped[at | bit] = jnp.where(take, two, pltpu.roll(one, 128 - CA * bit, 1))
        pieces = swapped
    return pieces


def neighbours(row, col):
    ahead = (
        jnp.where(col == N_COL - 1, lax.rem(row + 1, N_ROW), row),
        lax.rem(col + 1, N_COL),
    )
    behind = (
        jnp.where(col == 0, lax.rem(row + N_ROW - 1, N_ROW), row),
        lax.rem(col + N_COL - 1, N_COL),
    )
    return ahead, behind


def tile_owners(row):
    along_z = [4 * (row // 4) + lax.rem(row + step, 4) for step in range(1, 4)]
    along_x = [lax.rem(row + 4 * step, N_ROW) for step in range(1, 4)]
    return [(other, other // 2) for other in along_z], [(other, other // 2) for other in along_x]


def band_kernel(
    start_ref,
    pair_ref,
    cot_hbm,
    gain_ref,
    proj_ref,
    feats_ref,
    counts_ref,
    query_w_ref,
    key_w_ref,
    first_w_ref,
    second_w_ref,
    third_w_ref,
    grads_ref,
    corner_grads_ref,
    atom_grad_ref,
    proj_grad_ref,
    band,
    corner_band,
    flat,
    corner_flat,
    zrow,
    zcorner,
    patch,
    patch_corner,
    feats_before,
    feats_after,
    counts_before,
    counts_after,
    cot_ref,
    act_ext,
    lhs,
    rhs,
    query_high,
    query_low,
    spread,
    cot,
    state,
    mixers,
    key_tiled,
    query_tiled,
    slot_from,
    slot_to,
    hot_ref,
    key_sum,
    query_sum,
    token_sum,
    key_before,
    key_after,
    patches,
    token_corner,
    tokens,
    tokens_high,
    tokens_low,
    weight_part,
    weight_corner,
    weight_z,
    weight_x,
    weight_total,
    load_sems,
    cot_sem,
    corner_load_sem,
    send_z,
    recv_z,
    send_c,
    recv_c,
    send_h,
    recv_h,
    send_t,
    recv_t,
    send_tc,
    recv_tc,
    send_k,
    recv_k,
    send_wc,
    recv_wc,
    send_wz,
    recv_wz,
    send_wx,
    recv_wx,
    send_w,
    recv_w,
):
    row = lax.axis_index("row")
    col = lax.axis_index("col")
    odd = row % 2
    half = row // 2
    is_main = col == half
    not_main = col != half
    holder = jnp.where(odd == 0, half - 1, half + 1)
    reader = (N_COL - 1) * odd
    exists = (holder >= 0) & (holder < N_COL)
    is_holder = exists & (col == holder)
    is_reader = exists & (col == reader)
    same_device = holder == reader
    other_device = holder != reader
    holder_col = jnp.clip(holder, 0, N_COL - 1)
    ahead, behind = neighbours(row, col)
    along_z, along_x = tile_owners(row)

    def remote(src, dst, send, recv, device):
        return pltpu.make_async_remote_copy(
            src_ref=src,
            dst_ref=dst,
            send_sem=send,
            recv_sem=recv,
            device_id=device,
            device_id_type=MESH,
        )

    def window_copy(group):
        first = pl.multiple_of(window_column(group, odd), 16)
        return pltpu.make_async_copy(
            pair_ref.at[pl.ds(8 * group, 8), pl.ds(first, KEYS)],
            band.at[group],
            load_sems.at[group],
        )

    first_row, first_col = corner_place(odd)
    corner_load = pltpu.make_async_copy(
        pair_ref.at[pl.ds(first_row, 16), pl.ds(pl.multiple_of(first_col, 16), 16)],
        corner_band,
        corner_load_sem,
    )
    cot_load = pltpu.make_async_copy(cot_hbm, cot_ref, cot_sem)

    @pl.when(is_main)
    def _():
        for group in range(GROUPS):
            window_copy(group).start()

    @pl.when(is_holder)
    def _():
        corner_load.start()

    cot_load.start()

    barrier = pltpu.get_barrier_semaphore()

    def greet(device):
        pl.semaphore_signal(barrier, inc=1, device_id=device, device_id_type=MESH)

    greet(ahead)
    greet(behind)

    @pl.when(not_main)
    def _():
        greet((row, half))

    @pl.when(is_main)
    def _():
        for step in range(1, N_COL):
            greet((row, lax.rem(col + step, N_COL)))
        for device in along_z + along_x:
            greet(device)

    @pl.when(is_holder & other_device)
    def _():
        greet((row, reader))

    @pl.when(is_reader & other_device)
    def _():
        greet((row, holder_col))

    greeted = 2 + jnp.where(is_main, N_COL - 1 + 6, 1)
    greeted += jnp.where((is_holder | is_reader) & other_device, 1, 0)

    @pl.when(is_main)
    def _():
        zrow[...] = jnp.zeros_like(zrow)
        spread_w = spread_projection(proj_ref[...])
        gain = gain_ref[...]

        def project(group, carry):
            window_copy(group).wait()
            hatted, _ = normalise(band[group])
            normed = (hatted * gain).astype(BF16)
            rows = jnp.concatenate([normed[i] for i in range(8)], axis=1)
            flat[pl.ds(pl.multiple_of(KEYS * group, 16), KEYS), :] = rows
            at = pl.multiple_of(window_column(group, odd) - TOK * odd + 16, 16)
            lanes = pl.ds(pl.multiple_of(128 * group, 128), 128)
            zrow[pl.ds(at, KEYS), lanes] = dot(rows, spread_w).astype(BF16)
            return carry

        lax.fori_loop(0, GROUPS, project, 0)

    @pl.when(is_holder)
    def _():
        spread_w = spread_projection(proj_ref[...])
        corner_load.wait()
        hatted, _ = normalise(corner_band[...])
        normed = (hatted * gain_ref[...]).astype(BF16)
        for part in range(2):
            rows = jnp.concatenate([normed[8 * part + i] for i in range(8)], axis=1)
            corner_flat[16 * part : 16 * part + 16, :] = rows
            zcorner[:, 128 * part : 128 * part + 128] = dot(rows, spread_w).astype(BF16)

    pl.semaphore_wait(barrier, greeted)

    def z_part(target, first):
        return zrow.at[pl.ds(key_base(target) + 16, KEYS), pl.ds(first, QTOK * CA)]

    def z_copy(target):
        src = z_part(target, query_base_static(target) * CA)
        return remote(src, patch, send_z.at[target], recv_z, (row, target))

    corner_copy = remote(zcorner, patch_corner, send_c, recv_c, (row, reader))

    @pl.when(is_main)
    def _():
        for target in range(N_COL):

            @pl.when(col != target)
            def _():
                z_copy(target).start()

        patch[...] = zrow[
            pl.ds(pl.multiple_of(key_base(col) + 16, 16), KEYS),
            pl.ds(pl.multiple_of(query_base(col) * CA, 128), QTOK * CA),
        ]

    @pl.when(is_holder & other_device)
    def _():
        corner_copy.start()

    @pl.when(is_holder & same_device)
    def _():
        patch_corner[...] = zcorner[...]

    halos = [
        remote(src, dst, send_h.at[at], recv_h.at[at], device)
        for at, (src, dst, device) in enumerate(
            (
                (feats_ref.at[pl.ds(ATOMS - HALO, HALO)], feats_before, ahead),
                (feats_ref.at[pl.ds(0, HALO)], feats_after, behind),
                (counts_ref, counts_before, ahead),
                (counts_ref, counts_after, behind),
            )
        )
    ]
    for copy in halos:
        copy.start()

    eye = channel_eye(LANES)
    eye16 = eye[:256]
    same = (iota((256, 256), 0) // CA) == (iota((256, 256), 1) // CA)

    def mixer(weight, flip):
        left = dot_nt(eye16, weight) if flip else dot(eye16, weight)
        wide = dot_nt(left.astype(BF16), eye16)
        return jnp.where(same, wide, 0.0).astype(BF16)

    mixers[0] = mixer(first_w_ref[...], False)
    mixers[1] = mixer(second_w_ref[...], False)
    mixers[2] = mixer(third_w_ref[...], True)
    mixers[3] = mixer(second_w_ref[...], True)
    mixers[4] = mixer(first_w_ref[...], True)
    key_tiled[...] = dot(eye, key_w_ref[...]).astype(BF16)
    query_tiled[...] = dot(eye, query_w_ref[...]).astype(BF16)
    eye_t = channel_eye_t(LANES)
    rhs[128:256, :] = dot_tn(key_w_ref[...], eye_t).astype(BF16)
    rhs[112:128, :] = jnp.zeros((16, LANES), BF16)

    def activate(feats):
        floats = feats.astype(F32)
        return floats * jax.nn.sigmoid(floats)

    own_act = activate(feats_ref[...]).astype(BF16)
    act_ext[HALO : HALO + ATOMS] = activate(feats_ref[...])

    lane_is_row = iota((QBLK, LANES), 1) // CA == iota((QBLK, LANES), 0)
    query_wide = dot_tn(query_w_ref[...], eye_t).astype(BF16)
    for block in range(NBLK):
        terms = dot(own_act[QBLK * block : QBLK * block + QBLK], query_wide)
        high, low = split(jnp.where(lane_is_row, terms, 0.0))
        query_high[QBLK * block : QBLK * block + QBLK] = high
        query_low[QBLK * block : QBLK * block + QBLK] = low

    own = counts_ref[...].astype(F32)

    def rows_of(counts, rows):
        return jnp.broadcast_to(counts, (rows, TOK)).astype(BF16)

    def as_mask(flag):
        return jnp.where(flag, 1.0, 0.0).astype(BF16)

    first_query = query_base(col)
    slot = iota((LANES, TOK), 0) // CA + first_query
    slot_index = iota((LANES, TOK), 1)
    own_rows = rows_of(own, 128)
    slot_from[...] = dot_nt(as_mask(slot_index < slot), own_rows)
    slot_to[...] = dot_nt(as_mask(slot_index < slot + 1), own_rows)

    lane_atom_row = (iota((1, LANES), 1) // CA).astype(F32)
    channel_match = (iota((256, 128), 0) % CA) == (iota((256, 128), 1) % CA)

    def block_place(block):
        first = col * ATOMS + block * QBLK
        token = 8 * (first // (8 * MOST)) - first_query
        return first, pl.multiple_of(token * CA, 128)

    def query_hot(block):
        first, at = block_place(block)
        low = slot_from[pl.ds(at, 256), :]
        high = slot_to[pl.ds(at, 256), :]
        parts = []
        for part in range(4):
            atom = lane_atom_row[:, 128 * part : 128 * part + 128] + first.astype(F32)
            hot = (low <= atom) & (atom < high) & channel_match
            parts.append(jnp.where(hot, 1.0, 0.0).astype(BF16))
        return jnp.concatenate(parts, axis=1)

    def key_first(block):
        return col * ATOMS + block * QBLK + start_ref[block]

    def hot_step(block, carry):
        hot_ref[block] = query_hot(block)
        return carry

    lax.fori_loop(0, NBLK, hot_step, 0)

    cot_load.wait()

    group = iota((16, 128), 1) // CA

    def spread_step(eight, carry):
        rows = cot_ref[pl.ds(pl.multiple_of(16 * eight, 16), 16), :].astype(F32)
        for half in range(2):
            at = pl.multiple_of(256 * eight + 128 * half, 128)
            for chunk in range(16):
                spread[pl.ds(at + 8 * chunk, 8), :] = rows[
                    8 * half : 8 * half + 8, 128 * chunk : 128 * chunk + 128
                ]
        return carry

    lax.fori_loop(0, ATOMS // 16, spread_step, 0)

    def swap_step(eight, carry):
        at = 128 * eight
        pieces = [spread[pl.ds(at + atom, 16, stride=8), :] for atom in range(8)]
        pieces = swap_groups(pieces, group)
        to = NBLK * KWIN * (eight % 4) + KWIN * (eight // 4)
        for key in range(8):
            cot[pl.ds(to + key, 16, stride=8), :] = pieces[key]
        return carry

    lax.fori_loop(0, ATOMS // 8, swap_step, 0)

    for copy in halos:
        copy.wait()
    act_ext[0:HALO] = activate(feats_before[...])
    act_ext[HALO + ATOMS : EXT] = activate(feats_after[...])

    base = key_base(col)
    before = counts_before[...].astype(F32)
    after = counts_after[...].astype(F32)

    def lane_bounds(offset):
        token = iota((TOK, 128), 1) + (base + offset)
        index = iota((TOK, 128), 0)
        total = dot(rows_of(own, 8), as_mask(index < token))
        total += dot(rows_of(after, 8), as_mask(index + TOK < token))
        return total - dot(rows_of(before, 8), as_mask(index - TOK >= token))

    def column_bounds(offset):
        token = iota((KEYS, TOK), 0) + (base + offset)
        index = iota((KEYS, TOK), 1)
        total = dot_nt(as_mask(index < token), rows_of(own, 128))
        total += dot_nt(as_mask(index + TOK < token), rows_of(after, 128))
        return total - dot_nt(as_mask(index - TOK >= token), rows_of(before, 128))

    lane = iota((8, 128), 1)
    far = 1.0e6
    lane_from = jnp.where(lane < 48, lane_bounds(0), jnp.where(lane < 112, -far, far))[0:1]
    lane_to = jnp.where(lane < 48, lane_bounds(1), jnp.where(lane < 112, far, -far))[0:1]
    column_from = column_bounds(0)
    column_to = column_bounds(1)

    @pl.when(is_main)
    def _():
        for target in range(N_COL):

            @pl.when(col != target)
            def _():
                z_copy(target).wait_send()

    @pl.when(not_main)
    def _():
        z_copy(0).wait_recv()

    @pl.when(is_holder & other_device)
    def _():
        corner_copy.wait_send()

    @pl.when(is_reader & other_device)
    def _():
        corner_copy.wait_recv()

    @pl.when(is_reader)
    def _():
        at = pl.multiple_of(32 * odd, 16), pl.multiple_of(256 * odd, 128)
        patch[pl.ds(at[0], 16), pl.ds(at[1], 256)] = patch_corner[...]

    def start_step(block, carry):
        _, at = block_place(block)
        hot = hot_ref[block]
        window = start_ref[block] + block * QBLK + HALO
        atom = (iota((KWIN, 128), 0) + key_first(block)).astype(F32)
        lhs[:, 0:128] = as_mask((lane_from <= atom) & (atom < lane_to))
        lhs[:, 128:256] = act_ext[pl.ds(window, KWIN), :].astype(BF16)
        rhs[0:48, :] = dot(patch[:, pl.ds(at, 256)], hot).astype(BF16)
        mine = pl.multiple_of(block * QBLK, QBLK)
        rhs[48:80, :] = query_high[pl.ds(mine, QBLK), :]
        rhs[80:112, :] = query_low[pl.ds(mine, QBLK), :]
        state[pl.ds(pl.multiple_of(block * KWIN, KWIN), KWIN), :] = dot(lhs[...], rhs[...])
        return carry

    lax.fori_loop(0, NBLK, start_step, 0)

    atom_low = jnp.where(row == 0, 0, -ROW_ATOMS)
    atom_high = jnp.where(row == N_ROW - 1, ROW_ATOMS, 2 * ROW_ATOMS)

    def slope(value, sigma, act):
        return sigma + act - act * sigma

    def mlp_step(step, carry):
        pair = step // 2
        at = pl.multiple_of(256 * pair, 256)
        place = pl.ds(at, 256), pl.ds(pl.multiple_of(256 * (step % 2), 256), 256)
        value = state[place]
        index = iota((256, 256), 0)
        begin = jnp.where(index < KWIN, key_first(2 * pair), key_first(2 * pair + 1) - KWIN)
        atom = index + begin
        parts = [
            cot[pl.ds(pl.multiple_of(at + NBLK * KWIN * (2 * (step % 2) + part), 256), 256), :]
            for part in range(2)
        ]
        grad = jnp.concatenate(parts, axis=1)
        grad = jnp.where((atom >= atom_low) & (atom < atom_high), grad, 0.0)
        sig_0 = sigmoid(value)
        act_0 = value * sig_0
        one = dot_split(act_0, mixers[0])
        sig_1 = sigmoid(one)
        act_1 = one * sig_1
        two = dot_split(act_1, mixers[1])
        sig_2 = sigmoid(two)
        back = dot(grad.astype(BF16), mixers[2]) * slope(two, sig_2, two * sig_2)
        back = dot_split(back, mixers[3]) * slope(one, sig_1, act_1)
        back = dot_split(back, mixers[4]) * slope(value, sig_0, act_0)
        state[place] = grad + back
        return carry

    lax.fori_loop(0, 8, mlp_step, 0)

    key_sum[...] = jnp.zeros_like(key_sum)
    token_sum[...] = jnp.zeros_like(token_sum)

    def sum_step(block, carry):
        _, at = block_place(block)
        window = start_ref[block] + block * QBLK + HALO
        back = state[pl.ds(pl.multiple_of(block * KWIN, KWIN), KWIN), :]
        high, low = split(back)
        by_key = dot(high, key_tiled[...]) + dot(low, key_tiled[...])
        reach = KWIN + HALO
        moved = as_mask(
            iota((reach, KWIN), 0) == iota((reach, KWIN), 1) + (start_ref[block] + HALO)
        )
        by_key_high, by_key_low = split(by_key)
        key_sum[pl.ds(pl.multiple_of(block * QBLK, QBLK), reach), :] += dot(
            moved, by_key_high
        ) + dot(moved, by_key_low)
        over_keys = jnp.sum(back, axis=0, keepdims=True)
        over_keys = jnp.where(lane_is_row, over_keys, 0.0)
        mine = pl.multiple_of(block * QBLK, QBLK)
        query_sum[pl.ds(mine, QBLK), :] = dot_split(over_keys, query_tiled[...])
        atom = (iota((KEYS, 128), 1) + key_first(block)).astype(F32)
        key_hot = as_mask((column_from <= atom) & (atom < column_to))
        by_token = dot(key_hot, high) + dot(key_hot, low)
        high, low = split(by_token)
        hot = hot_ref[block]
        token_sum[:, pl.ds(at, 256)] += dot_nt(high, hot) + dot_nt(low, hot)
        return carry

    lax.fori_loop(0, NBLK, sum_step, 0)

    def token_copy(source):
        return remote(token_sum, patches.at[source], send_t, recv_t.at[source], (row, half))

    corner_part = token_sum.at[
        pl.ds(pl.multiple_of(32 * odd, 16), 16), pl.ds(pl.multiple_of(256 * odd, 128), 256)
    ]
    token_corner_copy = remote(corner_part, token_corner, send_tc, recv_tc, (row, holder_col))

    @pl.when(not_main)
    def _():
        token_copy(col).start()

    @pl.when(is_main)
    def _():
        patches[col] = token_sum[...]

    @pl.when(is_reader & other_device)
    def _():
        token_corner_copy.start()

    @pl.when(is_reader & same_device)
    def _():
        token_corner[...] = corner_part[...]

    key_halos = [
        remote(src, dst, send_k.at[at], recv_k.at[at], device)
        for at, (src, dst, device) in enumerate(
            (
                (key_sum.at[pl.ds(HALO + ATOMS, HALO)], key_before, ahead),
                (key_sum.at[pl.ds(0, HALO)], key_after, behind),
            )
        )
    ]
    for copy in key_halos:
        copy.start()

    def diagonal(wide):
        total = wide[0:CA, 0:128]
        for i in range(1, 8):
            total += wide[CA * i : CA * i + CA, 128 * i : 128 * i + 128]
        return total

    def gradient(block, rows_high, rows_low, spread_w, gain):
        hatted, inv_scale = normalise(block)
        wide = dot(rows_high, spread_w) + dot(rows_low, spread_w)
        scaled = jnp.stack([wide[:, 128 * i : 128 * i + 128] for i in range(8)]) * gain
        first_mean = jnp.mean(scaled, axis=-1, keepdims=True)
        second_mean = jnp.mean(scaled * hatted, axis=-1, keepdims=True)
        return (inv_scale * (scaled - first_mean - hatted * second_mean)).astype(BF16)

    corner_weight_copy = remote(
        weight_part, weight_corner, send_wc, recv_wc, (row, half)
    )

    @pl.when(is_holder)
    def _():
        @pl.when(other_device)
        def _():
            token_corner_copy.wait_recv()

        spread_w = spread_projection_t(proj_ref[...])
        gain = gain_ref[...]
        total = jnp.zeros((CA, CP), F32)
        for part in range(2):
            high, low = split(token_corner[:, 128 * part : 128 * part + 128])
            rows = corner_flat[16 * part : 16 * part + 16, :]
            total += diagonal(dot_tn(high, rows) + dot_tn(low, rows))
        weight_part[...] = total
        corner_weight_copy.start()
        for part in range(2):
            high, low = split(token_corner[:, 128 * part : 128 * part + 128])
            corner_grads_ref[part] = gradient(
                corner_band[8 * part : 8 * part + 8], high, low, spread_w, gain
            )

    z_copies = [
        remote(weight_part, weight_z.at[at], send_wz.at[at], recv_wz.at[at], device)
        for at, device in enumerate(along_z)
    ]
    x_copies = [
        remote(weight_total.at[0], weight_x.at[at], send_wx.at[at], recv_wx.at[at], device)
        for at, device in enumerate(along_x)
    ]

    def total_copy(target):
        return remote(
            weight_total.at[1], weight_total.at[1], send_w.at[target], recv_w, (row, target)
        )

    @pl.when(is_main)
    def _():
        tokens[...] = jnp.zeros_like(tokens)
        for source in range(N_COL):

            @pl.when(col != source)
            def _():
                token_copy(source).wait_recv()

            at = key_base(source) + 16
            lanes = query_base_static(source) * CA
            tokens[at : at + KEYS, lanes : lanes + QTOK * CA] += patches[source]

        def cut(group, carry):
            at = pl.multiple_of(window_column(group, odd) - TOK * odd + 16, 16)
            lanes = pl.ds(pl.multiple_of(128 * group, 128), 128)
            high, low = split(tokens[pl.ds(at, KEYS), lanes])
            to = pl.ds(pl.multiple_of(KEYS * group, 16), KEYS)
            tokens_high[to, :] = high
            tokens_low[to, :] = low
            return carry

        lax.fori_loop(0, GROUPS, cut, 0)
        total = diagonal(
            dot_tn(tokens_high[...], flat[...]) + dot_tn(tokens_low[...], flat[...])
        )

        @pl.when(exists)
        def _():
            corner_weight_copy.wait_recv()

        total += jnp.where(exists, weight_corner[...], 0.0)
        weight_part[...] = total
        for copy in z_copies:
            copy.start()
        spread_w = spread_projection_t(proj_ref[...])
        gain = gain_ref[...]

        def grad_step(group, carry):
            rows = pl.ds(pl.multiple_of(KEYS * group, 16), KEYS)
            grads_ref[group] = gradient(
                band[group], tokens_high[rows, :], tokens_low[rows, :], spread_w, gain
            )
            return carry

        lax.fori_loop(0, GROUPS // 2, grad_step, 0)
        for at, copy in enumerate(z_copies):
            copy.wait_recv()
            total += weight_z[at]
        weight_total[0] = total
        for copy in x_copies:
            copy.start()
        lax.fori_loop(GROUPS // 2, GROUPS, grad_step, 0)
        for at, copy in enumerate(x_copies):
            copy.wait_recv()
            total += weight_x[at]
        weight_total[1] = total
        for target in range(N_COL):

            @pl.when(col != target)
            def _():
                total_copy(target).start()

    for copy in key_halos:
        copy.wait()
    total = query_sum[...] + key_sum[HALO : HALO + ATOMS]
    lead = total[:HALO] + key_before[...]
    trail = total[ATOMS - HALO :] + key_after[...]
    total = jnp.concatenate([lead, total[HALO : ATOMS - HALO], trail], axis=0)
    floats = feats_ref[...].astype(F32)
    sigma = jax.nn.sigmoid(floats)
    atom_grad_ref[...] = (total * (sigma * (1.0 + floats * (1.0 - sigma)))).astype(BF16)

    @pl.when(not_main)
    def _():
        token_copy(col).wait_send()

    @pl.when(is_reader & other_device)
    def _():
        token_corner_copy.wait_send()

    @pl.when(is_holder)
    def _():
        corner_weight_copy.wait_send()

    @pl.when(is_main)
    def _():
        for copy in z_copies + x_copies:
            copy.wait_send()
        for target in range(N_COL):

            @pl.when(col != target)
            def _():
                total_copy(target).wait_send()

    @pl.when(not_main)
    def _():
        total_copy(0).wait_recv()

    proj_grad_ref[...] = weight_total[1]


def band_pass(start, pair_repr, cot, gain, proj, feats, counts, weights):
    vmem = pl.BlockSpec(memory_space=pltpu.VMEM)
    any_spec = pl.BlockSpec(memory_space=pl.ANY)
    dma = pltpu.SemaphoreType.DMA
    return pl.pallas_call(
        band_kernel,
        out_shape=(
            jax.ShapeDtypeStruct((GROUPS, 8, KEYS, CP), BF16),
            jax.ShapeDtypeStruct((2, 8, 16, CP), BF16),
            jax.ShapeDtypeStruct((ATOMS, CP), BF16),
            jax.ShapeDtypeStruct((CA, CP), F32),
        ),
        in_specs=[pl.BlockSpec(memory_space=pltpu.SMEM), any_spec, any_spec] + [vmem] * 9,
        out_specs=(vmem,) * 4,
        scratch_shapes=[
            pltpu.VMEM((GROUPS, 8, KEYS, CP), BF16),
            pltpu.VMEM((16, 16, CP), BF16),
            pltpu.VMEM((GROUPS * KEYS, 8 * CP), BF16),
            pltpu.VMEM((32, 8 * CP), BF16),
            pltpu.VMEM((128, TOK * CA), BF16),
            pltpu.VMEM((16, 256), BF16),
            pltpu.VMEM((KEYS, QTOK * CA), BF16),
            pltpu.VMEM((16, 256), BF16),
            pltpu.VMEM((HALO, CP), BF16),
            pltpu.VMEM((HALO, CP), BF16),
            pltpu.VMEM((1, TOK), jnp.int32),
            pltpu.VMEM((1, TOK), jnp.int32),
            pltpu.VMEM((ATOMS, KWIN * CA), BF16),
            pltpu.VMEM((EXT, CP), F32),
            pltpu.VMEM((KWIN, 256), BF16),
            pltpu.VMEM((256, LANES), BF16),
            pltpu.VMEM((ATOMS, LANES), BF16),
            pltpu.VMEM((ATOMS, LANES), BF16),
            pltpu.VMEM((ATOMS * 16, 128), F32),
            pltpu.VMEM((4 * NBLK * KWIN, 128), F32),
            pltpu.VMEM((NBLK * KWIN, LANES), F32),
            pltpu.VMEM((5, 256, 256), BF16),
            pltpu.VMEM((LANES, CP), BF16),
            pltpu.VMEM((LANES, CP), BF16),
            pltpu.VMEM((LANES, 128), F32),
            pltpu.VMEM((LANES, 128), F32),
            pltpu.VMEM((NBLK, 256, LANES), BF16),
            pltpu.VMEM((EXT, CP), F32),
            pltpu.VMEM((ATOMS, CP), F32),
            pltpu.VMEM((KEYS, QTOK * CA), F32),
            pltpu.VMEM((HALO, CP), F32),
            pltpu.VMEM((HALO, CP), F32),
            pltpu.VMEM((N_COL, KEYS, QTOK * CA), F32),
            pltpu.VMEM((16, 256), F32),
            pltpu.VMEM((128, TOK * CA), F32),
            pltpu.VMEM((GROUPS * KEYS, 128), BF16),
            pltpu.VMEM((GROUPS * KEYS, 128), BF16),
            pltpu.VMEM((CA, CP), F32),
            pltpu.VMEM((CA, CP), F32),
            pltpu.VMEM((3, CA, CP), F32),
            pltpu.VMEM((3, CA, CP), F32),
            pltpu.VMEM((2, CA, CP), F32),
            dma((GROUPS,)),
            dma,
            dma,
            dma((N_COL,)),
            dma,
            dma,
            dma,
            dma((4,)),
            dma((4,)),
            dma,
            dma((N_COL,)),
            dma,
            dma,
            dma((2,)),
            dma((2,)),
            dma,
            dma,
            dma((3,)),
            dma((3,)),
            dma((3,)),
            dma((3,)),
            dma((N_COL,)),
            dma,
        ],
        compiler_params=pltpu.CompilerParams(
            collective_id=0, has_side_effects=True, vmem_limit_bytes=VMEM_LIMIT
        ),
        name="band_pass",
    )(start, pair_repr, cot, gain, proj, feats, counts, *weights)


def place_kernel(
    grads_ref,
    corner_ref,
    atom_ref,
    proj_ref,
    pair_grad_ref,
    atom_grad_ref,
    proj_grad_ref,
    rows,
    zeros,
    load_sems,
    corner_sem,
    store_sems,
):
    row = lax.axis_index("row")
    col = lax.axis_index("col")
    odd = row % 2
    half = row // 2
    is_main = col == half
    holder = jnp.where(odd == 0, half - 1, half + 1)
    is_holder = col == holder
    plain = (col != half) & (col != holder)

    def load(group):
        first = pl.multiple_of(window_column(group, odd), 16)
        return pltpu.make_async_copy(
            grads_ref.at[group], rows.at[group, :, pl.ds(first, KEYS)], load_sems.at[group]
        )

    def store(group, source):
        return pltpu.make_async_copy(
            source, pair_grad_ref.at[pl.ds(8 * group, 8)], store_sems.at[group]
        )

    @pl.when(is_main)
    def _():
        rows[...] = jnp.zeros_like(rows)
        for group in range(GROUPS):
            load(group).start()
        for group in range(GROUPS):
            load(group).wait()
            store(group, rows.at[group]).start()

    zeros[...] = jnp.zeros_like(zeros)

    @pl.when(is_holder)
    def _():
        first_row, first_col = corner_place(odd)
        rows[0:2] = jnp.zeros((2, 8, COLS, CP), BF16)
        copy = pltpu.make_async_copy(
            corner_ref,
            rows.at[pl.ds(0, 2), :, pl.ds(pl.multiple_of(first_col, 16), 16)],
            corner_sem,
        )
        copy.start()
        for group in range(2, GROUPS - 2):
            store(group, zeros).start()
        copy.wait()
        for part in range(2):

            @pl.when(odd == 0)
            def _():
                store(part, rows.at[part]).start()
                store(GROUPS - 2 + part, zeros).start()

            @pl.when(odd == 1)
            def _():
                store(part, zeros).start()
                store(GROUPS - 2 + part, rows.at[part]).start()

    @pl.when(plain)
    def _():
        for group in range(GROUPS):
            store(group, zeros).start()

    atom_grad_ref[...] = atom_ref[...]
    proj_grad_ref[...] = proj_ref[...]
    for group in range(GROUPS):
        store(group, zeros).wait()


def place(grads, corner, atom_grad, proj_grad):
    vmem = pl.BlockSpec(memory_space=pltpu.VMEM)
    any_spec = pl.BlockSpec(memory_space=pl.ANY)
    return pl.pallas_call(
        place_kernel,
        out_shape=(
            jax.ShapeDtypeStruct((TOK, COLS, CP), BF16),
            jax.ShapeDtypeStruct((ATOMS, CP), BF16),
            jax.ShapeDtypeStruct((CA, CP), F32),
        ),
        in_specs=[any_spec, any_spec, vmem, vmem],
        out_specs=(any_spec, vmem, vmem),
        scratch_shapes=[
            pltpu.VMEM((GROUPS, 8, COLS, CP), BF16),
            pltpu.VMEM((8, COLS, CP), BF16),
            pltpu.SemaphoreType.DMA((GROUPS,)),
            pltpu.SemaphoreType.DMA,
            pltpu.SemaphoreType.DMA((GROUPS,)),
        ],
        compiler_params=pltpu.CompilerParams(vmem_limit_bytes=VMEM_LIMIT),
        name="place",
    )(grads, corner, atom_grad, proj_grad)


def shards(
    pair_repr,
    pair_gain,
    proj_weight,
    query_weight,
    key_weight,
    mlp_first,
    mlp_second,
    mlp_third,
    atom_feats,
    token_counts,
    key_start,
    pair_cotangent,
):
    grads, corner, atom_grad, proj_grad = band_pass(
        key_start,
        pair_repr,
        pair_cotangent,
        pair_gain.reshape(1, CP),
        proj_weight.T,
        atom_feats,
        token_counts,
        (query_weight.T, key_weight.T, mlp_first, mlp_second, mlp_third),
    )
    pair_grad, atom_grad, proj_grad = place(grads, corner, atom_grad, proj_grad)
    return pair_grad, atom_grad, proj_grad.T


def solution(mesh):
    placed = (
        P("row", "col", None),
        P(),
        P(),
        P(),
        P(),
        P(),
        P(),
        P(),
        P(("row", "col"), None),
        P("row", None),
        P(("row", "col")),
        P(("row", "col"), None),
    )
    return jax.shard_map(
        shards,
        mesh=mesh,
        in_specs=placed,
        out_specs=(P("row", "col", None), P(("row", "col"), None), P()),
        check_vma=False,
    )
```

```python
import jax
import jax.numpy as jnp
from jax import lax
from jax.experimental import pallas as pl
from jax.experimental.pallas import tpu as pltpu
from jax.sharding import PartitionSpec as P

F32 = jnp.float32
BF16 = jnp.bfloat16
MESH = pl.DeviceIdType.MESH

N_ROW = 16
N_COL = 8
TOK = 96
COLS = 192
CP = 128
CA = 16
QBLK = 32
KWIN = 128
MOST = 23
ATOMS = 256
ROW_ATOMS = 2048
SLACK = TOK * MOST - ROW_ATOMS
HALO = KWIN - QBLK
EXT = ATOMS + 2 * HALO
NBLK = ATOMS // QBLK
LANES = QBLK * CA
KEYS = 48
QTOK = 32
GROUPS = TOK // 8
VMEM_LIMIT = 56 * 1024 * 1024
MLP_ROWS = 1024
NEAR = 19
TOKEN_PART = (
    (0, 40, 0, 384),
    (0, 40, 0, 384),
    (0, 32, 0, 512),
    (8, 32, 0, 384),
    (8, 32, 0, 384),
    (0, 32, 0, 512),
    (8, 40, 0, 384),
    (8, 40, 128, 384),
)


def key_base(col):
    return 16 * ((11 * col - 5 + 16) // 16) - 16


def query_base(col):
    return jnp.minimum(8 * ((11 * col) // 8), TOK - QTOK)


def query_base_static(col):
    return min(8 * ((11 * col) // 8), TOK - QTOK)


def iota(shape, dim):
    return lax.broadcasted_iota(jnp.int32, shape, dim)


def dot(a, b):
    return jnp.dot(a, b, preferred_element_type=F32)


def dot_nt(a, b):
    return lax.dot_general(a, b, (((1,), (1,)), ((), ())), preferred_element_type=F32)


def dot_tn(a, b):
    return lax.dot_general(a, b, (((0,), (0,)), ((), ())), preferred_element_type=F32)


def split(x):
    high = x.astype(BF16)
    low = (x - high.astype(F32)).astype(BF16)
    return high, low


def dot_split(x, w):
    high, low = split(x)
    return dot(high, w) + dot(low, w)


def dot_twice(x, w):
    return dot(jnp.concatenate(split(x), axis=1), w)


def sigmoid(x):
    return 0.5 * jnp.tanh(0.5 * x) + 0.5


def mesh_place():
    row = lax.axis_index("row")
    col = lax.axis_index("col")
    return row, col


def normalise(block):
    floats = block.astype(F32)
    centre = floats - jnp.mean(floats, axis=-1, keepdims=True)
    spread = jnp.mean(centre * centre, axis=-1, keepdims=True)
    inv_scale = lax.rsqrt(spread + 1e-05)
    return centre * inv_scale, inv_scale


def channel_eye(rows):
    return ((iota((rows, CA), 0) & (CA - 1)) == iota((rows, CA), 1)).astype(F32).astype(BF16)


def channel_eye_t(lanes):
    return ((iota((CA, lanes), 1) & (CA - 1)) == iota((CA, lanes), 0)).astype(F32).astype(BF16)


def spread_projection(proj):
    eye_t = channel_eye_t(CP)
    wide = dot_tn(proj, eye_t)
    lane = iota((CP, CP), 1) // CA
    return jnp.concatenate(
        [jnp.where(lane == i, wide, 0.0).astype(BF16) for i in range(8)], axis=0
    )


def spread_projection_t(proj):
    eye = channel_eye(CP)
    tall = dot(eye, proj)
    row = iota((CP, CP), 0) // CA
    return jnp.concatenate(
        [jnp.where(row == i, tall, 0.0).astype(BF16) for i in range(8)], axis=1
    )


def window_column(group, odd):
    first = 16 * ((8 * group - 13 + 16) // 16) - 16
    return jnp.clip(first + TOK * odd, 0, COLS - KEYS)


def corner_place(odd):
    return 80 * odd, 176 * (1 - odd)


def swap_groups(pieces, group):
    for bit in (1, 2, 4):
        take = (group & bit) != 0
        swapped = list(pieces)
        for at in range(8):
            if at & bit == 0:
                one, two = pieces[at], pieces[at | bit]
                swapped[at] = jnp.where(take, pltpu.roll(two, CA * bit, 1), one)
                swapped[at | bit] = jnp.where(take, two, pltpu.roll(one, 128 - CA * bit, 1))
        pieces = swapped
    return pieces


def neighbours(row, col):
    ahead = (
        jnp.where(col == N_COL - 1, lax.rem(row + 1, N_ROW), row),
        lax.rem(col + 1, N_COL),
    )
    behind = (
        jnp.where(col == 0, lax.rem(row + N_ROW - 1, N_ROW), row),
        lax.rem(col + N_COL - 1, N_COL),
    )
    return ahead, behind


def like_places(row, col):
    along_z = [(4 * (row // 4) + lax.rem(row + step, 4), col) for step in range(1, 4)]
    along_x = [(lax.rem(row + 4 * step, N_ROW), col) for step in range(1, 4)]
    return along_z, along_x


def band_kernel(
    start_ref,
    pair_ref,
    cot_hbm,
    gain_hbm,
    proj_hbm,
    feats_hbm,
    counts_hbm,
    query_w_hbm,
    key_w_hbm,
    first_w_hbm,
    second_w_hbm,
    third_w_hbm,
    grads_hbm,
    corner_grads_hbm,
    atom_grad_ref,
    proj_grad_ref,
    gain_ref,
    proj_ref,
    feats_ref,
    counts_ref,
    query_w_ref,
    key_w_ref,
    first_w_ref,
    second_w_ref,
    third_w_ref,
    grads,
    corner_grads,
    band,
    corner_band,
    zrow,
    zcorner,
    patch,
    patch_corner,
    raw,
    feats_before,
    feats_after,
    counts_before,
    counts_after,
    cot_ref,
    act_ext,
    rhs,
    query_high,
    query_low,
    spread,
    cot,
    state,
    mixers,
    key_tiled,
    query_tiled,
    slot_from,
    slot_to,
    hot_ref,
    key_sum,
    query_sum,
    token_sum,
    key_before,
    key_after,
    patches,
    token_corner,
    tokens,
    near_flat,
    near_high,
    near_low,
    weight_sent,
    weight_z,
    weight_x,
    weight_row,
    small_sems,
    load_sems,
    cot_sem,
    corner_load_sem,
    send_z,
    recv_z,
    send_c,
    recv_c,
    send_r,
    recv_r,
    send_rc,
    recv_rc,
    send_h,
    recv_h,
    send_t,
    recv_t,
    send_tc,
    recv_tc,
    send_k,
    recv_k,
    send_wz,
    recv_wz,
    send_wx,
    recv_wx,
    send_wr,
    recv_wr,
):
    row = lax.axis_index("row")
    col = lax.axis_index("col")
    odd = row % 2
    half = row // 2
    is_main = col == half
    not_main = col != half
    holder = jnp.where(odd == 0, half - 1, half + 1)
    reader = (N_COL - 1) * odd
    exists = (holder >= 0) & (holder < N_COL)
    is_holder = exists & (col == holder)
    is_reader = exists & (col == reader)
    same_device = holder == reader
    other_device = holder != reader
    holder_col = jnp.clip(holder, 0, N_COL - 1)
    ahead, behind = neighbours(row, col)
    along_z, along_x = like_places(row, col)
    along_row = [(row, lax.rem(col + step, N_COL)) for step in range(1, N_COL)]

    def remote(src, dst, send, recv, device):
        return pltpu.make_async_remote_copy(
            src_ref=src,
            dst_ref=dst,
            send_sem=send,
            recv_sem=recv,
            device_id=device,
            device_id_type=MESH,
        )

    raw[...] = jnp.zeros_like(raw)

    barrier = pltpu.get_barrier_semaphore()

    def greet(device):
        pl.semaphore_signal(barrier, inc=1, device_id=device, device_id_type=MESH)

    @pl.when(col == 0)
    def _():
        greet(behind)

    @pl.when(col == N_COL - 1)
    def _():
        greet(ahead)

    for device in along_row + along_z + along_x:
        greet(device)
    greeted = N_COL - 1 + 6 + jnp.where((col == 0) | (col == N_COL - 1), 1, 0)

    def window_copy(group):
        first = pl.multiple_of(window_column(group, odd), 16)
        return pltpu.make_async_copy(
            pair_ref.at[pl.ds(8 * group, 8), pl.ds(first, KEYS)],
            band.at[group],
            load_sems.at[group],
        )

    first_row, first_col = corner_place(odd)
    corner_load = pltpu.make_async_copy(
        pair_ref.at[pl.ds(first_row, 16), pl.ds(pl.multiple_of(first_col, 16), 16)],
        corner_band,
        corner_load_sem,
    )
    cot_load = pltpu.make_async_copy(cot_hbm, cot_ref, cot_sem)

    @pl.when(is_main)
    def _():
        for group in range(GROUPS):
            window_copy(group).start()

    @pl.when(is_holder)
    def _():
        corner_load.start()

    cot_load.start()
    smalls = [
        pltpu.make_async_copy(src, dst, small_sems.at[at])
        for at, (src, dst) in enumerate(
            (
                (gain_hbm, gain_ref),
                (proj_hbm, proj_ref),
                (feats_hbm, feats_ref),
                (counts_hbm, counts_ref),
                (query_w_hbm, query_w_ref),
                (key_w_hbm, key_w_ref),
                (first_w_hbm, first_w_ref),
                (second_w_hbm, second_w_ref),
                (third_w_hbm, third_w_ref),
            )
        )
    ]
    for copy in smalls:
        copy.start()
    for copy in smalls:
        copy.wait()

    @pl.when(is_main)
    def _():
        zrow[...] = jnp.zeros_like(zrow)
        spread_w = spread_projection(proj_ref[...])
        gain = gain_ref[...]

        def project(group, carry):
            window_copy(group).wait()
            hatted, _ = normalise(band[group])
            normed = (hatted * gain).astype(BF16)
            rows = jnp.concatenate([normed[i] for i in range(8)], axis=1)
            at = pl.multiple_of(window_column(group, odd) - TOK * odd + 16, 16)
            lanes = pl.ds(pl.multiple_of(128 * group, 128), 128)
            zrow[pl.ds(at, KEYS), lanes] = dot(rows, spread_w).astype(BF16)
            return carry

        lax.fori_loop(0, GROUPS, project, 0)

    @pl.when(is_holder)
    def _():
        spread_w = spread_projection(proj_ref[...])
        corner_load.wait()
        hatted, _ = normalise(corner_band[...])
        normed = (hatted * gain_ref[...]).astype(BF16)
        for part in range(2):
            rows = jnp.concatenate([normed[8 * part + i] for i in range(8)], axis=1)
            zcorner[:, 128 * part : 128 * part + 128] = dot(rows, spread_w).astype(BF16)

    cot_load.wait()

    group = iota((16, 128), 1) // CA

    def spread_step(eight, carry):
        rows = cot_ref[pl.ds(pl.multiple_of(16 * eight, 16), 16), :].astype(F32)
        for half in range(2):
            at = pl.multiple_of(256 * eight + 128 * half, 128)
            for chunk in range(16):
                spread[pl.ds(at + 8 * chunk, 8), :] = rows[
                    8 * half : 8 * half + 8, 128 * chunk : 128 * chunk + 128
                ]
        return carry

    lax.fori_loop(0, ATOMS // 16, spread_step, 0, unroll=2)

    pl.semaphore_wait(barrier, greeted)

    def z_part(target, first):
        return zrow.at[pl.ds(key_base(target) + 16, KEYS), pl.ds(first, QTOK * CA)]

    def z_copy(target):
        src = z_part(target, query_base_static(target) * CA)
        return remote(src, patch, send_z.at[target], recv_z, (row, target))

    corner_copy = remote(zcorner, patch_corner, send_c, recv_c, (row, reader))

    def raw_parts(target):
        rows = pl.ds(11 * target, NEAR)
        to_rows = pl.ds(11 * target - query_base_static(target), NEAR)
        first = key_base(target)

        def part(skip, width, parity):
            src = pair_ref.at[rows, pl.ds(first + skip + TOK * parity, width)]
            return src, raw.at[to_rows, pl.ds(skip, width)]

        return [
            (odd == parity, *part(16 if cut_low else 0, KEYS - 16 if cut_low or cut_high else KEYS, parity))
            for parity in range(2)
            for cut_low in (first + TOK * parity < 0,)
            for cut_high in (first + TOK * parity + KEYS > COLS,)
        ]

    def for_raw(target, act):
        for when, src, dst in raw_parts(target):

            @pl.when(when & (col != target))
            def _():
                act(remote(src, dst, send_r.at[target], recv_r, (row, target)), True)

            @pl.when(when & (col == target))
            def _():
                act(pltpu.make_async_copy(src, dst, recv_r), False)

    raw_corner_src = pair_ref.at[
        pl.ds(first_row, 16), pl.ds(pl.multiple_of(first_col, 16), 16)
    ]
    raw_corner_dst = raw.at[pl.ds(16 * odd, 16), pl.ds(pl.multiple_of(32 * odd, 16), 16)]
    raw_corner_copy = remote(raw_corner_src, raw_corner_dst, send_rc, recv_rc, (row, reader))
    raw_corner_local = pltpu.make_async_copy(raw_corner_src, raw_corner_dst, recv_rc)

    @pl.when(is_main)
    def _():
        for target in range(N_COL):

            @pl.when(col != target)
            def _():
                z_copy(target).start()

        patch[...] = zrow[
            pl.ds(pl.multiple_of(key_base(col) + 16, 16), KEYS),
            pl.ds(pl.multiple_of(query_base(col) * CA, 128), QTOK * CA),
        ]

    @pl.when(is_holder & other_device)
    def _():
        corner_copy.start()
        raw_corner_copy.start()

    @pl.when(is_holder & same_device)
    def _():
        patch_corner[...] = zcorner[...]
        raw_corner_local.start()

    halos = [
        remote(src, dst, send_h.at[at], recv_h.at[at], device)
        for at, (src, dst, device) in enumerate(
            (
                (feats_hbm.at[pl.ds(ATOMS - HALO, HALO)], feats_before, ahead),
                (feats_hbm.at[pl.ds(0, HALO)], feats_after, behind),
                (counts_hbm, counts_before, ahead),
                (counts_hbm, counts_after, behind),
            )
        )
    ]
    for copy in halos:
        copy.start()

    @pl.when(is_main)
    def _():
        for target in range(N_COL):
            for_raw(target, lambda copy, far: copy.start())

    eye = channel_eye(LANES)
    eye16 = eye[:256]
    same = (iota((256, 256), 0) // CA) == (iota((256, 256), 1) // CA)

    def mixer(weight, flip):
        left = dot_nt(eye16, weight) if flip else dot(eye16, weight)
        wide = dot_nt(left.astype(BF16), eye16)
        wide = jnp.where(same, wide, 0.0).astype(BF16)
        return jnp.concatenate([wide, wide], axis=0)

    mixers[0] = mixer(first_w_ref[...], False)
    mixers[1] = mixer(second_w_ref[...], False)
    mixers[2] = mixer(third_w_ref[...], True)
    mixers[3] = mixer(second_w_ref[...], True)
    mixers[4] = mixer(first_w_ref[...], True)
    key_tiled[...] = dot(eye, key_w_ref[...]).astype(BF16)
    query_tiled[...] = dot(eye, query_w_ref[...]).astype(BF16)
    eye_t = channel_eye_t(LANES)
    rhs[0:16, :] = jnp.zeros((16, LANES), BF16)
    rhs[16:144, :] = dot_tn(key_w_ref[...], eye_t).astype(BF16)

    def activate(feats):
        floats = feats.astype(F32)
        return floats * jax.nn.sigmoid(floats)

    own_act = activate(feats_ref[...]).astype(BF16)
    act_ext[HALO : HALO + ATOMS] = activate(feats_ref[...])

    lane_is_row = iota((QBLK, LANES), 1) // CA == iota((QBLK, LANES), 0)
    query_wide = dot_tn(query_w_ref[...], eye_t).astype(BF16)
    for block in range(NBLK):
        terms = dot(own_act[QBLK * block : QBLK * block + QBLK], query_wide)
        high, low = split(jnp.where(lane_is_row, terms, 0.0))
        query_high[QBLK * block : QBLK * block + QBLK] = high
        query_low[QBLK * block : QBLK * block + QBLK] = low

    own = counts_ref[...].astype(F32)

    def rows_of(counts, rows):
        return jnp.broadcast_to(counts, (rows, TOK)).astype(BF16)

    def as_mask(flag):
        return jnp.where(flag, 1.0, 0.0).astype(BF16)

    first_query = query_base(col)
    slot = iota((LANES, TOK), 0) // CA + first_query
    slot_index = iota((LANES, TOK), 1)
    own_rows = rows_of(own, 128)
    slot_from[...] = dot_nt(as_mask(slot_index < slot), own_rows)
    slot_to[...] = dot_nt(as_mask(slot_index < slot + 1), own_rows)

    lane_atom_row = (iota((1, LANES), 1) // CA).astype(F32)
    channel_match = (iota((256, 128), 0) % CA) == (iota((256, 128), 1) % CA)

    def block_place(block):
        first = col * ATOMS + block * QBLK
        token = 8 * (first // (8 * MOST)) - first_query
        return first, pl.multiple_of(token * CA, 128)

    def query_hot(block):
        first, at = block_place(block)
        low = slot_from[pl.ds(at, 256), :]
        high = slot_to[pl.ds(at, 256), :]
        parts = []
        for part in range(4):
            atom = lane_atom_row[:, 128 * part : 128 * part + 128] + first.astype(F32)
            hot = (low <= atom) & (atom < high) & channel_match
            parts.append(jnp.where(hot, 1.0, 0.0).astype(BF16))
        return jnp.concatenate(parts, axis=1)

    def key_first(block):
        return col * ATOMS + block * QBLK + start_ref[block]

    def hot_step(block, carry):
        hot_ref[block] = query_hot(block)
        return carry

    lax.fori_loop(0, NBLK, hot_step, 0, unroll=2)

    def swap_step(eight, carry):
        at = 128 * eight
        pieces = [spread[pl.ds(at + atom, 16, stride=8), :] for atom in range(8)]
        pieces = swap_groups(pieces, group)
        to = NBLK * KWIN * (eight % 4) + KWIN * (eight // 4)
        for key in range(8):
            cot[pl.ds(to + key, 16, stride=8), :] = pieces[key]
        return carry

    lax.fori_loop(0, ATOMS // 8, swap_step, 0, unroll=4)

    for copy in halos:
        copy.wait()
    act_ext[0:HALO] = activate(feats_before[...])
    act_ext[HALO + ATOMS : EXT] = activate(feats_after[...])

    base = key_base(col)
    before = counts_before[...].astype(F32)
    after = counts_after[...].astype(F32)

    def lane_bounds(offset):
        token = iota((TOK, 128), 1) + (base + offset)
        index = iota((TOK, 128), 0)
        total = dot(rows_of(own, 8), as_mask(index < token))
        total += dot(rows_of(after, 8), as_mask(index + TOK < token))
        return total - dot(rows_of(before, 8), as_mask(index - TOK >= token))

    def column_bounds(offset):
        token = iota((KEYS, TOK), 0) + (base + offset)
        index = iota((KEYS, TOK), 1)
        total = dot_nt(as_mask(index < token), rows_of(own, 128))
        total += dot_nt(as_mask(index + TOK < token), rows_of(after, 128))
        return total - dot_nt(as_mask(index - TOK >= token), rows_of(before, 128))

    lane = iota((8, 128), 1)
    far = 1.0e6
    lane_from = jnp.where(lane < 48, lane_bounds(0), jnp.where(lane < 112, -far, far))[0:1]
    lane_to = jnp.where(lane < 48, lane_bounds(1), jnp.where(lane < 112, far, -far))[0:1]
    column_from = column_bounds(0)
    column_to = column_bounds(1)

    @pl.when(is_main)
    def _():
        for target in range(N_COL):

            @pl.when(col != target)
            def _():
                z_copy(target).wait_send()

    @pl.when(not_main)
    def _():
        z_copy(0).wait_recv()

    @pl.when(is_holder & other_device)
    def _():
        corner_copy.wait_send()

    @pl.when(is_reader & other_device)
    def _():
        corner_copy.wait_recv()

    @pl.when(is_reader)
    def _():
        at = pl.multiple_of(32 * odd, 16), pl.multiple_of(256 * odd, 128)
        patch[pl.ds(at[0], 16), pl.ds(at[1], 256)] = patch_corner[...]

    def start_step(block, carry):
        _, at = block_place(block)
        hot = hot_ref[block]
        window = start_ref[block] + block * QBLK + HALO
        atom = (iota((KWIN, 128), 0) + key_first(block)).astype(F32)
        mine = pl.ds(pl.multiple_of(block * QBLK, QBLK), QBLK)
        left = jnp.concatenate(
            [
                as_mask((lane_from <= atom) & (atom < lane_to)),
                act_ext[pl.ds(window, KWIN), :].astype(BF16),
            ],
            axis=1,
        )
        right = jnp.concatenate(
            [
                dot(patch[:, pl.ds(at, 256)], hot).astype(BF16),
                query_high[mine, :],
                query_low[mine, :],
                rhs[...],
            ],
            axis=0,
        )
        state[pl.ds(pl.multiple_of(block * KWIN, KWIN), KWIN), :] = dot(left, right)
        return carry

    lax.fori_loop(0, NBLK, start_step, 0, unroll=2)

    atom_low = jnp.where(row == 0, 0, -ROW_ATOMS)
    atom_high = jnp.where(row == N_ROW - 1, ROW_ATOMS, 2 * ROW_ATOMS)

    def slope(value, sigma, act):
        return sigma + act - act * sigma

    def mlp_step(step, carry):
        at = pl.multiple_of(MLP_ROWS * (step // 2), MLP_ROWS)
        place = pl.ds(at, MLP_ROWS), pl.ds(pl.multiple_of(256 * (step % 2), 256), 256)
        value = state[place]
        index = iota((KWIN, 256), 0)
        atom = jnp.concatenate(
            [
                index + key_first(MLP_ROWS // KWIN * (step // 2) + block)
                for block in range(MLP_ROWS // KWIN)
            ],
            axis=0,
        )
        parts = [
            cot[pl.ds(pl.multiple_of(at + NBLK * KWIN * (2 * (step % 2) + part), MLP_ROWS), MLP_ROWS), :]
            for part in range(2)
        ]
        grad = jnp.concatenate(parts, axis=1)
        grad = jnp.where((atom >= atom_low) & (atom < atom_high), grad, 0.0)
        sig_0 = sigmoid(value)
        act_0 = value * sig_0
        one = dot_twice(act_0, mixers[0])
        sig_1 = sigmoid(one)
        act_1 = one * sig_1
        two = dot_twice(act_1, mixers[1])
        sig_2 = sigmoid(two)
        back = dot(grad.astype(BF16), mixers[2, 0:256]) * slope(two, sig_2, two * sig_2)
        back = dot_twice(back, mixers[3]) * slope(one, sig_1, act_1)
        back = dot_twice(back, mixers[4]) * slope(value, sig_0, act_0)
        state[place] = grad + back
        return carry

    lax.fori_loop(0, 2 * NBLK * KWIN // MLP_ROWS, mlp_step, 0)

    key_sum[...] = jnp.zeros_like(key_sum)
    token_sum[...] = jnp.zeros_like(token_sum)

    def sum_step(block, carry):
        _, at = block_place(block)
        window = start_ref[block] + block * QBLK + HALO
        back = state[pl.ds(pl.multiple_of(block * KWIN, KWIN), KWIN), :]
        high, low = split(back)
        by_key = dot(high, key_tiled[...]) + dot(low, key_tiled[...])
        reach = KWIN + HALO
        moved = as_mask(
            iota((reach, KWIN), 0) == iota((reach, KWIN), 1) + (start_ref[block] + HALO)
        )
        by_key_high, by_key_low = split(by_key)
        key_sum[pl.ds(pl.multiple_of(block * QBLK, QBLK), reach), :] += dot(
            moved, by_key_high
        ) + dot(moved, by_key_low)
        over_keys = jnp.sum(back, axis=0, keepdims=True)
        over_keys = jnp.where(lane_is_row, over_keys, 0.0)
        mine = pl.multiple_of(block * QBLK, QBLK)
        query_sum[pl.ds(mine, QBLK), :] = dot_split(over_keys, query_tiled[...])
        atom = (iota((KEYS, 128), 1) + key_first(block)).astype(F32)
        key_hot = as_mask((column_from <= atom) & (atom < column_to))
        by_token = dot(key_hot, high) + dot(key_hot, low)
        high, low = split(by_token)
        hot = hot_ref[block]
        token_sum[:, pl.ds(at, 256)] += dot_nt(high, hot) + dot_nt(low, hot)
        return carry

    lax.fori_loop(0, NBLK, sum_step, 0, unroll=2)

    def token_copy(source):
        row_at, row_count, lane_at, lane_count = TOKEN_PART[source]
        part = pl.ds(row_at, row_count), pl.ds(lane_at, lane_count)
        return remote(
            token_sum.at[part], patches.at[(source, *part)], send_t, recv_t.at[source], (row, half)
        )

    corner_part = token_sum.at[
        pl.ds(pl.multiple_of(32 * odd, 16), 16), pl.ds(pl.multiple_of(256 * odd, 128), 256)
    ]
    token_corner_copy = remote(corner_part, token_corner, send_tc, recv_tc, (row, holder_col))

    for source in range(N_COL):

        @pl.when(not_main & (col == source))
        def _():
            token_copy(source).start()

    @pl.when(is_reader & other_device)
    def _():
        token_corner_copy.start()

    @pl.when(is_reader & same_device)
    def _():
        token_corner[...] = corner_part[...]

    key_halos = [
        remote(src, dst, send_k.at[at], recv_k.at[at], device)
        for at, (src, dst, device) in enumerate(
            (
                (key_sum.at[pl.ds(HALO + ATOMS, HALO)], key_before, ahead),
                (key_sum.at[pl.ds(0, HALO)], key_after, behind),
            )
        )
    ]
    for copy in key_halos:
        copy.start()

    @pl.when(is_main)
    def _():
        for target in range(N_COL):
            for_raw(target, lambda copy, far: copy.wait_send() if far else copy.wait())

    for target in range(N_COL):

        for when, src, dst in raw_parts(target):

            @pl.when(when & not_main & (col == target))
            def _():
                remote(src, dst, send_r.at[target], recv_r, (row, target)).wait_recv()

    @pl.when(is_reader & other_device)
    def _():
        raw_corner_copy.wait_recv()

    @pl.when(is_reader & same_device)
    def _():
        raw_corner_local.wait()

    gain = gain_ref[...]

    def near_step(eight, carry):
        hatted, _ = normalise(raw[pl.ds(8 * eight, 8)])
        normed = (hatted * gain).astype(BF16)
        rows = pl.ds(pl.multiple_of(KEYS * eight, 16), KEYS)
        near_flat[rows, :] = jnp.concatenate([normed[i] for i in range(8)], axis=1)
        high, low = split(token_sum[:, pl.ds(pl.multiple_of(128 * eight, 128), 128)])
        near_high[rows, :] = high
        near_low[rows, :] = low
        return carry

    lax.fori_loop(0, QTOK // 8, near_step, 0)
    wide = dot_tn(near_high[...], near_flat[...]) + dot_tn(near_low[...], near_flat[...])
    weight = wide[0:CA, 0:128]
    for i in range(1, 8):
        weight += wide[CA * i : CA * i + CA, 128 * i : 128 * i + 128]
    weight_sent[0] = weight
    z_copies = [
        remote(weight_sent.at[0], weight_z.at[at], send_wz.at[at], recv_wz.at[at], device)
        for at, device in enumerate(along_z)
    ]
    x_copies = [
        remote(weight_sent.at[1], weight_x.at[at], send_wx.at[at], recv_wx.at[at], device)
        for at, device in enumerate(along_x)
    ]
    row_copies = [
        remote(weight_sent.at[2], weight_row.at[at], send_wr.at[at], recv_wr.at[at], device)
        for at, device in enumerate(along_row)
    ]
    for copy in z_copies:
        copy.start()

    for copy in key_halos:
        copy.wait()
    total = query_sum[...] + key_sum[HALO : HALO + ATOMS]
    lead = total[:HALO] + key_before[...]
    trail = total[ATOMS - HALO :] + key_after[...]
    total = jnp.concatenate([lead, total[HALO : ATOMS - HALO], trail], axis=0)
    floats = feats_ref[...].astype(F32)
    sigma = jax.nn.sigmoid(floats)
    atom_grad_ref[...] = (total * (sigma * (1.0 + floats * (1.0 - sigma)))).astype(BF16)

    for at, copy in enumerate(z_copies):
        copy.wait_recv()
        weight += weight_z[at]
    weight_sent[1] = weight
    for copy in x_copies:
        copy.start()

    spread_wt = spread_projection_t(proj_ref[...])

    def gradient(block, token_rows):
        high, low = split(token_rows)
        hatted, inv_scale = normalise(block)
        wide = dot(high, spread_wt) + dot(low, spread_wt)
        scaled = jnp.stack([wide[:, 128 * i : 128 * i + 128] for i in range(8)]) * gain
        first_mean = jnp.mean(scaled, axis=-1, keepdims=True)
        second_mean = jnp.mean(scaled * hatted, axis=-1, keepdims=True)
        return (inv_scale * (scaled - first_mean - hatted * second_mean)).astype(BF16)

    def grad_out(group):
        return pltpu.make_async_copy(grads.at[group], grads_hbm.at[group], load_sems.at[group])

    corner_out = pltpu.make_async_copy(corner_grads, corner_grads_hbm, corner_load_sem)

    def grad_step(group, carry):
        at = pl.multiple_of(window_column(group, odd) - TOK * odd + 16, 16)
        lanes = pl.ds(pl.multiple_of(128 * group, 128), 128)
        grads[group] = gradient(band[group], tokens[pl.ds(at, KEYS), lanes])
        grad_out(group).start()
        return carry

    @pl.when(is_main)
    def _():
        tokens[...] = jnp.zeros_like(tokens)
        for source in range(N_COL):
            row_at, row_count, lane_at, lane_count = TOKEN_PART[source]
            part = pl.ds(row_at, row_count), pl.ds(lane_at, lane_count)

            @pl.when(col != source)
            def _():
                token_copy(source).wait_recv()

            @pl.when(col == source)
            def _():
                patches[(source, *part)] = token_sum[part]

            at = key_base(source) + 16 + row_at
            lanes = query_base_static(source) * CA + lane_at
            tokens[at : at + row_count, lanes : lanes + lane_count] += patches[(source, *part)]
        lax.fori_loop(0, GROUPS // 2, grad_step, 0)

    @pl.when(is_holder)
    def _():
        @pl.when(other_device)
        def _():
            token_corner_copy.wait_recv()

        for part in range(2):
            corner_grads[8 * part : 8 * part + 8] = gradient(
                corner_band[8 * part : 8 * part + 8],
                token_corner[:, 128 * part : 128 * part + 128],
            )
        corner_out.start()

    for at, copy in enumerate(x_copies):
        copy.wait_recv()
        weight += weight_x[at]
    weight_sent[2] = weight
    for copy in row_copies:
        copy.start()

    @pl.when(is_main)
    def _():
        lax.fori_loop(GROUPS // 2, GROUPS, grad_step, 0)

    for at, copy in enumerate(row_copies):
        copy.wait_recv()
        weight += weight_row[at]
    proj_grad_ref[...] = weight

    for copy in z_copies + x_copies + row_copies:
        copy.wait_send()

    for source in range(N_COL):

        @pl.when(not_main & (col == source))
        def _():
            token_copy(source).wait_send()

    @pl.when(is_reader & other_device)
    def _():
        token_corner_copy.wait_send()

    @pl.when(is_holder & other_device)
    def _():
        raw_corner_copy.wait_send()

    @pl.when(is_main)
    def _():
        def grad_wait(group, carry):
            grad_out(group).wait()
            return carry

        lax.fori_loop(0, GROUPS, grad_wait, 0)

    @pl.when(is_holder)
    def _():
        corner_out.wait()


def band_pass(start, pair_repr, cot, gain, proj, feats, counts, weights):
    vmem = pl.BlockSpec(memory_space=pltpu.VMEM)
    any_spec = pl.BlockSpec(memory_space=pl.ANY)
    dma = pltpu.SemaphoreType.DMA
    return pl.pallas_call(
        band_kernel,
        out_shape=(
            jax.ShapeDtypeStruct((GROUPS, 8, KEYS, CP), BF16),
            jax.ShapeDtypeStruct((16, 16, CP), BF16),
            jax.ShapeDtypeStruct((ATOMS, CP), BF16),
            jax.ShapeDtypeStruct((CA, CP), F32),
        ),
        in_specs=[pl.BlockSpec(memory_space=pltpu.SMEM)] + [any_spec] * 11,
        out_specs=(any_spec, any_spec, vmem, vmem),
        scratch_shapes=[
            pltpu.VMEM((1, CP), F32),
            pltpu.VMEM((CA, CP), BF16),
            pltpu.VMEM((ATOMS, CP), BF16),
            pltpu.VMEM((1, TOK), jnp.int32),
            pltpu.VMEM((CA, CP), BF16),
            pltpu.VMEM((CA, CP), BF16),
            pltpu.VMEM((CA, CA), BF16),
            pltpu.VMEM((CA, CA), BF16),
            pltpu.VMEM((CA, CA), BF16),
            pltpu.VMEM((GROUPS, 8, KEYS, CP), BF16),
            pltpu.VMEM((16, 16, CP), BF16),
            pltpu.VMEM((GROUPS, 8, KEYS, CP), BF16),
            pltpu.VMEM((16, 16, CP), BF16),
            pltpu.VMEM((128, TOK * CA), BF16),
            pltpu.VMEM((16, 256), BF16),
            pltpu.VMEM((KEYS, QTOK * CA), BF16),
            pltpu.VMEM((16, 256), BF16),
            pltpu.VMEM((QTOK, KEYS, CP), BF16),
            pltpu.VMEM((HALO, CP), BF16),
            pltpu.VMEM((HALO, CP), BF16),
            pltpu.VMEM((1, TOK), jnp.int32),
            pltpu.VMEM((1, TOK), jnp.int32),
            pltpu.VMEM((ATOMS, KWIN * CA), BF16),
            pltpu.VMEM((EXT, CP), F32),
            pltpu.VMEM((144, LANES), BF16),
            pltpu.VMEM((ATOMS, LANES), BF16),
            pltpu.VMEM((ATOMS, LANES), BF16),
            pltpu.VMEM((ATOMS * 16, 128), F32),
            pltpu.VMEM((4 * NBLK * KWIN, 128), F32),
            pltpu.VMEM((NBLK * KWIN, LANES), F32),
            pltpu.VMEM((5, 512, 256), BF16),
            pltpu.VMEM((LANES, CP), BF16),
            pltpu.VMEM((LANES, CP), BF16),
            pltpu.VMEM((LANES, 128), F32),
            pltpu.VMEM((LANES, 128), F32),
            pltpu.VMEM((NBLK, 256, LANES), BF16),
            pltpu.VMEM((EXT, CP), F32),
            pltpu.VMEM((ATOMS, CP), F32),
            pltpu.VMEM((KEYS, QTOK * CA), F32),
            pltpu.VMEM((HALO, CP), F32),
            pltpu.VMEM((HALO, CP), F32),
            pltpu.VMEM((N_COL, KEYS, QTOK * CA), F32),
            pltpu.VMEM((16, 256), F32),
            pltpu.VMEM((128, TOK * CA), F32),
            pltpu.VMEM((QTOK // 8 * KEYS, 8 * CP), BF16),
            pltpu.VMEM((QTOK // 8 * KEYS, 128), BF16),
            pltpu.VMEM((QTOK // 8 * KEYS, 128), BF16),
            pltpu.VMEM((3, CA, CP), F32),
            pltpu.VMEM((3, CA, CP), F32),
            pltpu.VMEM((3, CA, CP), F32),
            pltpu.VMEM((N_COL - 1, CA, CP), F32),
            dma((9,)),
            dma((GROUPS,)),
            dma,
            dma,
            dma((N_COL,)),
            dma,
            dma,
            dma,
            dma((N_COL,)),
            dma,
            dma,
            dma,
            dma((4,)),
            dma((4,)),
            dma,
            dma((N_COL,)),
            dma,
            dma,
            dma((2,)),
            dma((2,)),
            dma((3,)),
            dma((3,)),
            dma((3,)),
            dma((3,)),
            dma((N_COL - 1,)),
            dma((N_COL - 1,)),
        ],
        compiler_params=pltpu.CompilerParams(
            collective_id=0, has_side_effects=True, vmem_limit_bytes=VMEM_LIMIT
        ),
        name="band_pass",
    )(start, pair_repr, cot, gain, proj, feats, counts, *weights)


def place_kernel(
    grads_ref,
    corner_ref,
    atom_ref,
    proj_ref,
    pair_grad_ref,
    atom_grad_ref,
    proj_grad_ref,
    zeros,
    held,
    sems,
):
    row = lax.axis_index("row")
    col = lax.axis_index("col")
    odd = row % 2
    half = row // 2
    is_main = col == half
    holder = jnp.where(odd == 0, half - 1, half + 1)
    is_holder = col == holder
    zeros[...] = jnp.zeros_like(zeros)

    def blank(group, first, last, sem):
        return pltpu.make_async_copy(
            zeros.at[:, pl.ds(0, last - first)],
            pair_grad_ref.at[pl.ds(8 * group, 8), pl.ds(first, last - first)],
            sem,
        )

    def pieces(kind, parity):
        copies, loads, stores = [], [], []
        for group in range(GROUPS):
            first, last, source = 0, 0, None
            if kind == "band":
                first = 16 * ((8 * group - 13 + 16) // 16) - 16 + TOK * parity
                first = min(max(first, 0), COLS - KEYS)
                last, source = first + KEYS, (grads_ref.at[group], held.at[group])
            elif kind == "corner" and group // 2 == 5 * parity:
                first = 176 * (1 - parity)
                last = first + 16
                source = (
                    corner_ref.at[pl.ds(8 * (group % 2), 8)],
                    held.at[group, :, pl.ds(0, 16)],
                )
            if source is not None:
                to = pair_grad_ref.at[pl.ds(8 * group, 8), pl.ds(first, last - first)]
                loads.append(pltpu.make_async_copy(*source, sems.at[group, 0]))
                stores.append(pltpu.make_async_copy(source[1], to, sems.at[group, 3]))
            if first > 0:
                copies.append(blank(group, 0, first, sems.at[group, 1]))
            if last < COLS:
                copies.append(blank(group, last, COLS, sems.at[group, 2]))
        return copies, loads, stores

    cases = (
        (is_main & (odd == 0), "band", 0),
        (is_main & (odd == 1), "band", 1),
        (is_holder & (odd == 0), "corner", 0),
        (is_holder & (odd == 1), "corner", 1),
        (jnp.logical_not(is_main | is_holder), "none", 0),
    )
    for when, kind, parity in cases:

        @pl.when(when)
        def _():
            copies, loads, stores = pieces(kind, parity)
            for copy in loads + copies:
                copy.start()
            for load, store in zip(loads, stores):
                load.wait()
                store.start()
            for copy in copies + stores:
                copy.wait()

    atom_grad_ref[...] = atom_ref[...]
    proj_grad_ref[...] = proj_ref[...]


def place(grads, corner, atom_grad, proj_grad):
    vmem = pl.BlockSpec(memory_space=pltpu.VMEM)
    any_spec = pl.BlockSpec(memory_space=pl.ANY)
    return pl.pallas_call(
        place_kernel,
        out_shape=(
            jax.ShapeDtypeStruct((TOK, COLS, CP), BF16),
            jax.ShapeDtypeStruct((ATOMS, CP), BF16),
            jax.ShapeDtypeStruct((CA, CP), F32),
        ),
        in_specs=[any_spec, any_spec, vmem, vmem],
        out_specs=(any_spec, vmem, vmem),
        scratch_shapes=[
            pltpu.VMEM((8, COLS, CP), BF16),
            pltpu.VMEM((GROUPS, 8, KEYS, CP), BF16),
            pltpu.SemaphoreType.DMA((GROUPS, 4)),
        ],
        compiler_params=pltpu.CompilerParams(vmem_limit_bytes=VMEM_LIMIT),
        name="place",
    )(grads, corner, atom_grad, proj_grad)


def shards(
    pair_repr,
    pair_gain,
    proj_weight,
    query_weight,
    key_weight,
    mlp_first,
    mlp_second,
    mlp_third,
    atom_feats,
    token_counts,
    key_start,
    pair_cotangent,
):
    grads, corner, atom_grad, proj_grad = band_pass(
        key_start,
        pair_repr,
        pair_cotangent,
        pair_gain.reshape(1, CP),
        proj_weight.T,
        atom_feats,
        token_counts,
        (query_weight.T, key_weight.T, mlp_first, mlp_second, mlp_third),
    )
    pair_grad, atom_grad, proj_grad = place(grads, corner, atom_grad, proj_grad)
    return pair_grad, atom_grad, proj_grad.T


def solution(mesh):
    placed = (
        P("row", "col", None),
        P(),
        P(),
        P(),
        P(),
        P(),
        P(),
        P(),
        P(("row", "col"), None),
        P("row", None),
        P(("row", "col")),
        P(("row", "col"), None),
    )
    return jax.shard_map(
        shards,
        mesh=mesh,
        in_specs=placed,
        out_specs=(P("row", "col", None), P(("row", "col"), None), P()),
        check_vma=False,
    )
```

```python
import jax
import jax.numpy as jnp
from jax import lax
from jax.experimental import pallas as pl
from jax.experimental.pallas import tpu as pltpu
from jax.sharding import PartitionSpec as P

F32 = jnp.float32
BF16 = jnp.bfloat16
MESH = pl.DeviceIdType.MESH

N_ROW = 16
N_COL = 8
TOK = 96
COLS = 192
CP = 128
CA = 16
QBLK = 32
KWIN = 128
MOST = 23
ATOMS = 256
ROW_ATOMS = 2048
SLACK = TOK * MOST - ROW_ATOMS
HALO = KWIN - QBLK
EXT = ATOMS + 2 * HALO
NBLK = ATOMS // QBLK
LANES = QBLK * CA
KEYS = 48
QTOK = 32
GROUPS = TOK // 8
VMEM_LIMIT = 56 * 1024 * 1024
MLP_ROWS = 1024
NEAR = 19
TOKEN_PART = (
    (0, 40, 0, 384),
    (0, 40, 0, 384),
    (0, 32, 0, 512),
    (8, 32, 0, 384),
    (8, 32, 0, 384),
    (0, 32, 0, 512),
    (8, 40, 0, 384),
    (8, 40, 128, 384),
)


def key_base(col):
    return 16 * ((11 * col - 5 + 16) // 16) - 16


def query_base(col):
    return jnp.minimum(8 * ((11 * col) // 8), TOK - QTOK)


def query_base_static(col):
    return min(8 * ((11 * col) // 8), TOK - QTOK)


def iota(shape, dim):
    return lax.broadcasted_iota(jnp.int32, shape, dim)


def dot(a, b):
    return jnp.dot(a, b, preferred_element_type=F32)


def dot_nt(a, b):
    return lax.dot_general(a, b, (((1,), (1,)), ((), ())), preferred_element_type=F32)


def dot_tn(a, b):
    return lax.dot_general(a, b, (((0,), (0,)), ((), ())), preferred_element_type=F32)


def split(x):
    high = x.astype(BF16)
    low = (x - high.astype(F32)).astype(BF16)
    return high, low


def dot_split(x, w):
    high, low = split(x)
    return dot(high, w) + dot(low, w)


def dot_twice(x, w):
    return dot(jnp.concatenate(split(x), axis=1), w)


def sigmoid(x):
    return 0.5 * jnp.tanh(0.5 * x) + 0.5


def mesh_place():
    row = lax.axis_index("row")
    col = lax.axis_index("col")
    return row, col


def normalise(block):
    floats = block.astype(F32)
    centre = floats - jnp.mean(floats, axis=-1, keepdims=True)
    spread = jnp.mean(centre * centre, axis=-1, keepdims=True)
    inv_scale = lax.rsqrt(spread + 1e-05)
    return centre * inv_scale, inv_scale


def channel_eye(rows):
    return ((iota((rows, CA), 0) & (CA - 1)) == iota((rows, CA), 1)).astype(F32).astype(BF16)


def channel_eye_t(lanes):
    return ((iota((CA, lanes), 1) & (CA - 1)) == iota((CA, lanes), 0)).astype(F32).astype(BF16)


def spread_projection(proj):
    eye_t = channel_eye_t(CP)
    wide = dot_tn(proj, eye_t)
    lane = iota((CP, CP), 1) // CA
    return jnp.concatenate(
        [jnp.where(lane == i, wide, 0.0).astype(BF16) for i in range(8)], axis=0
    )


def spread_projection_t(proj):
    eye = channel_eye(CP)
    tall = dot(eye, proj)
    row = iota((CP, CP), 0) // CA
    return jnp.concatenate(
        [jnp.where(row == i, tall, 0.0).astype(BF16) for i in range(8)], axis=1
    )


def window_column(group, odd):
    first = 16 * ((8 * group - 13 + 16) // 16) - 16
    return jnp.clip(first + TOK * odd, 0, COLS - KEYS)


def corner_place(odd):
    return 80 * odd, 176 * (1 - odd)


def swap_groups(pieces, group):
    for bit in (1, 2, 4):
        take = (group & bit) != 0
        swapped = list(pieces)
        for at in range(8):
            if at & bit == 0:
                one, two = pieces[at], pieces[at | bit]
                swapped[at] = jnp.where(take, pltpu.roll(two, CA * bit, 1), one)
                swapped[at | bit] = jnp.where(take, two, pltpu.roll(one, 128 - CA * bit, 1))
        pieces = swapped
    return pieces


def neighbours(row, col):
    ahead = (
        jnp.where(col == N_COL - 1, lax.rem(row + 1, N_ROW), row),
        lax.rem(col + 1, N_COL),
    )
    behind = (
        jnp.where(col == 0, lax.rem(row + N_ROW - 1, N_ROW), row),
        lax.rem(col + N_COL - 1, N_COL),
    )
    return ahead, behind


def like_places(row, col):
    return [(lax.rem(row + step, N_ROW), col) for step in range(1, N_ROW)]


def band_kernel(
    start_ref,
    pair_ref,
    cot_hbm,
    gain_hbm,
    proj_hbm,
    feats_hbm,
    counts_hbm,
    query_w_hbm,
    key_w_hbm,
    first_w_hbm,
    second_w_hbm,
    third_w_hbm,
    grads_hbm,
    corner_grads_hbm,
    atom_grad_ref,
    proj_grad_ref,
    gain_ref,
    proj_ref,
    feats_ref,
    counts_ref,
    query_w_ref,
    key_w_ref,
    first_w_ref,
    second_w_ref,
    third_w_ref,
    grads,
    corner_grads,
    band,
    corner_band,
    zrow,
    zcorner,
    patch,
    patch_corner,
    raw,
    feats_before,
    feats_after,
    counts_before,
    counts_after,
    cot_ref,
    act_ext,
    rhs,
    query_high,
    query_low,
    spread,
    cot,
    state,
    mixers,
    key_tiled,
    query_tiled,
    slot_from,
    slot_to,
    hot_ref,
    key_sum,
    query_sum,
    token_sum,
    key_before,
    key_after,
    patches,
    token_corner,
    tokens,
    near_flat,
    near_high,
    near_low,
    weight_sent,
    weight_row,
    weight_grid,
    small_sems,
    load_sems,
    cot_sem,
    corner_load_sem,
    send_z,
    recv_z,
    send_c,
    recv_c,
    send_r,
    recv_r,
    send_rc,
    recv_rc,
    send_h,
    recv_h,
    send_t,
    recv_t,
    send_tc,
    recv_tc,
    send_k,
    recv_k,
    send_wr,
    recv_wr,
    send_wg,
    recv_wg,
):
    row = lax.axis_index("row")
    col = lax.axis_index("col")
    odd = row % 2
    half = row // 2
    is_main = col == half
    not_main = col != half
    holder = jnp.where(odd == 0, half - 1, half + 1)
    reader = (N_COL - 1) * odd
    exists = (holder >= 0) & (holder < N_COL)
    is_holder = exists & (col == holder)
    is_reader = exists & (col == reader)
    same_device = holder == reader
    other_device = holder != reader
    holder_col = jnp.clip(holder, 0, N_COL - 1)
    ahead, behind = neighbours(row, col)
    along_grid = like_places(row, col)
    along_row = [(row, lax.rem(col + step, N_COL)) for step in range(1, N_COL)]

    def remote(src, dst, send, recv, device):
        return pltpu.make_async_remote_copy(
            src_ref=src,
            dst_ref=dst,
            send_sem=send,
            recv_sem=recv,
            device_id=device,
            device_id_type=MESH,
        )

    raw[...] = jnp.zeros_like(raw)

    barrier = pltpu.get_barrier_semaphore()

    def greet(device):
        pl.semaphore_signal(barrier, inc=1, device_id=device, device_id_type=MESH)

    @pl.when(col == 0)
    def _():
        greet(behind)

    @pl.when(col == N_COL - 1)
    def _():
        greet(ahead)

    for device in along_row + along_grid:
        greet(device)
    greeted = N_COL + N_ROW - 2 + jnp.where((col == 0) | (col == N_COL - 1), 1, 0)

    def window_copy(group):
        first = pl.multiple_of(window_column(group, odd), 16)
        return pltpu.make_async_copy(
            pair_ref.at[pl.ds(8 * group, 8), pl.ds(first, KEYS)],
            band.at[group],
            load_sems.at[group],
        )

    first_row, first_col = corner_place(odd)
    corner_load = pltpu.make_async_copy(
        pair_ref.at[pl.ds(first_row, 16), pl.ds(pl.multiple_of(first_col, 16), 16)],
        corner_band,
        corner_load_sem,
    )
    cot_load = pltpu.make_async_copy(cot_hbm, cot_ref, cot_sem)

    @pl.when(is_main)
    def _():
        for group in range(GROUPS):
            window_copy(group).start()

    @pl.when(is_holder)
    def _():
        corner_load.start()

    cot_load.start()
    smalls = [
        pltpu.make_async_copy(src, dst, small_sems.at[at])
        for at, (src, dst) in enumerate(
            (
                (gain_hbm, gain_ref),
                (proj_hbm, proj_ref),
                (feats_hbm, feats_ref),
                (counts_hbm, counts_ref),
                (query_w_hbm, query_w_ref),
                (key_w_hbm, key_w_ref),
                (first_w_hbm, first_w_ref),
                (second_w_hbm, second_w_ref),
                (third_w_hbm, third_w_ref),
            )
        )
    ]
    for copy in smalls:
        copy.start()
    for copy in smalls:
        copy.wait()

    @pl.when(is_main)
    def _():
        zrow[...] = jnp.zeros_like(zrow)
        spread_w = spread_projection(proj_ref[...])
        gain = gain_ref[...]

        def project(group, carry):
            window_copy(group).wait()
            hatted, _ = normalise(band[group])
            normed = (hatted * gain).astype(BF16)
            rows = jnp.concatenate([normed[i] for i in range(8)], axis=1)
            at = pl.multiple_of(window_column(group, odd) - TOK * odd + 16, 16)
            lanes = pl.ds(pl.multiple_of(128 * group, 128), 128)
            zrow[pl.ds(at, KEYS), lanes] = dot(rows, spread_w).astype(BF16)
            return carry

        lax.fori_loop(0, GROUPS, project, 0)

    @pl.when(is_holder)
    def _():
        spread_w = spread_projection(proj_ref[...])
        corner_load.wait()
        hatted, _ = normalise(corner_band[...])
        normed = (hatted * gain_ref[...]).astype(BF16)
        for part in range(2):
            rows = jnp.concatenate([normed[8 * part + i] for i in range(8)], axis=1)
            zcorner[:, 128 * part : 128 * part + 128] = dot(rows, spread_w).astype(BF16)

    cot_load.wait()

    group = iota((16, 128), 1) // CA

    def spread_step(eight, carry):
        rows = cot_ref[pl.ds(pl.multiple_of(16 * eight, 16), 16), :].astype(F32)
        for half in range(2):
            at = pl.multiple_of(256 * eight + 128 * half, 128)
            for chunk in range(16):
                spread[pl.ds(at + 8 * chunk, 8), :] = rows[
                    8 * half : 8 * half + 8, 128 * chunk : 128 * chunk + 128
                ]
        return carry

    lax.fori_loop(0, ATOMS // 16, spread_step, 0, unroll=2)

    pl.semaphore_wait(barrier, greeted)

    def z_part(target, first):
        return zrow.at[pl.ds(key_base(target) + 16, KEYS), pl.ds(first, QTOK * CA)]

    def z_copy(target):
        src = z_part(target, query_base_static(target) * CA)
        return remote(src, patch, send_z.at[target], recv_z, (row, target))

    corner_copy = remote(zcorner, patch_corner, send_c, recv_c, (row, reader))

    def raw_parts(target):
        rows = pl.ds(11 * target, NEAR)
        to_rows = pl.ds(11 * target - query_base_static(target), NEAR)
        first = key_base(target)

        def part(skip, width, parity):
            src = pair_ref.at[rows, pl.ds(first + skip + TOK * parity, width)]
            return src, raw.at[to_rows, pl.ds(skip, width)]

        return [
            (odd == parity, *part(16 if cut_low else 0, KEYS - 16 if cut_low or cut_high else KEYS, parity))
            for parity in range(2)
            for cut_low in (first + TOK * parity < 0,)
            for cut_high in (first + TOK * parity + KEYS > COLS,)
        ]

    def for_raw(target, act):
        for when, src, dst in raw_parts(target):

            @pl.when(when & (col != target))
            def _():
                act(remote(src, dst, send_r.at[target], recv_r, (row, target)), True)

            @pl.when(when & (col == target))
            def _():
                act(pltpu.make_async_copy(src, dst, recv_r), False)

    raw_corner_src = pair_ref.at[
        pl.ds(first_row, 16), pl.ds(pl.multiple_of(first_col, 16), 16)
    ]
    raw_corner_dst = raw.at[pl.ds(16 * odd, 16), pl.ds(pl.multiple_of(32 * odd, 16), 16)]
    raw_corner_copy = remote(raw_corner_src, raw_corner_dst, send_rc, recv_rc, (row, reader))
    raw_corner_local = pltpu.make_async_copy(raw_corner_src, raw_corner_dst, recv_rc)

    @pl.when(is_main)
    def _():
        for target in range(N_COL):

            @pl.when(col != target)
            def _():
                z_copy(target).start()

        patch[...] = zrow[
            pl.ds(pl.multiple_of(key_base(col) + 16, 16), KEYS),
            pl.ds(pl.multiple_of(query_base(col) * CA, 128), QTOK * CA),
        ]

    @pl.when(is_holder & other_device)
    def _():
        corner_copy.start()
        raw_corner_copy.start()

    @pl.when(is_holder & same_device)
    def _():
        patch_corner[...] = zcorner[...]
        raw_corner_local.start()

    halos = [
        remote(src, dst, send_h.at[at], recv_h.at[at], device)
        for at, (src, dst, device) in enumerate(
            (
                (feats_hbm.at[pl.ds(ATOMS - HALO, HALO)], feats_before, ahead),
                (feats_hbm.at[pl.ds(0, HALO)], feats_after, behind),
                (counts_hbm, counts_before, ahead),
                (counts_hbm, counts_after, behind),
            )
        )
    ]
    for copy in halos:
        copy.start()

    @pl.when(is_main)
    def _():
        for target in range(N_COL):
            for_raw(target, lambda copy, far: copy.start())

    eye = channel_eye(LANES)
    eye16 = eye[:256]
    same = (iota((256, 256), 0) // CA) == (iota((256, 256), 1) // CA)

    def mixer(weight, flip):
        left = dot_nt(eye16, weight) if flip else dot(eye16, weight)
        wide = dot_nt(left.astype(BF16), eye16)
        wide = jnp.where(same, wide, 0.0).astype(BF16)
        return jnp.concatenate([wide, wide], axis=0)

    mixers[0] = mixer(first_w_ref[...], False)
    mixers[1] = mixer(second_w_ref[...], False)
    mixers[2] = mixer(third_w_ref[...], True)
    mixers[3] = mixer(second_w_ref[...], True)
    mixers[4] = mixer(first_w_ref[...], True)
    key_tiled[...] = dot(eye, key_w_ref[...]).astype(BF16)
    query_tiled[...] = dot(eye, query_w_ref[...]).astype(BF16)
    eye_t = channel_eye_t(LANES)
    rhs[0:16, :] = jnp.zeros((16, LANES), BF16)
    rhs[16:144, :] = dot_tn(key_w_ref[...], eye_t).astype(BF16)

    def activate(feats):
        floats = feats.astype(F32)
        return floats * jax.nn.sigmoid(floats)

    own_act = activate(feats_ref[...]).astype(BF16)
    act_ext[HALO : HALO + ATOMS] = activate(feats_ref[...])

    lane_is_row = iota((QBLK, LANES), 1) // CA == iota((QBLK, LANES), 0)
    query_wide = dot_tn(query_w_ref[...], eye_t).astype(BF16)
    for block in range(NBLK):
        terms = dot(own_act[QBLK * block : QBLK * block + QBLK], query_wide)
        high, low = split(jnp.where(lane_is_row, terms, 0.0))
        query_high[QBLK * block : QBLK * block + QBLK] = high
        query_low[QBLK * block : QBLK * block + QBLK] = low

    own = counts_ref[...].astype(F32)

    def rows_of(counts, rows):
        return jnp.broadcast_to(counts, (rows, TOK)).astype(BF16)

    def as_mask(flag):
        return jnp.where(flag, 1.0, 0.0).astype(BF16)

    first_query = query_base(col)
    slot = iota((LANES, TOK), 0) // CA + first_query
    slot_index = iota((LANES, TOK), 1)
    own_rows = rows_of(own, 128)
    slot_from[...] = dot_nt(as_mask(slot_index < slot), own_rows)
    slot_to[...] = dot_nt(as_mask(slot_index < slot + 1), own_rows)

    lane_atom_row = (iota((1, LANES), 1) // CA).astype(F32)
    channel_match = (iota((256, 128), 0) % CA) == (iota((256, 128), 1) % CA)

    def block_place(block):
        first = col * ATOMS + block * QBLK
        token = 8 * (first // (8 * MOST)) - first_query
        return first, pl.multiple_of(token * CA, 128)

    def query_hot(block):
        first, at = block_place(block)
        low = slot_from[pl.ds(at, 256), :]
        high = slot_to[pl.ds(at, 256), :]
        parts = []
        for part in range(4):
            atom = lane_atom_row[:, 128 * part : 128 * part + 128] + first.astype(F32)
            hot = (low <= atom) & (atom < high) & channel_match
            parts.append(jnp.where(hot, 1.0, 0.0).astype(BF16))
        return jnp.concatenate(parts, axis=1)

    def key_first(block):
        return col * ATOMS + block * QBLK + start_ref[block]

    def hot_step(block, carry):
        hot_ref[block] = query_hot(block)
        return carry

    lax.fori_loop(0, NBLK, hot_step, 0, unroll=2)

    def swap_step(eight, carry):
        at = 128 * eight
        pieces = [spread[pl.ds(at + atom, 16, stride=8), :] for atom in range(8)]
        pieces = swap_groups(pieces, group)
        to = NBLK * KWIN * (eight % 4) + KWIN * (eight // 4)
        for key in range(8):
            cot[pl.ds(to + key, 16, stride=8), :] = pieces[key]
        return carry

    lax.fori_loop(0, ATOMS // 8, swap_step, 0, unroll=4)

    for copy in halos:
        copy.wait()
    act_ext[0:HALO] = activate(feats_before[...])
    act_ext[HALO + ATOMS : EXT] = activate(feats_after[...])

    base = key_base(col)
    before = counts_before[...].astype(F32)
    after = counts_after[...].astype(F32)

    def lane_bounds(offset):
        token = iota((TOK, 128), 1) + (base + offset)
        index = iota((TOK, 128), 0)
        total = dot(rows_of(own, 8), as_mask(index < token))
        total += dot(rows_of(after, 8), as_mask(index + TOK < token))
        return total - dot(rows_of(before, 8), as_mask(index - TOK >= token))

    def column_bounds(offset):
        token = iota((KEYS, TOK), 0) + (base + offset)
        index = iota((KEYS, TOK), 1)
        total = dot_nt(as_mask(index < token), rows_of(own, 128))
        total += dot_nt(as_mask(index + TOK < token), rows_of(after, 128))
        return total - dot_nt(as_mask(index - TOK >= token), rows_of(before, 128))

    lane = iota((8, 128), 1)
    far = 1.0e6
    lane_from = jnp.where(lane < 48, lane_bounds(0), jnp.where(lane < 112, -far, far))[0:1]
    lane_to = jnp.where(lane < 48, lane_bounds(1), jnp.where(lane < 112, far, -far))[0:1]
    column_from = column_bounds(0)
    column_to = column_bounds(1)

    @pl.when(is_main)
    def _():
        for target in range(N_COL):

            @pl.when(col != target)
            def _():
                z_copy(target).wait_send()

    @pl.when(not_main)
    def _():
        z_copy(0).wait_recv()

    @pl.when(is_holder & other_device)
    def _():
        corner_copy.wait_send()

    @pl.when(is_reader & other_device)
    def _():
        corner_copy.wait_recv()

    @pl.when(is_reader)
    def _():
        at = pl.multiple_of(32 * odd, 16), pl.multiple_of(256 * odd, 128)
        patch[pl.ds(at[0], 16), pl.ds(at[1], 256)] = patch_corner[...]

    def start_step(block, carry):
        _, at = block_place(block)
        hot = hot_ref[block]
        window = start_ref[block] + block * QBLK + HALO
        atom = (iota((KWIN, 128), 0) + key_first(block)).astype(F32)
        mine = pl.ds(pl.multiple_of(block * QBLK, QBLK), QBLK)
        left = jnp.concatenate(
            [
                as_mask((lane_from <= atom) & (atom < lane_to)),
                act_ext[pl.ds(window, KWIN), :].astype(BF16),
            ],
            axis=1,
        )
        right = jnp.concatenate(
            [
                dot(patch[:, pl.ds(at, 256)], hot).astype(BF16),
                query_high[mine, :],
                query_low[mine, :],
                rhs[...],
            ],
            axis=0,
        )
        state[pl.ds(pl.multiple_of(block * KWIN, KWIN), KWIN), :] = dot(left, right)
        return carry

    lax.fori_loop(0, NBLK, start_step, 0, unroll=2)

    atom_low = jnp.where(row == 0, 0, -ROW_ATOMS)
    atom_high = jnp.where(row == N_ROW - 1, ROW_ATOMS, 2 * ROW_ATOMS)

    def slope(value, sigma, act):
        return sigma + act - act * sigma

    def mlp_step(step, carry):
        at = pl.multiple_of(MLP_ROWS * (step // 2), MLP_ROWS)
        place = pl.ds(at, MLP_ROWS), pl.ds(pl.multiple_of(256 * (step % 2), 256), 256)
        value = state[place]
        index = iota((KWIN, 256), 0)
        atom = jnp.concatenate(
            [
                index + key_first(MLP_ROWS // KWIN * (step // 2) + block)
                for block in range(MLP_ROWS // KWIN)
            ],
            axis=0,
        )
        parts = [
            cot[pl.ds(pl.multiple_of(at + NBLK * KWIN * (2 * (step % 2) + part), MLP_ROWS), MLP_ROWS), :]
            for part in range(2)
        ]
        grad = jnp.concatenate(parts, axis=1)
        grad = jnp.where((atom >= atom_low) & (atom < atom_high), grad, 0.0)
        sig_0 = sigmoid(value)
        act_0 = value * sig_0
        one = dot_twice(act_0, mixers[0])
        sig_1 = sigmoid(one)
        act_1 = one * sig_1
        two = dot_twice(act_1, mixers[1])
        sig_2 = sigmoid(two)
        back = dot(grad.astype(BF16), mixers[2, 0:256]) * slope(two, sig_2, two * sig_2)
        back = dot_twice(back, mixers[3]) * slope(one, sig_1, act_1)
        back = dot_twice(back, mixers[4]) * slope(value, sig_0, act_0)
        state[place] = grad + back
        return carry

    lax.fori_loop(0, 2 * NBLK * KWIN // MLP_ROWS, mlp_step, 0)

    key_sum[...] = jnp.zeros_like(key_sum)
    token_sum[...] = jnp.zeros_like(token_sum)

    def sum_step(block, carry):
        _, at = block_place(block)
        window = start_ref[block] + block * QBLK + HALO
        back = state[pl.ds(pl.multiple_of(block * KWIN, KWIN), KWIN), :]
        high, low = split(back)
        by_key = dot(high, key_tiled[...]) + dot(low, key_tiled[...])
        reach = KWIN + HALO
        moved = as_mask(
            iota((reach, KWIN), 0) == iota((reach, KWIN), 1) + (start_ref[block] + HALO)
        )
        by_key_high, by_key_low = split(by_key)
        key_sum[pl.ds(pl.multiple_of(block * QBLK, QBLK), reach), :] += dot(
            moved, by_key_high
        ) + dot(moved, by_key_low)
        over_keys = jnp.sum(back, axis=0, keepdims=True)
        over_keys = jnp.where(lane_is_row, over_keys, 0.0)
        mine = pl.multiple_of(block * QBLK, QBLK)
        query_sum[pl.ds(mine, QBLK), :] = dot_split(over_keys, query_tiled[...])
        atom = (iota((KEYS, 128), 1) + key_first(block)).astype(F32)
        key_hot = as_mask((column_from <= atom) & (atom < column_to))
        by_token = dot(key_hot, high) + dot(key_hot, low)
        high, low = split(by_token)
        hot = hot_ref[block]
        token_sum[:, pl.ds(at, 256)] += dot_nt(high, hot) + dot_nt(low, hot)
        return carry

    lax.fori_loop(0, NBLK, sum_step, 0, unroll=2)

    def token_copy(source):
        row_at, row_count, lane_at, lane_count = TOKEN_PART[source]
        part = pl.ds(row_at, row_count), pl.ds(lane_at, lane_count)
        return remote(
            token_sum.at[part], patches.at[(source, *part)], send_t, recv_t.at[source], (row, half)
        )

    corner_part = token_sum.at[
        pl.ds(pl.multiple_of(32 * odd, 16), 16), pl.ds(pl.multiple_of(256 * odd, 128), 256)
    ]
    token_corner_copy = remote(corner_part, token_corner, send_tc, recv_tc, (row, holder_col))

    for source in range(N_COL):

        @pl.when(not_main & (col == source))
        def _():
            token_copy(source).start()

    @pl.when(is_reader & other_device)
    def _():
        token_corner_copy.start()

    @pl.when(is_reader & same_device)
    def _():
        token_corner[...] = corner_part[...]

    key_halos = [
        remote(src, dst, send_k.at[at], recv_k.at[at], device)
        for at, (src, dst, device) in enumerate(
            (
                (key_sum.at[pl.ds(HALO + ATOMS, HALO)], key_before, ahead),
                (key_sum.at[pl.ds(0, HALO)], key_after, behind),
            )
        )
    ]
    for copy in key_halos:
        copy.start()

    @pl.when(is_main)
    def _():
        for target in range(N_COL):
            for_raw(target, lambda copy, far: copy.wait_send() if far else copy.wait())

    for target in range(N_COL):

        for when, src, dst in raw_parts(target):

            @pl.when(when & not_main & (col == target))
            def _():
                remote(src, dst, send_r.at[target], recv_r, (row, target)).wait_recv()

    @pl.when(is_reader & other_device)
    def _():
        raw_corner_copy.wait_recv()

    @pl.when(is_reader & same_device)
    def _():
        raw_corner_local.wait()

    gain = gain_ref[...]

    def near_step(eight, carry):
        hatted, _ = normalise(raw[pl.ds(8 * eight, 8)])
        normed = (hatted * gain).astype(BF16)
        rows = pl.ds(pl.multiple_of(KEYS * eight, 16), KEYS)
        near_flat[rows, :] = jnp.concatenate([normed[i] for i in range(8)], axis=1)
        high, low = split(token_sum[:, pl.ds(pl.multiple_of(128 * eight, 128), 128)])
        near_high[rows, :] = high
        near_low[rows, :] = low
        return carry

    lax.fori_loop(0, QTOK // 8, near_step, 0)
    wide = dot_tn(near_high[...], near_flat[...]) + dot_tn(near_low[...], near_flat[...])
    weight = wide[0:CA, 0:128]
    for i in range(1, 8):
        weight += wide[CA * i : CA * i + CA, 128 * i : 128 * i + 128]
    weight_sent[0] = weight
    row_copies = [
        remote(weight_sent.at[0], weight_row.at[at], send_wr.at[at], recv_wr.at[at], device)
        for at, device in enumerate(along_row)
    ]
    grid_copies = [
        remote(weight_sent.at[1], weight_grid.at[at], send_wg.at[at], recv_wg.at[at], device)
        for at, device in enumerate(along_grid)
    ]
    for copy in row_copies:
        copy.start()
    for at, copy in enumerate(row_copies):
        copy.wait_recv()
        weight += weight_row[at]
    weight_sent[1] = weight
    for copy in grid_copies:
        copy.start()

    spread_wt = spread_projection_t(proj_ref[...])

    def gradient(block, token_rows):
        high, low = split(token_rows)
        hatted, inv_scale = normalise(block)
        wide = dot(high, spread_wt) + dot(low, spread_wt)
        scaled = jnp.stack([wide[:, 128 * i : 128 * i + 128] for i in range(8)]) * gain
        first_mean = jnp.mean(scaled, axis=-1, keepdims=True)
        second_mean = jnp.mean(scaled * hatted, axis=-1, keepdims=True)
        return (inv_scale * (scaled - first_mean - hatted * second_mean)).astype(BF16)

    def grad_out(group):
        return pltpu.make_async_copy(grads.at[group], grads_hbm.at[group], load_sems.at[group])

    corner_out = pltpu.make_async_copy(corner_grads, corner_grads_hbm, corner_load_sem)

    def grad_step(group, carry):
        at = pl.multiple_of(window_column(group, odd) - TOK * odd + 16, 16)
        lanes = pl.ds(pl.multiple_of(128 * group, 128), 128)
        grads[group] = gradient(band[group], tokens[pl.ds(at, KEYS), lanes])
        grad_out(group).start()
        return carry

    @pl.when(is_main)
    def _():
        tokens[...] = jnp.zeros_like(tokens)
        for source in range(N_COL):
            row_at, row_count, lane_at, lane_count = TOKEN_PART[source]
            part = pl.ds(row_at, row_count), pl.ds(lane_at, lane_count)

            @pl.when(col != source)
            def _():
                token_copy(source).wait_recv()

            @pl.when(col == source)
            def _():
                patches[(source, *part)] = token_sum[part]

            at = key_base(source) + 16 + row_at
            lanes = query_base_static(source) * CA + lane_at
            tokens[at : at + row_count, lanes : lanes + lane_count] += patches[(source, *part)]
        lax.fori_loop(0, GROUPS // 2, grad_step, 0)

    @pl.when(is_holder)
    def _():
        @pl.when(other_device)
        def _():
            token_corner_copy.wait_recv()

        for part in range(2):
            corner_grads[8 * part : 8 * part + 8] = gradient(
                corner_band[8 * part : 8 * part + 8],
                token_corner[:, 128 * part : 128 * part + 128],
            )
        corner_out.start()

    @pl.when(is_main)
    def _():
        lax.fori_loop(GROUPS // 2, GROUPS, grad_step, 0)

    for copy in key_halos:
        copy.wait()
    total = query_sum[...] + key_sum[HALO : HALO + ATOMS]
    lead = total[:HALO] + key_before[...]
    trail = total[ATOMS - HALO :] + key_after[...]
    total = jnp.concatenate([lead, total[HALO : ATOMS - HALO], trail], axis=0)
    floats = feats_ref[...].astype(F32)
    sigma = jax.nn.sigmoid(floats)
    atom_grad_ref[...] = (total * (sigma * (1.0 + floats * (1.0 - sigma)))).astype(BF16)

    for at, copy in enumerate(grid_copies):
        copy.wait_recv()
        weight += weight_grid[at]
    proj_grad_ref[...] = weight

    for copy in row_copies + grid_copies:
        copy.wait_send()

    for source in range(N_COL):

        @pl.when(not_main & (col == source))
        def _():
            token_copy(source).wait_send()

    @pl.when(is_reader & other_device)
    def _():
        token_corner_copy.wait_send()

    @pl.when(is_holder & other_device)
    def _():
        raw_corner_copy.wait_send()

    @pl.when(is_main)
    def _():
        def grad_wait(group, carry):
            grad_out(group).wait()
            return carry

        lax.fori_loop(0, GROUPS, grad_wait, 0)

    @pl.when(is_holder)
    def _():
        corner_out.wait()


def band_pass(start, pair_repr, cot, gain, proj, feats, counts, weights):
    vmem = pl.BlockSpec(memory_space=pltpu.VMEM)
    any_spec = pl.BlockSpec(memory_space=pl.ANY)
    dma = pltpu.SemaphoreType.DMA
    return pl.pallas_call(
        band_kernel,
        out_shape=(
            jax.ShapeDtypeStruct((GROUPS, 8, KEYS, CP), BF16),
            jax.ShapeDtypeStruct((16, 16, CP), BF16),
            jax.ShapeDtypeStruct((ATOMS, CP), BF16),
            jax.ShapeDtypeStruct((CA, CP), F32),
        ),
        in_specs=[pl.BlockSpec(memory_space=pltpu.SMEM)] + [any_spec] * 11,
        out_specs=(any_spec, any_spec, vmem, vmem),
        scratch_shapes=[
            pltpu.VMEM((1, CP), F32),
            pltpu.VMEM((CA, CP), BF16),
            pltpu.VMEM((ATOMS, CP), BF16),
            pltpu.VMEM((1, TOK), jnp.int32),
            pltpu.VMEM((CA, CP), BF16),
            pltpu.VMEM((CA, CP), BF16),
            pltpu.VMEM((CA, CA), BF16),
            pltpu.VMEM((CA, CA), BF16),
            pltpu.VMEM((CA, CA), BF16),
            pltpu.VMEM((GROUPS, 8, KEYS, CP), BF16),
            pltpu.VMEM((16, 16, CP), BF16),
            pltpu.VMEM((GROUPS, 8, KEYS, CP), BF16),
            pltpu.VMEM((16, 16, CP), BF16),
            pltpu.VMEM((128, TOK * CA), BF16),
            pltpu.VMEM((16, 256), BF16),
            pltpu.VMEM((KEYS, QTOK * CA), BF16),
            pltpu.VMEM((16, 256), BF16),
            pltpu.VMEM((QTOK, KEYS, CP), BF16),
            pltpu.VMEM((HALO, CP), BF16),
            pltpu.VMEM((HALO, CP), BF16),
            pltpu.VMEM((1, TOK), jnp.int32),
            pltpu.VMEM((1, TOK), jnp.int32),
            pltpu.VMEM((ATOMS, KWIN * CA), BF16),
            pltpu.VMEM((EXT, CP), F32),
            pltpu.VMEM((144, LANES), BF16),
            pltpu.VMEM((ATOMS, LANES), BF16),
            pltpu.VMEM((ATOMS, LANES), BF16),
            pltpu.VMEM((ATOMS * 16, 128), F32),
            pltpu.VMEM((4 * NBLK * KWIN, 128), F32),
            pltpu.VMEM((NBLK * KWIN, LANES), F32),
            pltpu.VMEM((5, 512, 256), BF16),
            pltpu.VMEM((LANES, CP), BF16),
            pltpu.VMEM((LANES, CP), BF16),
            pltpu.VMEM((LANES, 128), F32),
            pltpu.VMEM((LANES, 128), F32),
            pltpu.VMEM((NBLK, 256, LANES), BF16),
            pltpu.VMEM((EXT, CP), F32),
            pltpu.VMEM((ATOMS, CP), F32),
            pltpu.VMEM((KEYS, QTOK * CA), F32),
            pltpu.VMEM((HALO, CP), F32),
            pltpu.VMEM((HALO, CP), F32),
            pltpu.VMEM((N_COL, KEYS, QTOK * CA), F32),
            pltpu.VMEM((16, 256), F32),
            pltpu.VMEM((128, TOK * CA), F32),
            pltpu.VMEM((QTOK // 8 * KEYS, 8 * CP), BF16),
            pltpu.VMEM((QTOK // 8 * KEYS, 128), BF16),
            pltpu.VMEM((QTOK // 8 * KEYS, 128), BF16),
            pltpu.VMEM((2, CA, CP), F32),
            pltpu.VMEM((N_COL - 1, CA, CP), F32),
            pltpu.VMEM((N_ROW - 1, CA, CP), F32),
            dma((9,)),
            dma((GROUPS,)),
            dma,
            dma,
            dma((N_COL,)),
            dma,
            dma,
            dma,
            dma((N_COL,)),
            dma,
            dma,
            dma,
            dma((4,)),
            dma((4,)),
            dma,
            dma((N_COL,)),
            dma,
            dma,
            dma((2,)),
            dma((2,)),
            dma((N_COL - 1,)),
            dma((N_COL - 1,)),
            dma((N_ROW - 1,)),
            dma((N_ROW - 1,)),
        ],
        compiler_params=pltpu.CompilerParams(
            collective_id=0, has_side_effects=True, vmem_limit_bytes=VMEM_LIMIT
        ),
        name="band_pass",
    )(start, pair_repr, cot, gain, proj, feats, counts, *weights)


def place_kernel(
    grads_ref,
    corner_ref,
    atom_ref,
    proj_ref,
    pair_grad_ref,
    atom_grad_ref,
    proj_grad_ref,
    zeros,
    held,
    sems,
):
    row = lax.axis_index("row")
    col = lax.axis_index("col")
    odd = row % 2
    half = row // 2
    is_main = col == half
    holder = jnp.where(odd == 0, half - 1, half + 1)
    is_holder = col == holder
    zeros[...] = jnp.zeros_like(zeros)

    def blank(group, first, last, sem):
        return pltpu.make_async_copy(
            zeros.at[:, pl.ds(0, last - first)],
            pair_grad_ref.at[pl.ds(8 * group, 8), pl.ds(first, last - first)],
            sem,
        )

    def pieces(kind, parity):
        copies, loads, stores = [], [], []
        for group in range(GROUPS):
            first, last, source = 0, 0, None
            if kind == "band":
                first = 16 * ((8 * group - 13 + 16) // 16) - 16 + TOK * parity
                first = min(max(first, 0), COLS - KEYS)
                last, source = first + KEYS, (grads_ref.at[group], held.at[group])
            elif kind == "corner" and group // 2 == 5 * parity:
                first = 176 * (1 - parity)
                last = first + 16
                source = (
                    corner_ref.at[pl.ds(8 * (group % 2), 8)],
                    held.at[group, :, pl.ds(0, 16)],
                )
            if source is not None:
                to = pair_grad_ref.at[pl.ds(8 * group, 8), pl.ds(first, last - first)]
                loads.append(pltpu.make_async_copy(*source, sems.at[group, 0]))
                stores.append(pltpu.make_async_copy(source[1], to, sems.at[group, 3]))
            if first > 0:
                copies.append(blank(group, 0, first, sems.at[group, 1]))
            if last < COLS:
                copies.append(blank(group, last, COLS, sems.at[group, 2]))
        return copies, loads, stores

    cases = (
        (is_main & (odd == 0), "band", 0),
        (is_main & (odd == 1), "band", 1),
        (is_holder & (odd == 0), "corner", 0),
        (is_holder & (odd == 1), "corner", 1),
        (jnp.logical_not(is_main | is_holder), "none", 0),
    )
    for when, kind, parity in cases:

        @pl.when(when)
        def _():
            copies, loads, stores = pieces(kind, parity)
            for copy in loads + copies:
                copy.start()
            for load, store in zip(loads, stores):
                load.wait()
                store.start()
            for copy in copies + stores:
                copy.wait()

    atom_grad_ref[...] = atom_ref[...]
    proj_grad_ref[...] = proj_ref[...]


def place(grads, corner, atom_grad, proj_grad):
    vmem = pl.BlockSpec(memory_space=pltpu.VMEM)
    any_spec = pl.BlockSpec(memory_space=pl.ANY)
    return pl.pallas_call(
        place_kernel,
        out_shape=(
            jax.ShapeDtypeStruct((TOK, COLS, CP), BF16),
            jax.ShapeDtypeStruct((ATOMS, CP), BF16),
            jax.ShapeDtypeStruct((CA, CP), F32),
        ),
        in_specs=[any_spec, any_spec, vmem, vmem],
        out_specs=(any_spec, vmem, vmem),
        scratch_shapes=[
            pltpu.VMEM((8, COLS, CP), BF16),
            pltpu.VMEM((GROUPS, 8, KEYS, CP), BF16),
            pltpu.SemaphoreType.DMA((GROUPS, 4)),
        ],
        compiler_params=pltpu.CompilerParams(vmem_limit_bytes=VMEM_LIMIT),
        name="place",
    )(grads, corner, atom_grad, proj_grad)


def shards(
    pair_repr,
    pair_gain,
    proj_weight,
    query_weight,
    key_weight,
    mlp_first,
    mlp_second,
    mlp_third,
    atom_feats,
    token_counts,
    key_start,
    pair_cotangent,
):
    grads, corner, atom_grad, proj_grad = band_pass(
        key_start,
        pair_repr,
        pair_cotangent,
        pair_gain.reshape(1, CP),
        proj_weight.T,
        atom_feats,
        token_counts,
        (query_weight.T, key_weight.T, mlp_first, mlp_second, mlp_third),
    )
    pair_grad, atom_grad, proj_grad = place(grads, corner, atom_grad, proj_grad)
    return pair_grad, atom_grad, proj_grad.T


def solution(mesh):
    placed = (
        P("row", "col", None),
        P(),
        P(),
        P(),
        P(),
        P(),
        P(),
        P(),
        P(("row", "col"), None),
        P("row", None),
        P(("row", "col")),
        P(("row", "col"), None),
    )
    return jax.shard_map(
        shards,
        mesh=mesh,
        in_specs=placed,
        out_specs=(P("row", "col", None), P(("row", "col"), None), P()),
        check_vma=False,
    )
```

```python
import jax
import jax.numpy as jnp
from jax import lax
from jax.experimental import pallas as pl
from jax.experimental.pallas import tpu as pltpu
from jax.sharding import PartitionSpec as P

F32 = jnp.float32
BF16 = jnp.bfloat16
MESH = pl.DeviceIdType.MESH

N_ROW = 16
N_COL = 8
TOK = 96
COLS = 192
CP = 128
CA = 16
QBLK = 32
KWIN = 128
MOST = 23
ATOMS = 256
ROW_ATOMS = 2048
SLACK = TOK * MOST - ROW_ATOMS
HALO = KWIN - QBLK
EXT = ATOMS + 2 * HALO
NBLK = ATOMS // QBLK
LANES = QBLK * CA
KEYS = 48
QTOK = 32
GROUPS = TOK // 8
VMEM_LIMIT = 56 * 1024 * 1024
MLP_ROWS = 1024
NEAR = 19
TOKEN_PART = (
    (0, 40, 0, 384),
    (0, 40, 0, 384),
    (0, 32, 0, 512),
    (8, 32, 0, 384),
    (8, 32, 0, 384),
    (0, 32, 0, 512),
    (8, 40, 0, 384),
    (8, 40, 128, 384),
)


def key_base(col):
    return 16 * ((11 * col - 5 + 16) // 16) - 16


def query_base(col):
    return jnp.minimum(8 * ((11 * col) // 8), TOK - QTOK)


def query_base_static(col):
    return min(8 * ((11 * col) // 8), TOK - QTOK)


def iota(shape, dim):
    return lax.broadcasted_iota(jnp.int32, shape, dim)


def dot(a, b):
    return jnp.dot(a, b, preferred_element_type=F32)


def dot_nt(a, b):
    return lax.dot_general(a, b, (((1,), (1,)), ((), ())), preferred_element_type=F32)


def dot_tn(a, b):
    return lax.dot_general(a, b, (((0,), (0,)), ((), ())), preferred_element_type=F32)


def split(x):
    high = x.astype(BF16)
    low = (x - high.astype(F32)).astype(BF16)
    return high, low


def dot_split(x, w):
    high, low = split(x)
    return dot(high, w) + dot(low, w)


def dot_twice(x, w):
    return dot(jnp.concatenate(split(x), axis=1), w)


def sigmoid(x):
    return 0.5 * jnp.tanh(0.5 * x) + 0.5


def mesh_place():
    row = lax.axis_index("row")
    col = lax.axis_index("col")
    return row, col


def normalise(block):
    floats = block.astype(F32)
    centre = floats - jnp.mean(floats, axis=-1, keepdims=True)
    spread = jnp.mean(centre * centre, axis=-1, keepdims=True)
    inv_scale = lax.rsqrt(spread + 1e-05)
    return centre * inv_scale, inv_scale


def channel_eye(rows):
    return ((iota((rows, CA), 0) & (CA - 1)) == iota((rows, CA), 1)).astype(F32).astype(BF16)


def channel_eye_t(lanes):
    return ((iota((CA, lanes), 1) & (CA - 1)) == iota((CA, lanes), 0)).astype(F32).astype(BF16)


def spread_projection(proj):
    eye_t = channel_eye_t(CP)
    wide = dot_tn(proj, eye_t)
    lane = iota((CP, CP), 1) // CA
    return jnp.concatenate(
        [jnp.where(lane == i, wide, 0.0).astype(BF16) for i in range(8)], axis=0
    )


def spread_projection_t(proj):
    eye = channel_eye(CP)
    tall = dot(eye, proj)
    row = iota((CP, CP), 0) // CA
    return jnp.concatenate(
        [jnp.where(row == i, tall, 0.0).astype(BF16) for i in range(8)], axis=1
    )


def window_column(group, odd):
    first = 16 * ((8 * group - 13 + 16) // 16) - 16
    return jnp.clip(first + TOK * odd, 0, COLS - KEYS)


def corner_place(odd):
    return 80 * odd, 176 * (1 - odd)


def swap_groups(pieces, group):
    for bit in (1, 2, 4):
        take = (group & bit) != 0
        swapped = list(pieces)
        for at in range(8):
            if at & bit == 0:
                one, two = pieces[at], pieces[at | bit]
                swapped[at] = jnp.where(take, pltpu.roll(two, CA * bit, 1), one)
                swapped[at | bit] = jnp.where(take, two, pltpu.roll(one, 128 - CA * bit, 1))
        pieces = swapped
    return pieces


def neighbours(row, col):
    ahead = (
        jnp.where(col == N_COL - 1, lax.rem(row + 1, N_ROW), row),
        lax.rem(col + 1, N_COL),
    )
    behind = (
        jnp.where(col == 0, lax.rem(row + N_ROW - 1, N_ROW), row),
        lax.rem(col + N_COL - 1, N_COL),
    )
    return ahead, behind


def like_places(row, col):
    return [(lax.rem(row + step, N_ROW), col) for step in range(1, N_ROW)]


def band_kernel(
    start_ref,
    pair_ref,
    cot_hbm,
    gain_hbm,
    proj_hbm,
    feats_hbm,
    counts_hbm,
    query_w_hbm,
    key_w_hbm,
    first_w_hbm,
    second_w_hbm,
    third_w_hbm,
    grads_hbm,
    corner_grads_hbm,
    atom_grad_ref,
    proj_grad_ref,
    gain_ref,
    proj_ref,
    feats_ref,
    counts_ref,
    query_w_ref,
    key_w_ref,
    first_w_ref,
    second_w_ref,
    third_w_ref,
    grads,
    corner_grads,
    band,
    corner_band,
    zrow,
    zcorner,
    patch,
    patch_corner,
    raw,
    feats_before,
    feats_after,
    counts_before,
    counts_after,
    cot_ref,
    act_ext,
    rhs,
    query_high,
    query_low,
    spread,
    cot,
    state,
    mixers,
    key_tiled,
    query_tiled,
    slot_from,
    slot_to,
    hot_ref,
    key_sum,
    query_sum,
    token_sum,
    key_before,
    key_after,
    patches,
    token_corner,
    tokens,
    near_flat,
    near_high,
    near_low,
    weight_sent,
    weight_row,
    weight_grid,
    small_sems,
    load_sems,
    cot_sem,
    corner_load_sem,
    send_z,
    recv_z,
    send_c,
    recv_c,
    send_r,
    recv_r,
    send_rc,
    recv_rc,
    send_h,
    recv_h,
    send_t,
    recv_t,
    send_tc,
    recv_tc,
    send_k,
    recv_k,
    send_wr,
    recv_wr,
    send_wg,
    recv_wg,
):
    row = lax.axis_index("row")
    col = lax.axis_index("col")
    odd = row % 2
    half = row // 2
    is_main = col == half
    not_main = col != half
    holder = jnp.where(odd == 0, half - 1, half + 1)
    reader = (N_COL - 1) * odd
    exists = (holder >= 0) & (holder < N_COL)
    is_holder = exists & (col == holder)
    is_reader = exists & (col == reader)
    same_device = holder == reader
    other_device = holder != reader
    holder_col = jnp.clip(holder, 0, N_COL - 1)
    ahead, behind = neighbours(row, col)
    along_grid = like_places(row, col)
    along_row = [(row, lax.rem(col + step, N_COL)) for step in range(1, N_COL)]

    def remote(src, dst, send, recv, device):
        return pltpu.make_async_remote_copy(
            src_ref=src,
            dst_ref=dst,
            send_sem=send,
            recv_sem=recv,
            device_id=device,
            device_id_type=MESH,
        )

    raw[...] = jnp.zeros_like(raw)

    barrier = pltpu.get_barrier_semaphore()

    def greet(device):
        pl.semaphore_signal(barrier, inc=1, device_id=device, device_id_type=MESH)

    @pl.when(col == 0)
    def _():
        greet(behind)

    @pl.when(col == N_COL - 1)
    def _():
        greet(ahead)

    for device in along_row + along_grid:
        greet(device)
    greeted = N_COL + N_ROW - 2 + jnp.where((col == 0) | (col == N_COL - 1), 1, 0)

    def window_copy(group):
        first = pl.multiple_of(window_column(group, odd), 16)
        return pltpu.make_async_copy(
            pair_ref.at[pl.ds(8 * group, 8), pl.ds(first, KEYS)],
            band.at[group],
            load_sems.at[group],
        )

    first_row, first_col = corner_place(odd)
    corner_load = pltpu.make_async_copy(
        pair_ref.at[pl.ds(first_row, 16), pl.ds(pl.multiple_of(first_col, 16), 16)],
        corner_band,
        corner_load_sem,
    )
    cot_load = pltpu.make_async_copy(cot_hbm, cot_ref, cot_sem)

    @pl.when(is_main)
    def _():
        for group in range(GROUPS):
            window_copy(group).start()

    @pl.when(is_holder)
    def _():
        corner_load.start()

    cot_load.start()
    smalls = [
        pltpu.make_async_copy(src, dst, small_sems.at[at])
        for at, (src, dst) in enumerate(
            (
                (gain_hbm, gain_ref),
                (proj_hbm, proj_ref),
                (feats_hbm, feats_ref),
                (counts_hbm, counts_ref),
                (query_w_hbm, query_w_ref),
                (key_w_hbm, key_w_ref),
                (first_w_hbm, first_w_ref),
                (second_w_hbm, second_w_ref),
                (third_w_hbm, third_w_ref),
            )
        )
    ]
    for copy in smalls:
        copy.start()
    for copy in smalls:
        copy.wait()

    @pl.when(is_main)
    def _():
        zrow[...] = jnp.zeros_like(zrow)
        spread_w = spread_projection(proj_ref[...])
        gain = gain_ref[...]

        def project(group, carry):
            window_copy(group).wait()
            hatted, _ = normalise(band[group])
            normed = (hatted * gain).astype(BF16)
            rows = jnp.concatenate([normed[i] for i in range(8)], axis=1)
            at = pl.multiple_of(window_column(group, odd) - TOK * odd + 16, 16)
            lanes = pl.ds(pl.multiple_of(128 * group, 128), 128)
            zrow[pl.ds(at, KEYS), lanes] = dot(rows, spread_w).astype(BF16)
            return carry

        lax.fori_loop(0, GROUPS, project, 0)

    @pl.when(is_holder)
    def _():
        spread_w = spread_projection(proj_ref[...])
        corner_load.wait()
        hatted, _ = normalise(corner_band[...])
        normed = (hatted * gain_ref[...]).astype(BF16)
        for part in range(2):
            rows = jnp.concatenate([normed[8 * part + i] for i in range(8)], axis=1)
            zcorner[:, 128 * part : 128 * part + 128] = dot(rows, spread_w).astype(BF16)

    cot_load.wait()

    group = iota((16, 128), 1) // CA

    def spread_step(eight, carry):
        rows = cot_ref[pl.ds(pl.multiple_of(16 * eight, 16), 16), :].astype(F32)
        for half in range(2):
            at = pl.multiple_of(256 * eight + 128 * half, 128)
            for chunk in range(16):
                spread[pl.ds(at + 8 * chunk, 8), :] = rows[
                    8 * half : 8 * half + 8, 128 * chunk : 128 * chunk + 128
                ]
        return carry

    lax.fori_loop(0, ATOMS // 16, spread_step, 0, unroll=2)

    pl.semaphore_wait(barrier, greeted)

    def z_part(target, first):
        return zrow.at[pl.ds(key_base(target) + 16, KEYS), pl.ds(first, QTOK * CA)]

    def z_copy(target):
        src = z_part(target, query_base_static(target) * CA)
        return remote(src, patch, send_z.at[target], recv_z, (row, target))

    corner_copy = remote(zcorner, patch_corner, send_c, recv_c, (row, reader))

    def raw_parts(target):
        rows = pl.ds(11 * target, NEAR)
        to_rows = pl.ds(11 * target - query_base_static(target), NEAR)
        first = key_base(target)

        def part(skip, width, parity):
            src = pair_ref.at[rows, pl.ds(first + skip + TOK * parity, width)]
            return src, raw.at[to_rows, pl.ds(skip, width)]

        return [
            (odd == parity, *part(16 if cut_low else 0, KEYS - 16 if cut_low or cut_high else KEYS, parity))
            for parity in range(2)
            for cut_low in (first + TOK * parity < 0,)
            for cut_high in (first + TOK * parity + KEYS > COLS,)
        ]

    def for_raw(target, act):
        for when, src, dst in raw_parts(target):

            @pl.when(when & (col != target))
            def _():
                act(remote(src, dst, send_r.at[target], recv_r, (row, target)), True)

            @pl.when(when & (col == target))
            def _():
                act(pltpu.make_async_copy(src, dst, recv_r), False)

    raw_corner_src = pair_ref.at[
        pl.ds(first_row, 16), pl.ds(pl.multiple_of(first_col, 16), 16)
    ]
    raw_corner_dst = raw.at[pl.ds(16 * odd, 16), pl.ds(pl.multiple_of(32 * odd, 16), 16)]
    raw_corner_copy = remote(raw_corner_src, raw_corner_dst, send_rc, recv_rc, (row, reader))
    raw_corner_local = pltpu.make_async_copy(raw_corner_src, raw_corner_dst, recv_rc)

    @pl.when(is_main)
    def _():
        for target in range(N_COL):

            @pl.when(col != target)
            def _():
                z_copy(target).start()

        patch[...] = zrow[
            pl.ds(pl.multiple_of(key_base(col) + 16, 16), KEYS),
            pl.ds(pl.multiple_of(query_base(col) * CA, 128), QTOK * CA),
        ]

    @pl.when(is_holder & other_device)
    def _():
        corner_copy.start()
        raw_corner_copy.start()

    @pl.when(is_holder & same_device)
    def _():
        patch_corner[...] = zcorner[...]
        raw_corner_local.start()

    halos = [
        remote(src, dst, send_h.at[at], recv_h.at[at], device)
        for at, (src, dst, device) in enumerate(
            (
                (feats_hbm.at[pl.ds(ATOMS - HALO, HALO)], feats_before, ahead),
                (feats_hbm.at[pl.ds(0, HALO)], feats_after, behind),
                (counts_hbm, counts_before, ahead),
                (counts_hbm, counts_after, behind),
            )
        )
    ]
    halos[0].start()
    halos[1].start()

    @pl.when(col == N_COL - 1)
    def _():
        halos[2].start()

    @pl.when(col == 0)
    def _():
        halos[3].start()

    @pl.when(is_main)
    def _():
        for target in range(N_COL):
            for_raw(target, lambda copy, far: copy.start())

    eye = channel_eye(LANES)
    eye16 = eye[:256]
    same = (iota((256, 256), 0) // CA) == (iota((256, 256), 1) // CA)

    def mixer(weight, flip):
        left = dot_nt(eye16, weight) if flip else dot(eye16, weight)
        wide = dot_nt(left.astype(BF16), eye16)
        wide = jnp.where(same, wide, 0.0).astype(BF16)
        return jnp.concatenate([wide, wide], axis=0)

    mixers[0] = mixer(first_w_ref[...], False)
    mixers[1] = mixer(second_w_ref[...], False)
    mixers[2] = mixer(third_w_ref[...], True)
    mixers[3] = mixer(second_w_ref[...], True)
    mixers[4] = mixer(first_w_ref[...], True)
    key_tiled[...] = dot(eye, key_w_ref[...]).astype(BF16)
    query_tiled[...] = dot(eye, query_w_ref[...]).astype(BF16)
    eye_t = channel_eye_t(LANES)
    rhs[0:16, :] = jnp.zeros((16, LANES), BF16)
    rhs[16:144, :] = dot_tn(key_w_ref[...], eye_t).astype(BF16)

    def activate(feats):
        floats = feats.astype(F32)
        return floats * jax.nn.sigmoid(floats)

    own_act = activate(feats_ref[...]).astype(BF16)
    act_ext[HALO : HALO + ATOMS] = activate(feats_ref[...])

    lane_is_row = iota((QBLK, LANES), 1) // CA == iota((QBLK, LANES), 0)
    query_wide = dot_tn(query_w_ref[...], eye_t).astype(BF16)
    for block in range(NBLK):
        terms = dot(own_act[QBLK * block : QBLK * block + QBLK], query_wide)
        high, low = split(jnp.where(lane_is_row, terms, 0.0))
        query_high[QBLK * block : QBLK * block + QBLK] = high
        query_low[QBLK * block : QBLK * block + QBLK] = low

    own = counts_ref[...].astype(F32)

    def rows_of(counts, rows):
        return jnp.broadcast_to(counts, (rows, TOK)).astype(BF16)

    def as_mask(flag):
        return jnp.where(flag, 1.0, 0.0).astype(BF16)

    first_query = query_base(col)
    slot = iota((LANES, TOK), 0) // CA + first_query
    slot_index = iota((LANES, TOK), 1)
    own_rows = rows_of(own, 128)
    slot_from[...] = dot_nt(as_mask(slot_index < slot), own_rows)
    slot_to[...] = dot_nt(as_mask(slot_index < slot + 1), own_rows)

    lane_atom_row = (iota((1, LANES), 1) // CA).astype(F32)
    channel_match = (iota((256, 128), 0) % CA) == (iota((256, 128), 1) % CA)

    def block_place(block):
        first = col * ATOMS + block * QBLK
        token = 8 * (first // (8 * MOST)) - first_query
        return first, pl.multiple_of(token * CA, 128)

    def query_hot(block):
        first, at = block_place(block)
        low = slot_from[pl.ds(at, 256), :]
        high = slot_to[pl.ds(at, 256), :]
        parts = []
        for part in range(4):
            atom = lane_atom_row[:, 128 * part : 128 * part + 128] + first.astype(F32)
            hot = (low <= atom) & (atom < high) & channel_match
            parts.append(jnp.where(hot, 1.0, 0.0).astype(BF16))
        return jnp.concatenate(parts, axis=1)

    def key_first(block):
        return col * ATOMS + block * QBLK + start_ref[block]

    def hot_step(block, carry):
        hot_ref[block] = query_hot(block)
        return carry

    lax.fori_loop(0, NBLK, hot_step, 0, unroll=2)

    def swap_step(eight, carry):
        at = 128 * eight
        pieces = [spread[pl.ds(at + atom, 16, stride=8), :] for atom in range(8)]
        pieces = swap_groups(pieces, group)
        to = NBLK * KWIN * (eight % 4) + KWIN * (eight // 4)
        for key in range(8):
            cot[pl.ds(to + key, 16, stride=8), :] = pieces[key]
        return carry

    lax.fori_loop(0, ATOMS // 8, swap_step, 0, unroll=4)

    halos[0].wait()
    halos[1].wait()

    @pl.when(col == N_COL - 1)
    def _():
        halos[2].wait_send()
        halos[3].wait_recv()

    @pl.when(col == 0)
    def _():
        halos[3].wait_send()
        halos[2].wait_recv()

    act_ext[0:HALO] = activate(feats_before[...])
    act_ext[HALO + ATOMS : EXT] = activate(feats_after[...])

    base = key_base(col)
    before = jnp.where(col == 0, counts_before[...], counts_ref[...]).astype(F32)
    after = jnp.where(col == N_COL - 1, counts_after[...], counts_ref[...]).astype(F32)

    def lane_bounds(offset):
        token = iota((TOK, 128), 1) + (base + offset)
        index = iota((TOK, 128), 0)
        total = dot(rows_of(own, 8), as_mask(index < token))
        total += dot(rows_of(after, 8), as_mask(index + TOK < token))
        return total - dot(rows_of(before, 8), as_mask(index - TOK >= token))

    def column_bounds(offset):
        token = iota((KEYS, TOK), 0) + (base + offset)
        index = iota((KEYS, TOK), 1)
        total = dot_nt(as_mask(index < token), rows_of(own, 128))
        total += dot_nt(as_mask(index + TOK < token), rows_of(after, 128))
        return total - dot_nt(as_mask(index - TOK >= token), rows_of(before, 128))

    lane = iota((8, 128), 1)
    far = 1.0e6
    lane_from = jnp.where(lane < 48, lane_bounds(0), jnp.where(lane < 112, -far, far))[0:1]
    lane_to = jnp.where(lane < 48, lane_bounds(1), jnp.where(lane < 112, far, -far))[0:1]
    column_from = column_bounds(0)
    column_to = column_bounds(1)

    @pl.when(is_main)
    def _():
        for target in range(N_COL):

            @pl.when(col != target)
            def _():
                z_copy(target).wait_send()

    @pl.when(not_main)
    def _():
        z_copy(0).wait_recv()

    @pl.when(is_holder & other_device)
    def _():
        corner_copy.wait_send()

    @pl.when(is_reader & other_device)
    def _():
        corner_copy.wait_recv()

    @pl.when(is_reader)
    def _():
        at = pl.multiple_of(32 * odd, 16), pl.multiple_of(256 * odd, 128)
        patch[pl.ds(at[0], 16), pl.ds(at[1], 256)] = patch_corner[...]

    def start_step(block, carry):
        _, at = block_place(block)
        hot = hot_ref[block]
        window = start_ref[block] + block * QBLK + HALO
        atom = (iota((KWIN, 128), 0) + key_first(block)).astype(F32)
        mine = pl.ds(pl.multiple_of(block * QBLK, QBLK), QBLK)
        left = jnp.concatenate(
            [
                as_mask((lane_from <= atom) & (atom < lane_to)),
                act_ext[pl.ds(window, KWIN), :].astype(BF16),
            ],
            axis=1,
        )
        right = jnp.concatenate(
            [
                dot(patch[:, pl.ds(at, 256)], hot).astype(BF16),
                query_high[mine, :],
                query_low[mine, :],
                rhs[...],
            ],
            axis=0,
        )
        state[pl.ds(pl.multiple_of(block * KWIN, KWIN), KWIN), :] = dot(left, right)
        return carry

    lax.fori_loop(0, NBLK, start_step, 0, unroll=2)

    atom_low = jnp.where(row == 0, 0, -ROW_ATOMS)
    atom_high = jnp.where(row == N_ROW - 1, ROW_ATOMS, 2 * ROW_ATOMS)

    def slope(value, sigma, act):
        return sigma + act - act * sigma

    def mlp_step(step, carry):
        at = pl.multiple_of(MLP_ROWS * (step // 2), MLP_ROWS)
        place = pl.ds(at, MLP_ROWS), pl.ds(pl.multiple_of(256 * (step % 2), 256), 256)
        value = state[place]
        index = iota((KWIN, 256), 0)
        atom = jnp.concatenate(
            [
                index + key_first(MLP_ROWS // KWIN * (step // 2) + block)
                for block in range(MLP_ROWS // KWIN)
            ],
            axis=0,
        )
        parts = [
            cot[pl.ds(pl.multiple_of(at + NBLK * KWIN * (2 * (step % 2) + part), MLP_ROWS), MLP_ROWS), :]
            for part in range(2)
        ]
        grad = jnp.concatenate(parts, axis=1)
        grad = jnp.where((atom >= atom_low) & (atom < atom_high), grad, 0.0)
        sig_0 = sigmoid(value)
        act_0 = value * sig_0
        one = dot_twice(act_0, mixers[0])
        sig_1 = sigmoid(one)
        act_1 = one * sig_1
        two = dot_twice(act_1, mixers[1])
        sig_2 = sigmoid(two)
        back = dot(grad.astype(BF16), mixers[2, 0:256]) * slope(two, sig_2, two * sig_2)
        back = dot(back.astype(BF16), mixers[3, 0:256]) * slope(one, sig_1, act_1)
        back = dot(back.astype(BF16), mixers[4, 0:256]) * slope(value, sig_0, act_0)
        state[place] = grad + back
        return carry

    lax.fori_loop(0, 2 * NBLK * KWIN // MLP_ROWS, mlp_step, 0)

    key_sum[...] = jnp.zeros_like(key_sum)
    token_sum[...] = jnp.zeros_like(token_sum)

    def sum_step(block, carry):
        _, at = block_place(block)
        window = start_ref[block] + block * QBLK + HALO
        back = state[pl.ds(pl.multiple_of(block * KWIN, KWIN), KWIN), :]
        high, low = split(back)
        by_key = dot(high, key_tiled[...]) + dot(low, key_tiled[...])
        reach = KWIN + HALO
        moved = as_mask(
            iota((reach, KWIN), 0) == iota((reach, KWIN), 1) + (start_ref[block] + HALO)
        )
        by_key_high, by_key_low = split(by_key)
        key_sum[pl.ds(pl.multiple_of(block * QBLK, QBLK), reach), :] += dot(
            moved, by_key_high
        ) + dot(moved, by_key_low)
        over_keys = jnp.sum(back, axis=0, keepdims=True)
        over_keys = jnp.where(lane_is_row, over_keys, 0.0)
        mine = pl.multiple_of(block * QBLK, QBLK)
        query_sum[pl.ds(mine, QBLK), :] = dot_split(over_keys, query_tiled[...])
        atom = (iota((KEYS, 128), 1) + key_first(block)).astype(F32)
        key_hot = as_mask((column_from <= atom) & (atom < column_to))
        by_token = dot(key_hot, high) + dot(key_hot, low)
        high, low = split(by_token)
        hot = hot_ref[block]
        token_sum[:, pl.ds(at, 256)] += dot_nt(high, hot) + dot_nt(low, hot)
        return carry

    lax.fori_loop(0, NBLK, sum_step, 0, unroll=2)

    def token_copy(source):
        row_at, row_count, lane_at, lane_count = TOKEN_PART[source]
        part = pl.ds(row_at, row_count), pl.ds(lane_at, lane_count)
        return remote(
            token_sum.at[part], patches.at[(source, *part)], send_t, recv_t.at[source], (row, half)
        )

    corner_part = token_sum.at[
        pl.ds(pl.multiple_of(32 * odd, 16), 16), pl.ds(pl.multiple_of(256 * odd, 128), 256)
    ]
    token_corner_copy = remote(corner_part, token_corner, send_tc, recv_tc, (row, holder_col))

    for source in range(N_COL):

        @pl.when(not_main & (col == source))
        def _():
            token_copy(source).start()

    @pl.when(is_reader & other_device)
    def _():
        token_corner_copy.start()

    @pl.when(is_reader & same_device)
    def _():
        token_corner[...] = corner_part[...]

    key_halos = [
        remote(src, dst, send_k.at[at], recv_k.at[at], device)
        for at, (src, dst, device) in enumerate(
            (
                (key_sum.at[pl.ds(HALO + ATOMS, HALO)], key_before, ahead),
                (key_sum.at[pl.ds(0, HALO)], key_after, behind),
            )
        )
    ]
    for copy in key_halos:
        copy.start()

    @pl.when(is_main)
    def _():
        for target in range(N_COL):
            for_raw(target, lambda copy, far: copy.wait_send() if far else copy.wait())

    for target in range(N_COL):

        for when, src, dst in raw_parts(target):

            @pl.when(when & not_main & (col == target))
            def _():
                remote(src, dst, send_r.at[target], recv_r, (row, target)).wait_recv()

    @pl.when(is_reader & other_device)
    def _():
        raw_corner_copy.wait_recv()

    @pl.when(is_reader & same_device)
    def _():
        raw_corner_local.wait()

    gain = gain_ref[...]

    def near_step(eight, carry):
        hatted, _ = normalise(raw[pl.ds(8 * eight, 8)])
        normed = (hatted * gain).astype(BF16)
        rows = pl.ds(pl.multiple_of(KEYS * eight, 16), KEYS)
        near_flat[rows, :] = jnp.concatenate([normed[i] for i in range(8)], axis=1)
        high, low = split(token_sum[:, pl.ds(pl.multiple_of(128 * eight, 128), 128)])
        near_high[rows, :] = high
        near_low[rows, :] = low
        return carry

    lax.fori_loop(0, QTOK // 8, near_step, 0)
    wide = dot_tn(near_high[...], near_flat[...]) + dot_tn(near_low[...], near_flat[...])
    weight = wide[0:CA, 0:128]
    for i in range(1, 8):
        weight += wide[CA * i : CA * i + CA, 128 * i : 128 * i + 128]
    weight_sent[0] = weight
    row_copies = [
        remote(weight_sent.at[0], weight_row.at[at], send_wr.at[at], recv_wr.at[at], device)
        for at, device in enumerate(along_row)
    ]
    grid_copies = [
        remote(weight_sent.at[1], weight_grid.at[at], send_wg.at[at], recv_wg.at[at], device)
        for at, device in enumerate(along_grid)
    ]
    for copy in row_copies:
        copy.start()
    for at, copy in enumerate(row_copies):
        copy.wait_recv()
        weight += weight_row[at]
    weight_sent[1] = weight
    for copy in grid_copies:
        copy.start()

    spread_wt = spread_projection_t(proj_ref[...])

    def gradient(block, token_rows):
        high, low = split(token_rows)
        hatted, inv_scale = normalise(block)
        wide = dot(high, spread_wt) + dot(low, spread_wt)
        scaled = jnp.stack([wide[:, 128 * i : 128 * i + 128] for i in range(8)]) * gain
        first_mean = jnp.mean(scaled, axis=-1, keepdims=True)
        second_mean = jnp.mean(scaled * hatted, axis=-1, keepdims=True)
        return (inv_scale * (scaled - first_mean - hatted * second_mean)).astype(BF16)

    def grad_out(group):
        return pltpu.make_async_copy(grads.at[group], grads_hbm.at[group], load_sems.at[group])

    corner_out = pltpu.make_async_copy(corner_grads, corner_grads_hbm, corner_load_sem)

    def grad_step(group, carry):
        at = pl.multiple_of(window_column(group, odd) - TOK * odd + 16, 16)
        lanes = pl.ds(pl.multiple_of(128 * group, 128), 128)
        grads[group] = gradient(band[group], tokens[pl.ds(at, KEYS), lanes])
        grad_out(group).start()
        return carry

    @pl.when(is_main)
    def _():
        tokens[...] = jnp.zeros_like(tokens)
        for source in range(N_COL):
            row_at, row_count, lane_at, lane_count = TOKEN_PART[source]
            part = pl.ds(row_at, row_count), pl.ds(lane_at, lane_count)

            @pl.when(col != source)
            def _():
                token_copy(source).wait_recv()

            @pl.when(col == source)
            def _():
                patches[(source, *part)] = token_sum[part]

            at = key_base(source) + 16 + row_at
            lanes = query_base_static(source) * CA + lane_at
            tokens[at : at + row_count, lanes : lanes + lane_count] += patches[(source, *part)]
        lax.fori_loop(0, GROUPS // 2, grad_step, 0)

    @pl.when(is_holder)
    def _():
        @pl.when(other_device)
        def _():
            token_corner_copy.wait_recv()

        for part in range(2):
            corner_grads[8 * part : 8 * part + 8] = gradient(
                corner_band[8 * part : 8 * part + 8],
                token_corner[:, 128 * part : 128 * part + 128],
            )
        corner_out.start()

    @pl.when(is_main)
    def _():
        lax.fori_loop(GROUPS // 2, GROUPS, grad_step, 0)

    for copy in key_halos:
        copy.wait()
    total = query_sum[...] + key_sum[HALO : HALO + ATOMS]
    lead = total[:HALO] + key_before[...]
    trail = total[ATOMS - HALO :] + key_after[...]
    total = jnp.concatenate([lead, total[HALO : ATOMS - HALO], trail], axis=0)
    floats = feats_ref[...].astype(F32)
    sigma = jax.nn.sigmoid(floats)
    atom_grad_ref[...] = (total * (sigma * (1.0 + floats * (1.0 - sigma)))).astype(BF16)

    for at, copy in enumerate(grid_copies):
        copy.wait_recv()
        weight += weight_grid[at]
    proj_grad_ref[...] = weight

    for copy in row_copies + grid_copies:
        copy.wait_send()

    for source in range(N_COL):

        @pl.when(not_main & (col == source))
        def _():
            token_copy(source).wait_send()

    @pl.when(is_reader & other_device)
    def _():
        token_corner_copy.wait_send()

    @pl.when(is_holder & other_device)
    def _():
        raw_corner_copy.wait_send()

    @pl.when(is_main)
    def _():
        def grad_wait(group, carry):
            grad_out(group).wait()
            return carry

        lax.fori_loop(0, GROUPS, grad_wait, 0)

    @pl.when(is_holder)
    def _():
        corner_out.wait()


def band_pass(start, pair_repr, cot, gain, proj, feats, counts, weights):
    vmem = pl.BlockSpec(memory_space=pltpu.VMEM)
    any_spec = pl.BlockSpec(memory_space=pl.ANY)
    dma = pltpu.SemaphoreType.DMA
    return pl.pallas_call(
        band_kernel,
        out_shape=(
            jax.ShapeDtypeStruct((GROUPS, 8, KEYS, CP), BF16),
            jax.ShapeDtypeStruct((16, 16, CP), BF16),
            jax.ShapeDtypeStruct((ATOMS, CP), BF16),
            jax.ShapeDtypeStruct((CA, CP), F32),
        ),
        in_specs=[pl.BlockSpec(memory_space=pltpu.SMEM)] + [any_spec] * 11,
        out_specs=(any_spec, any_spec, vmem, vmem),
        scratch_shapes=[
            pltpu.VMEM((1, CP), F32),
            pltpu.VMEM((CA, CP), BF16),
            pltpu.VMEM((ATOMS, CP), BF16),
            pltpu.VMEM((1, TOK), jnp.int32),
            pltpu.VMEM((CA, CP), BF16),
            pltpu.VMEM((CA, CP), BF16),
            pltpu.VMEM((CA, CA), BF16),
            pltpu.VMEM((CA, CA), BF16),
            pltpu.VMEM((CA, CA), BF16),
            pltpu.VMEM((GROUPS, 8, KEYS, CP), BF16),
            pltpu.VMEM((16, 16, CP), BF16),
            pltpu.VMEM((GROUPS, 8, KEYS, CP), BF16),
            pltpu.VMEM((16, 16, CP), BF16),
            pltpu.VMEM((128, TOK * CA), BF16),
            pltpu.VMEM((16, 256), BF16),
            pltpu.VMEM((KEYS, QTOK * CA), BF16),
            pltpu.VMEM((16, 256), BF16),
            pltpu.VMEM((QTOK, KEYS, CP), BF16),
            pltpu.VMEM((HALO, CP), BF16),
            pltpu.VMEM((HALO, CP), BF16),
            pltpu.VMEM((1, TOK), jnp.int32),
            pltpu.VMEM((1, TOK), jnp.int32),
            pltpu.VMEM((ATOMS, KWIN * CA), BF16),
            pltpu.VMEM((EXT, CP), F32),
            pltpu.VMEM((144, LANES), BF16),
            pltpu.VMEM((ATOMS, LANES), BF16),
            pltpu.VMEM((ATOMS, LANES), BF16),
            pltpu.VMEM((ATOMS * 16, 128), F32),
            pltpu.VMEM((4 * NBLK * KWIN, 128), F32),
            pltpu.VMEM((NBLK * KWIN, LANES), F32),
            pltpu.VMEM((5, 512, 256), BF16),
            pltpu.VMEM((LANES, CP), BF16),
            pltpu.VMEM((LANES, CP), BF16),
            pltpu.VMEM((LANES, 128), F32),
            pltpu.VMEM((LANES, 128), F32),
            pltpu.VMEM((NBLK, 256, LANES), BF16),
            pltpu.VMEM((EXT, CP), F32),
            pltpu.VMEM((ATOMS, CP), F32),
            pltpu.VMEM((KEYS, QTOK * CA), F32),
            pltpu.VMEM((HALO, CP), F32),
            pltpu.VMEM((HALO, CP), F32),
            pltpu.VMEM((N_COL, KEYS, QTOK * CA), F32),
            pltpu.VMEM((16, 256), F32),
            pltpu.VMEM((128, TOK * CA), F32),
            pltpu.VMEM((QTOK // 8 * KEYS, 8 * CP), BF16),
            pltpu.VMEM((QTOK // 8 * KEYS, 128), BF16),
            pltpu.VMEM((QTOK // 8 * KEYS, 128), BF16),
            pltpu.VMEM((2, CA, CP), F32),
            pltpu.VMEM((N_COL - 1, CA, CP), F32),
            pltpu.VMEM((N_ROW - 1, CA, CP), F32),
            dma((9,)),
            dma((GROUPS,)),
            dma,
            dma,
            dma((N_COL,)),
            dma,
            dma,
            dma,
            dma((N_COL,)),
            dma,
            dma,
            dma,
            dma((4,)),
            dma((4,)),
            dma,
            dma((N_COL,)),
            dma,
            dma,
            dma((2,)),
            dma((2,)),
            dma((N_COL - 1,)),
            dma((N_COL - 1,)),
            dma((N_ROW - 1,)),
            dma((N_ROW - 1,)),
        ],
        compiler_params=pltpu.CompilerParams(
            collective_id=0, has_side_effects=True, vmem_limit_bytes=VMEM_LIMIT
        ),
        name="band_pass",
    )(start, pair_repr, cot, gain, proj, feats, counts, *weights)


def place_kernel(
    grads_ref,
    corner_ref,
    atom_ref,
    proj_ref,
    pair_grad_ref,
    atom_grad_ref,
    proj_grad_ref,
    zeros,
    held,
    sems,
):
    row = lax.axis_index("row")
    col = lax.axis_index("col")
    odd = row % 2
    half = row // 2
    is_main = col == half
    holder = jnp.where(odd == 0, half - 1, half + 1)
    is_holder = col == holder
    zeros[...] = jnp.zeros_like(zeros)

    def blank(group, first, last, sem):
        return pltpu.make_async_copy(
            zeros.at[:, pl.ds(0, last - first)],
            pair_grad_ref.at[pl.ds(8 * group, 8), pl.ds(first, last - first)],
            sem,
        )

    def pieces(kind, parity):
        copies, loads, stores = [], [], []
        for group in range(GROUPS):
            first, last, source = 0, 0, None
            if kind == "band":
                first = 16 * ((8 * group - 13 + 16) // 16) - 16 + TOK * parity
                first = min(max(first, 0), COLS - KEYS)
                last, source = first + KEYS, (grads_ref.at[group], held.at[group])
            elif kind == "corner" and group // 2 == 5 * parity:
                first = 176 * (1 - parity)
                last = first + 16
                source = (
                    corner_ref.at[pl.ds(8 * (group % 2), 8)],
                    held.at[group, :, pl.ds(0, 16)],
                )
            if source is not None:
                to = pair_grad_ref.at[pl.ds(8 * group, 8), pl.ds(first, last - first)]
                loads.append(pltpu.make_async_copy(*source, sems.at[group, 0]))
                stores.append(pltpu.make_async_copy(source[1], to, sems.at[group, 3]))
            if first > 0:
                copies.append(blank(group, 0, first, sems.at[group, 1]))
            if last < COLS:
                copies.append(blank(group, last, COLS, sems.at[group, 2]))
        return copies, loads, stores

    cases = (
        (is_main & (odd == 0), "band", 0),
        (is_main & (odd == 1), "band", 1),
        (is_holder & (odd == 0), "corner", 0),
        (is_holder & (odd == 1), "corner", 1),
        (jnp.logical_not(is_main | is_holder), "none", 0),
    )
    for when, kind, parity in cases:

        @pl.when(when)
        def _():
            copies, loads, stores = pieces(kind, parity)
            for copy in loads + copies:
                copy.start()
            for load, store in zip(loads, stores):
                load.wait()
                store.start()
            for copy in copies + stores:
                copy.wait()

    atom_grad_ref[...] = atom_ref[...]
    proj_grad_ref[...] = proj_ref[...]


def place(grads, corner, atom_grad, proj_grad):
    vmem = pl.BlockSpec(memory_space=pltpu.VMEM)
    any_spec = pl.BlockSpec(memory_space=pl.ANY)
    return pl.pallas_call(
        place_kernel,
        out_shape=(
            jax.ShapeDtypeStruct((TOK, COLS, CP), BF16),
            jax.ShapeDtypeStruct((ATOMS, CP), BF16),
            jax.ShapeDtypeStruct((CA, CP), F32),
        ),
        in_specs=[any_spec, any_spec, vmem, vmem],
        out_specs=(any_spec, vmem, vmem),
        scratch_shapes=[
            pltpu.VMEM((8, COLS, CP), BF16),
            pltpu.VMEM((GROUPS, 8, KEYS, CP), BF16),
            pltpu.SemaphoreType.DMA((GROUPS, 4)),
        ],
        compiler_params=pltpu.CompilerParams(vmem_limit_bytes=VMEM_LIMIT),
        name="place",
    )(grads, corner, atom_grad, proj_grad)


def shards(
    pair_repr,
    pair_gain,
    proj_weight,
    query_weight,
    key_weight,
    mlp_first,
    mlp_second,
    mlp_third,
    atom_feats,
    token_counts,
    key_start,
    pair_cotangent,
):
    grads, corner, atom_grad, proj_grad = band_pass(
        key_start,
        pair_repr,
        pair_cotangent,
        pair_gain.reshape(1, CP),
        proj_weight.T,
        atom_feats,
        token_counts,
        (query_weight.T, key_weight.T, mlp_first, mlp_second, mlp_third),
    )
    pair_grad, atom_grad, proj_grad = place(grads, corner, atom_grad, proj_grad)
    return pair_grad, atom_grad, proj_grad.T


def solution(mesh):
    placed = (
        P("row", "col", None),
        P(),
        P(),
        P(),
        P(),
        P(),
        P(),
        P(),
        P(("row", "col"), None),
        P("row", None),
        P(("row", "col")),
        P(("row", "col"), None),
    )
    return jax.shard_map(
        shards,
        mesh=mesh,
        in_specs=placed,
        out_specs=(P("row", "col", None), P(("row", "col"), None), P()),
        check_vma=False,
    )
```

```python
import jax
import jax.numpy as jnp
from jax import lax
from jax.experimental import pallas as pl
from jax.experimental.pallas import tpu as pltpu
from jax.sharding import PartitionSpec as P

F32 = jnp.float32
BF16 = jnp.bfloat16
MESH = pl.DeviceIdType.MESH

N_ROW = 16
N_COL = 8
TOK = 96
COLS = 192
CP = 128
CA = 16
QBLK = 32
KWIN = 128
MOST = 23
ATOMS = 256
ROW_ATOMS = 2048
SLACK = TOK * MOST - ROW_ATOMS
HALO = KWIN - QBLK
EXT = ATOMS + 2 * HALO
NBLK = ATOMS // QBLK
LANES = QBLK * CA
KEYS = 48
QTOK = 32
GROUPS = TOK // 8
VMEM_LIMIT = 56 * 1024 * 1024
MLP_ROWS = 1024
NEAR = 19
TOKEN_PART = (
    (0, 40, 0, 384),
    (0, 40, 0, 384),
    (0, 32, 0, 512),
    (8, 32, 0, 384),
    (8, 32, 0, 384),
    (0, 32, 0, 512),
    (8, 40, 0, 384),
    (8, 40, 128, 384),
)


def key_base(col):
    return 16 * ((11 * col - 5 + 16) // 16) - 16


def query_base(col):
    return jnp.minimum(8 * ((11 * col) // 8), TOK - QTOK)


def query_base_static(col):
    return min(8 * ((11 * col) // 8), TOK - QTOK)


def iota(shape, dim):
    return lax.broadcasted_iota(jnp.int32, shape, dim)


def dot(a, b):
    return jnp.dot(a, b, preferred_element_type=F32)


def dot_nt(a, b):
    return lax.dot_general(a, b, (((1,), (1,)), ((), ())), preferred_element_type=F32)


def dot_tn(a, b):
    return lax.dot_general(a, b, (((0,), (0,)), ((), ())), preferred_element_type=F32)


def split(x):
    high = x.astype(BF16)
    low = (x - high.astype(F32)).astype(BF16)
    return high, low


def dot_split(x, w):
    high, low = split(x)
    return dot(high, w) + dot(low, w)


def dot_twice(x, w):
    return dot(jnp.concatenate(split(x), axis=1), w)


def sigmoid(x):
    return 0.5 * jnp.tanh(0.5 * x) + 0.5


def mesh_place():
    row = lax.axis_index("row")
    col = lax.axis_index("col")
    return row, col


def normalise(block):
    floats = block.astype(F32)
    centre = floats - jnp.mean(floats, axis=-1, keepdims=True)
    spread = jnp.mean(centre * centre, axis=-1, keepdims=True)
    inv_scale = lax.rsqrt(spread + 1e-05)
    return centre * inv_scale, inv_scale


def channel_eye(rows):
    return ((iota((rows, CA), 0) & (CA - 1)) == iota((rows, CA), 1)).astype(F32).astype(BF16)


def channel_eye_t(lanes):
    return ((iota((CA, lanes), 1) & (CA - 1)) == iota((CA, lanes), 0)).astype(F32).astype(BF16)


def spread_projection(proj):
    eye_t = channel_eye_t(CP)
    wide = dot_tn(proj, eye_t)
    lane = iota((CP, CP), 1) // CA
    return jnp.concatenate(
        [jnp.where(lane == i, wide, 0.0).astype(BF16) for i in range(8)], axis=0
    )


def spread_projection_t(proj):
    eye = channel_eye(CP)
    tall = dot(eye, proj)
    row = iota((CP, CP), 0) // CA
    return jnp.concatenate(
        [jnp.where(row == i, tall, 0.0).astype(BF16) for i in range(8)], axis=1
    )


def window_column(group, odd):
    first = 16 * ((8 * group - 13 + 16) // 16) - 16
    return jnp.clip(first + TOK * odd, 0, COLS - KEYS)


def corner_place(odd):
    return 80 * odd, 176 * (1 - odd)


def swap_groups(pieces, group):
    for bit in (1, 2, 4):
        take = (group & bit) != 0
        swapped = list(pieces)
        for at in range(8):
            if at & bit == 0:
                one, two = pieces[at], pieces[at | bit]
                swapped[at] = jnp.where(take, pltpu.roll(two, CA * bit, 1), one)
                swapped[at | bit] = jnp.where(take, two, pltpu.roll(one, 128 - CA * bit, 1))
        pieces = swapped
    return pieces


def neighbours(row, col):
    ahead = (
        jnp.where(col == N_COL - 1, lax.rem(row + 1, N_ROW), row),
        lax.rem(col + 1, N_COL),
    )
    behind = (
        jnp.where(col == 0, lax.rem(row + N_ROW - 1, N_ROW), row),
        lax.rem(col + N_COL - 1, N_COL),
    )
    return ahead, behind


def like_places(row, col):
    return [(lax.rem(row + step, N_ROW), col) for step in range(1, N_ROW)]


def band_kernel(
    start_ref,
    pair_ref,
    cot_hbm,
    gain_hbm,
    proj_hbm,
    feats_hbm,
    counts_hbm,
    query_w_hbm,
    key_w_hbm,
    first_w_hbm,
    second_w_hbm,
    third_w_hbm,
    grads_hbm,
    corner_grads_hbm,
    atom_grad_ref,
    proj_grad_ref,
    gain_ref,
    proj_ref,
    feats_ref,
    counts_ref,
    query_w_ref,
    key_w_ref,
    first_w_ref,
    second_w_ref,
    third_w_ref,
    grads,
    corner_grads,
    band,
    corner_band,
    zrow,
    zcorner,
    patch,
    patch_corner,
    raw,
    feats_before,
    feats_after,
    counts_before,
    counts_after,
    cot_ref,
    act_ext,
    rhs,
    query_high,
    query_low,
    spread,
    cot,
    state,
    mixers,
    key_tiled,
    query_tiled,
    slot_from,
    slot_to,
    hot_ref,
    key_sum,
    query_sum,
    token_sum,
    key_before,
    key_after,
    patches,
    token_corner,
    tokens,
    near_flat,
    near_high,
    near_low,
    weight_sent,
    weight_row,
    weight_grid,
    small_sems,
    load_sems,
    cot_sem,
    corner_load_sem,
    send_z,
    recv_z,
    send_c,
    recv_c,
    send_r,
    recv_r,
    send_rc,
    recv_rc,
    send_h,
    recv_h,
    send_t,
    recv_t,
    send_tc,
    recv_tc,
    send_k,
    recv_k,
    send_wr,
    recv_wr,
    send_wg,
    recv_wg,
):
    row = lax.axis_index("row")
    col = lax.axis_index("col")
    odd = row % 2
    half = row // 2
    is_main = col == half
    not_main = col != half
    holder = jnp.where(odd == 0, half - 1, half + 1)
    reader = (N_COL - 1) * odd
    exists = (holder >= 0) & (holder < N_COL)
    is_holder = exists & (col == holder)
    is_reader = exists & (col == reader)
    same_device = holder == reader
    other_device = holder != reader
    holder_col = jnp.clip(holder, 0, N_COL - 1)
    ahead, behind = neighbours(row, col)
    along_grid = like_places(row, col)
    along_row = [(row, lax.rem(col + step, N_COL)) for step in range(1, N_COL)]

    def remote(src, dst, send, recv, device):
        return pltpu.make_async_remote_copy(
            src_ref=src,
            dst_ref=dst,
            send_sem=send,
            recv_sem=recv,
            device_id=device,
            device_id_type=MESH,
        )

    raw[...] = jnp.zeros_like(raw)

    barrier = pltpu.get_barrier_semaphore()

    def greet(device):
        pl.semaphore_signal(barrier, inc=1, device_id=device, device_id_type=MESH)

    @pl.when(col == 0)
    def _():
        greet(behind)

    @pl.when(col == N_COL - 1)
    def _():
        greet(ahead)

    for device in along_row + along_grid:
        greet(device)
    greeted = N_COL + N_ROW - 2 + jnp.where((col == 0) | (col == N_COL - 1), 1, 0)

    def window_copy(group):
        first = pl.multiple_of(window_column(group, odd), 16)
        return pltpu.make_async_copy(
            pair_ref.at[pl.ds(8 * group, 8), pl.ds(first, KEYS)],
            band.at[group],
            load_sems.at[group],
        )

    first_row, first_col = corner_place(odd)
    corner_load = pltpu.make_async_copy(
        pair_ref.at[pl.ds(first_row, 16), pl.ds(pl.multiple_of(first_col, 16), 16)],
        corner_band,
        corner_load_sem,
    )
    cot_load = pltpu.make_async_copy(cot_hbm, cot_ref, cot_sem)

    @pl.when(is_main)
    def _():
        for group in range(GROUPS):
            window_copy(group).start()

    @pl.when(is_holder)
    def _():
        corner_load.start()

    cot_load.start()
    smalls = [
        pltpu.make_async_copy(src, dst, small_sems.at[at])
        for at, (src, dst) in enumerate(
            (
                (gain_hbm, gain_ref),
                (proj_hbm, proj_ref),
                (feats_hbm, feats_ref),
                (counts_hbm, counts_ref),
                (query_w_hbm, query_w_ref),
                (key_w_hbm, key_w_ref),
                (first_w_hbm, first_w_ref),
                (second_w_hbm, second_w_ref),
                (third_w_hbm, third_w_ref),
            )
        )
    ]
    for copy in smalls:
        copy.start()
    for copy in smalls:
        copy.wait()

    @pl.when(is_main)
    def _():
        zrow[...] = jnp.zeros_like(zrow)
        spread_w = spread_projection(proj_ref[...])
        gain = gain_ref[...]

        def project(group, carry):
            window_copy(group).wait()
            hatted, _ = normalise(band[group])
            normed = (hatted * gain).astype(BF16)
            rows = jnp.concatenate([normed[i] for i in range(8)], axis=1)
            at = pl.multiple_of(window_column(group, odd) - TOK * odd + 16, 16)
            lanes = pl.ds(pl.multiple_of(128 * group, 128), 128)
            zrow[pl.ds(at, KEYS), lanes] = dot(rows, spread_w).astype(BF16)
            return carry

        lax.fori_loop(0, GROUPS, project, 0)

    @pl.when(is_holder)
    def _():
        spread_w = spread_projection(proj_ref[...])
        corner_load.wait()
        hatted, _ = normalise(corner_band[...])
        normed = (hatted * gain_ref[...]).astype(BF16)
        for part in range(2):
            rows = jnp.concatenate([normed[8 * part + i] for i in range(8)], axis=1)
            zcorner[:, 128 * part : 128 * part + 128] = dot(rows, spread_w).astype(BF16)

    cot_load.wait()

    group = iota((16, 128), 1) // CA

    def spread_step(eight, carry):
        rows = cot_ref[pl.ds(pl.multiple_of(16 * eight, 16), 16), :].astype(F32)
        for half in range(2):
            at = pl.multiple_of(256 * eight + 128 * half, 128)
            for chunk in range(16):
                spread[pl.ds(at + 8 * chunk, 8), :] = rows[
                    8 * half : 8 * half + 8, 128 * chunk : 128 * chunk + 128
                ]
        return carry

    lax.fori_loop(0, ATOMS // 16, spread_step, 0, unroll=2)

    pl.semaphore_wait(barrier, greeted)

    def z_part(target, first):
        return zrow.at[pl.ds(key_base(target) + 16, KEYS), pl.ds(first, QTOK * CA)]

    def z_copy(target):
        src = z_part(target, query_base_static(target) * CA)
        return remote(src, patch, send_z.at[target], recv_z, (row, target))

    corner_copy = remote(zcorner, patch_corner, send_c, recv_c, (row, reader))

    def raw_parts(target):
        rows = pl.ds(11 * target, NEAR)
        to_rows = pl.ds(11 * target - query_base_static(target), NEAR)
        first = key_base(target)

        def part(skip, width, parity):
            src = pair_ref.at[rows, pl.ds(first + skip + TOK * parity, width)]
            return src, raw.at[to_rows, pl.ds(skip, width)]

        return [
            (odd == parity, *part(16 if cut_low else 0, KEYS - 16 if cut_low or cut_high else KEYS, parity))
            for parity in range(2)
            for cut_low in (first + TOK * parity < 0,)
            for cut_high in (first + TOK * parity + KEYS > COLS,)
        ]

    def for_raw(target, act):
        for when, src, dst in raw_parts(target):

            @pl.when(when & (col != target))
            def _():
                act(remote(src, dst, send_r.at[target], recv_r, (row, target)), True)

            @pl.when(when & (col == target))
            def _():
                act(pltpu.make_async_copy(src, dst, recv_r), False)

    raw_corner_src = pair_ref.at[
        pl.ds(first_row, 16), pl.ds(pl.multiple_of(first_col, 16), 16)
    ]
    raw_corner_dst = raw.at[pl.ds(16 * odd, 16), pl.ds(pl.multiple_of(32 * odd, 16), 16)]
    raw_corner_copy = remote(raw_corner_src, raw_corner_dst, send_rc, recv_rc, (row, reader))
    raw_corner_local = pltpu.make_async_copy(raw_corner_src, raw_corner_dst, recv_rc)

    @pl.when(is_main)
    def _():
        for target in range(N_COL):

            @pl.when(col != target)
            def _():
                z_copy(target).start()

        patch[...] = zrow[
            pl.ds(pl.multiple_of(key_base(col) + 16, 16), KEYS),
            pl.ds(pl.multiple_of(query_base(col) * CA, 128), QTOK * CA),
        ]

    @pl.when(is_holder & other_device)
    def _():
        corner_copy.start()
        raw_corner_copy.start()

    @pl.when(is_holder & same_device)
    def _():
        patch_corner[...] = zcorner[...]
        raw_corner_local.start()

    halos = [
        remote(src, dst, send_h.at[at], recv_h.at[at], device)
        for at, (src, dst, device) in enumerate(
            (
                (feats_hbm.at[pl.ds(ATOMS - HALO, HALO)], feats_before, ahead),
                (feats_hbm.at[pl.ds(0, HALO)], feats_after, behind),
                (counts_hbm, counts_before, ahead),
                (counts_hbm, counts_after, behind),
            )
        )
    ]
    halos[0].start()
    halos[1].start()

    @pl.when(col == N_COL - 1)
    def _():
        halos[2].start()

    @pl.when(col == 0)
    def _():
        halos[3].start()

    @pl.when(is_main)
    def _():
        for target in range(N_COL):
            for_raw(target, lambda copy, far: copy.start())

    eye = channel_eye(LANES)
    eye16 = eye[:256]
    same = (iota((256, 256), 0) // CA) == (iota((256, 256), 1) // CA)

    def mixer(weight, flip):
        left = dot_nt(eye16, weight) if flip else dot(eye16, weight)
        wide = dot_nt(left.astype(BF16), eye16)
        wide = jnp.where(same, wide, 0.0).astype(BF16)
        return jnp.concatenate([wide, wide], axis=0)

    mixers[0] = mixer(first_w_ref[...], False)
    mixers[1] = mixer(second_w_ref[...], False)
    mixers[2] = mixer(third_w_ref[...], True)
    mixers[3] = mixer(second_w_ref[...], True)
    mixers[4] = mixer(first_w_ref[...], True)
    key_tiled[...] = dot(eye, key_w_ref[...]).astype(BF16)
    query_tiled[...] = dot(eye, query_w_ref[...]).astype(BF16)
    eye_t = channel_eye_t(LANES)
    rhs[0:16, :] = jnp.zeros((16, LANES), BF16)
    rhs[16:144, :] = dot_tn(key_w_ref[...], eye_t).astype(BF16)

    def activate(feats):
        floats = feats.astype(F32)
        return floats * jax.nn.sigmoid(floats)

    own_act = activate(feats_ref[...]).astype(BF16)
    act_ext[HALO : HALO + ATOMS] = activate(feats_ref[...])

    lane_is_row = iota((QBLK, LANES), 1) // CA == iota((QBLK, LANES), 0)
    query_wide = dot_tn(query_w_ref[...], eye_t).astype(BF16)
    for block in range(NBLK):
        terms = dot(own_act[QBLK * block : QBLK * block + QBLK], query_wide)
        high, low = split(jnp.where(lane_is_row, terms, 0.0))
        query_high[QBLK * block : QBLK * block + QBLK] = high
        query_low[QBLK * block : QBLK * block + QBLK] = low

    own = counts_ref[...].astype(F32)

    def rows_of(counts, rows):
        return jnp.broadcast_to(counts, (rows, TOK)).astype(BF16)

    def as_mask(flag):
        return jnp.where(flag, 1.0, 0.0).astype(BF16)

    first_query = query_base(col)
    slot = iota((LANES, TOK), 0) // CA + first_query
    slot_index = iota((LANES, TOK), 1)
    own_rows = rows_of(own, 128)
    slot_from[...] = dot_nt(as_mask(slot_index < slot), own_rows)
    slot_to[...] = dot_nt(as_mask(slot_index < slot + 1), own_rows)

    lane_atom_row = (iota((1, LANES), 1) // CA).astype(F32)
    channel_match = (iota((256, 128), 0) % CA) == (iota((256, 128), 1) % CA)

    def block_place(block):
        first = col * ATOMS + block * QBLK
        token = 8 * (first // (8 * MOST)) - first_query
        return first, pl.multiple_of(token * CA, 128)

    def query_hot(block):
        first, at = block_place(block)
        low = slot_from[pl.ds(at, 256), :]
        high = slot_to[pl.ds(at, 256), :]
        parts = []
        for part in range(4):
            atom = lane_atom_row[:, 128 * part : 128 * part + 128] + first.astype(F32)
            hot = (low <= atom) & (atom < high) & channel_match
            parts.append(jnp.where(hot, 1.0, 0.0).astype(BF16))
        return jnp.concatenate(parts, axis=1)

    def key_first(block):
        return col * ATOMS + block * QBLK + start_ref[block]

    def hot_step(block, carry):
        hot_ref[block] = query_hot(block)
        return carry

    lax.fori_loop(0, NBLK, hot_step, 0, unroll=2)

    def swap_step(eight, carry):
        at = 128 * eight
        pieces = [spread[pl.ds(at + atom, 16, stride=8), :] for atom in range(8)]
        pieces = swap_groups(pieces, group)
        to = NBLK * KWIN * (eight % 4) + KWIN * (eight // 4)
        for key in range(8):
            cot[pl.ds(to + key, 16, stride=8), :] = pieces[key]
        return carry

    lax.fori_loop(0, ATOMS // 8, swap_step, 0, unroll=4)

    halos[0].wait()
    halos[1].wait()

    @pl.when(col == N_COL - 1)
    def _():
        halos[2].wait_send()
        halos[3].wait_recv()

    @pl.when(col == 0)
    def _():
        halos[3].wait_send()
        halos[2].wait_recv()

    act_ext[0:HALO] = activate(feats_before[...])
    act_ext[HALO + ATOMS : EXT] = activate(feats_after[...])

    base = key_base(col)
    before = jnp.where(col == 0, counts_before[...], counts_ref[...]).astype(F32)
    after = jnp.where(col == N_COL - 1, counts_after[...], counts_ref[...]).astype(F32)

    def lane_bounds(offset):
        token = iota((TOK, 128), 1) + (base + offset)
        index = iota((TOK, 128), 0)
        total = dot(rows_of(own, 8), as_mask(index < token))
        total += dot(rows_of(after, 8), as_mask(index + TOK < token))
        return total - dot(rows_of(before, 8), as_mask(index - TOK >= token))

    def column_bounds(offset):
        token = iota((KEYS, TOK), 0) + (base + offset)
        index = iota((KEYS, TOK), 1)
        total = dot_nt(as_mask(index < token), rows_of(own, 128))
        total += dot_nt(as_mask(index + TOK < token), rows_of(after, 128))
        return total - dot_nt(as_mask(index - TOK >= token), rows_of(before, 128))

    lane = iota((8, 128), 1)
    far = 1.0e6
    lane_from = jnp.where(lane < 48, lane_bounds(0), jnp.where(lane < 112, -far, far))[0:1]
    lane_to = jnp.where(lane < 48, lane_bounds(1), jnp.where(lane < 112, far, -far))[0:1]
    column_from = column_bounds(0)
    column_to = column_bounds(1)

    @pl.when(is_main)
    def _():
        for target in range(N_COL):

            @pl.when(col != target)
            def _():
                z_copy(target).wait_send()

    @pl.when(not_main)
    def _():
        z_copy(0).wait_recv()

    @pl.when(is_holder & other_device)
    def _():
        corner_copy.wait_send()

    @pl.when(is_reader & other_device)
    def _():
        corner_copy.wait_recv()

    @pl.when(is_reader)
    def _():
        at = pl.multiple_of(32 * odd, 16), pl.multiple_of(256 * odd, 128)
        patch[pl.ds(at[0], 16), pl.ds(at[1], 256)] = patch_corner[...]

    def start_step(block, carry):
        _, at = block_place(block)
        hot = hot_ref[block]
        window = start_ref[block] + block * QBLK + HALO
        atom = (iota((KWIN, 128), 0) + key_first(block)).astype(F32)
        mine = pl.ds(pl.multiple_of(block * QBLK, QBLK), QBLK)
        left = jnp.concatenate(
            [
                as_mask((lane_from <= atom) & (atom < lane_to)),
                act_ext[pl.ds(window, KWIN), :].astype(BF16),
            ],
            axis=1,
        )
        right = jnp.concatenate(
            [
                dot(patch[:, pl.ds(at, 256)], hot).astype(BF16),
                query_high[mine, :],
                query_low[mine, :],
                rhs[...],
            ],
            axis=0,
        )
        state[pl.ds(pl.multiple_of(block * KWIN, KWIN), KWIN), :] = dot(left, right)
        return carry

    lax.fori_loop(0, NBLK, start_step, 0, unroll=2)

    atom_low = jnp.where(row == 0, 0, -ROW_ATOMS)
    atom_high = jnp.where(row == N_ROW - 1, ROW_ATOMS, 2 * ROW_ATOMS)

    def slope(value, sigma, act):
        return sigma + act - act * sigma

    def mlp_step(step, carry):
        at = pl.multiple_of(MLP_ROWS * (step // 2), MLP_ROWS)
        place = pl.ds(at, MLP_ROWS), pl.ds(pl.multiple_of(256 * (step % 2), 256), 256)
        value = state[place]
        index = iota((KWIN, 256), 0)
        atom = jnp.concatenate(
            [
                index + key_first(MLP_ROWS // KWIN * (step // 2) + block)
                for block in range(MLP_ROWS // KWIN)
            ],
            axis=0,
        )
        parts = [
            cot[pl.ds(pl.multiple_of(at + NBLK * KWIN * (2 * (step % 2) + part), MLP_ROWS), MLP_ROWS), :]
            for part in range(2)
        ]
        grad = jnp.concatenate(parts, axis=1)
        grad = jnp.where((atom >= atom_low) & (atom < atom_high), grad, 0.0)
        sig_0 = sigmoid(value)
        act_0 = value * sig_0
        one = dot_twice(act_0, mixers[0])
        sig_1 = sigmoid(one)
        act_1 = one * sig_1
        two = dot_twice(act_1, mixers[1])
        sig_2 = sigmoid(two)
        back = dot(grad.astype(BF16), mixers[2, 0:256]) * slope(two, sig_2, two * sig_2)
        back = dot(back.astype(BF16), mixers[3, 0:256]) * slope(one, sig_1, act_1)
        back = dot(back.astype(BF16), mixers[4, 0:256]) * slope(value, sig_0, act_0)
        state[place] = grad + back
        return carry

    lax.fori_loop(0, 2 * NBLK * KWIN // MLP_ROWS, mlp_step, 0)

    key_sum[...] = jnp.zeros_like(key_sum)
    token_sum[...] = jnp.zeros_like(token_sum)

    def sum_step(block, carry):
        _, at = block_place(block)
        window = start_ref[block] + block * QBLK + HALO
        back = state[pl.ds(pl.multiple_of(block * KWIN, KWIN), KWIN), :]
        high, low = split(back)
        by_key = dot(high, key_tiled[...]) + dot(low, key_tiled[...])
        reach = KWIN + HALO
        moved = as_mask(
            iota((reach, KWIN), 0) == iota((reach, KWIN), 1) + (start_ref[block] + HALO)
        )
        by_key_high, by_key_low = split(by_key)
        key_sum[pl.ds(pl.multiple_of(block * QBLK, QBLK), reach), :] += dot(
            moved, by_key_high
        ) + dot(moved, by_key_low)
        over_keys = jnp.sum(back, axis=0, keepdims=True)
        over_keys = jnp.where(lane_is_row, over_keys, 0.0)
        mine = pl.multiple_of(block * QBLK, QBLK)
        query_sum[pl.ds(mine, QBLK), :] = dot_split(over_keys, query_tiled[...])
        atom = (iota((KEYS, 128), 1) + key_first(block)).astype(F32)
        key_hot = as_mask((column_from <= atom) & (atom < column_to))
        by_token = dot(key_hot, high) + dot(key_hot, low)
        high, low = split(by_token)
        hot = hot_ref[block]
        token_sum[:, pl.ds(at, 256)] += dot_nt(high, hot) + dot_nt(low, hot)
        return carry

    lax.fori_loop(0, NBLK, sum_step, 0, unroll=2)

    def token_copy(source):
        row_at, row_count, lane_at, lane_count = TOKEN_PART[source]
        part = pl.ds(row_at, row_count), pl.ds(lane_at, lane_count)
        return remote(
            token_sum.at[part], patches.at[(source, *part)], send_t, recv_t.at[source], (row, half)
        )

    corner_part = token_sum.at[
        pl.ds(pl.multiple_of(32 * odd, 16), 16), pl.ds(pl.multiple_of(256 * odd, 128), 256)
    ]
    token_corner_copy = remote(corner_part, token_corner, send_tc, recv_tc, (row, holder_col))

    for source in range(N_COL):

        @pl.when(not_main & (col == source))
        def _():
            token_copy(source).start()

    @pl.when(is_reader & other_device)
    def _():
        token_corner_copy.start()

    @pl.when(is_reader & same_device)
    def _():
        token_corner[...] = corner_part[...]

    key_halos = [
        remote(src, dst, send_k.at[at], recv_k.at[at], device)
        for at, (src, dst, device) in enumerate(
            (
                (key_sum.at[pl.ds(HALO + ATOMS, HALO)], key_before, ahead),
                (key_sum.at[pl.ds(0, HALO)], key_after, behind),
            )
        )
    ]
    for copy in key_halos:
        copy.start()

    @pl.when(is_main)
    def _():
        for target in range(N_COL):
            for_raw(target, lambda copy, far: copy.wait_send() if far else copy.wait())

    for target in range(N_COL):

        for when, src, dst in raw_parts(target):

            @pl.when(when & not_main & (col == target))
            def _():
                remote(src, dst, send_r.at[target], recv_r, (row, target)).wait_recv()

    @pl.when(is_reader & other_device)
    def _():
        raw_corner_copy.wait_recv()

    @pl.when(is_reader & same_device)
    def _():
        raw_corner_local.wait()

    gain = gain_ref[...]

    def near_step(eight, carry):
        hatted, _ = normalise(raw[pl.ds(8 * eight, 8)])
        normed = (hatted * gain).astype(BF16)
        rows = pl.ds(pl.multiple_of(KEYS * eight, 16), KEYS)
        near_flat[rows, :] = jnp.concatenate([normed[i] for i in range(8)], axis=1)
        high, low = split(token_sum[:, pl.ds(pl.multiple_of(128 * eight, 128), 128)])
        near_high[rows, :] = high
        near_low[rows, :] = low
        return carry

    lax.fori_loop(0, QTOK // 8, near_step, 0, unroll=2)
    wide = dot_tn(near_high[...], near_flat[...]) + dot_tn(near_low[...], near_flat[...])
    weight = wide[0:CA, 0:128]
    for i in range(1, 8):
        weight += wide[CA * i : CA * i + CA, 128 * i : 128 * i + 128]
    weight_sent[0] = weight
    row_copies = [
        remote(weight_sent.at[0], weight_row.at[at], send_wr.at[at], recv_wr.at[at], device)
        for at, device in enumerate(along_row)
    ]
    grid_copies = [
        remote(weight_sent.at[1], weight_grid.at[at], send_wg.at[at], recv_wg.at[at], device)
        for at, device in enumerate(along_grid)
    ]
    for copy in row_copies:
        copy.start()
    for at, copy in enumerate(row_copies):
        copy.wait_recv()
        weight += weight_row[at]
    weight_sent[1] = weight
    for copy in grid_copies:
        copy.start()

    spread_wt = spread_projection_t(proj_ref[...])

    def gradient(block, token_rows):
        high, low = split(token_rows)
        hatted, inv_scale = normalise(block)
        wide = dot(high, spread_wt) + dot(low, spread_wt)
        scaled = jnp.stack([wide[:, 128 * i : 128 * i + 128] for i in range(8)]) * gain
        first_mean = jnp.mean(scaled, axis=-1, keepdims=True)
        second_mean = jnp.mean(scaled * hatted, axis=-1, keepdims=True)
        return (inv_scale * (scaled - first_mean - hatted * second_mean)).astype(BF16)

    def grad_out(group):
        return pltpu.make_async_copy(grads.at[group], grads_hbm.at[group], load_sems.at[group])

    corner_out = pltpu.make_async_copy(corner_grads, corner_grads_hbm, corner_load_sem)

    def grad_step(group, carry):
        at = pl.multiple_of(window_column(group, odd) - TOK * odd + 16, 16)
        lanes = pl.ds(pl.multiple_of(128 * group, 128), 128)
        grads[group] = gradient(band[group], tokens[pl.ds(at, KEYS), lanes])
        grad_out(group).start()
        return carry

    @pl.when(is_main)
    def _():
        tokens[...] = jnp.zeros_like(tokens)
        for source in range(N_COL):
            row_at, row_count, lane_at, lane_count = TOKEN_PART[source]
            part = pl.ds(row_at, row_count), pl.ds(lane_at, lane_count)

            @pl.when(col != source)
            def _():
                token_copy(source).wait_recv()

            @pl.when(col == source)
            def _():
                patches[(source, *part)] = token_sum[part]

            at = key_base(source) + 16 + row_at
            lanes = query_base_static(source) * CA + lane_at
            tokens[at : at + row_count, lanes : lanes + lane_count] += patches[(source, *part)]
        lax.fori_loop(0, GROUPS // 2, grad_step, 0, unroll=2)

    @pl.when(is_holder)
    def _():
        @pl.when(other_device)
        def _():
            token_corner_copy.wait_recv()

        for part in range(2):
            corner_grads[8 * part : 8 * part + 8] = gradient(
                corner_band[8 * part : 8 * part + 8],
                token_corner[:, 128 * part : 128 * part + 128],
            )
        corner_out.start()

    @pl.when(is_main)
    def _():
        lax.fori_loop(GROUPS // 2, GROUPS, grad_step, 0, unroll=2)

    for copy in key_halos:
        copy.wait()
    total = query_sum[...] + key_sum[HALO : HALO + ATOMS]
    lead = total[:HALO] + key_before[...]
    trail = total[ATOMS - HALO :] + key_after[...]
    total = jnp.concatenate([lead, total[HALO : ATOMS - HALO], trail], axis=0)
    floats = feats_ref[...].astype(F32)
    sigma = jax.nn.sigmoid(floats)
    atom_grad_ref[...] = (total * (sigma * (1.0 + floats * (1.0 - sigma)))).astype(BF16)

    for at, copy in enumerate(grid_copies):
        copy.wait_recv()
        weight += weight_grid[at]
    proj_grad_ref[...] = weight

    for copy in row_copies + grid_copies:
        copy.wait_send()

    for source in range(N_COL):

        @pl.when(not_main & (col == source))
        def _():
            token_copy(source).wait_send()

    @pl.when(is_reader & other_device)
    def _():
        token_corner_copy.wait_send()

    @pl.when(is_holder & other_device)
    def _():
        raw_corner_copy.wait_send()

    @pl.when(is_main)
    def _():
        def grad_wait(group, carry):
            grad_out(group).wait()
            return carry

        lax.fori_loop(0, GROUPS, grad_wait, 0)

    @pl.when(is_holder)
    def _():
        corner_out.wait()


def band_pass(start, pair_repr, cot, gain, proj, feats, counts, weights):
    vmem = pl.BlockSpec(memory_space=pltpu.VMEM)
    any_spec = pl.BlockSpec(memory_space=pl.ANY)
    dma = pltpu.SemaphoreType.DMA
    return pl.pallas_call(
        band_kernel,
        out_shape=(
            jax.ShapeDtypeStruct((GROUPS, 8, KEYS, CP), BF16),
            jax.ShapeDtypeStruct((16, 16, CP), BF16),
            jax.ShapeDtypeStruct((ATOMS, CP), BF16),
            jax.ShapeDtypeStruct((CA, CP), F32),
        ),
        in_specs=[pl.BlockSpec(memory_space=pltpu.SMEM)] + [any_spec] * 11,
        out_specs=(any_spec, any_spec, vmem, vmem),
        scratch_shapes=[
            pltpu.VMEM((1, CP), F32),
            pltpu.VMEM((CA, CP), BF16),
            pltpu.VMEM((ATOMS, CP), BF16),
            pltpu.VMEM((1, TOK), jnp.int32),
            pltpu.VMEM((CA, CP), BF16),
            pltpu.VMEM((CA, CP), BF16),
            pltpu.VMEM((CA, CA), BF16),
            pltpu.VMEM((CA, CA), BF16),
            pltpu.VMEM((CA, CA), BF16),
            pltpu.VMEM((GROUPS, 8, KEYS, CP), BF16),
            pltpu.VMEM((16, 16, CP), BF16),
            pltpu.VMEM((GROUPS, 8, KEYS, CP), BF16),
            pltpu.VMEM((16, 16, CP), BF16),
            pltpu.VMEM((128, TOK * CA), BF16),
            pltpu.VMEM((16, 256), BF16),
            pltpu.VMEM((KEYS, QTOK * CA), BF16),
            pltpu.VMEM((16, 256), BF16),
            pltpu.VMEM((QTOK, KEYS, CP), BF16),
            pltpu.VMEM((HALO, CP), BF16),
            pltpu.VMEM((HALO, CP), BF16),
            pltpu.VMEM((1, TOK), jnp.int32),
            pltpu.VMEM((1, TOK), jnp.int32),
            pltpu.VMEM((ATOMS, KWIN * CA), BF16),
            pltpu.VMEM((EXT, CP), F32),
            pltpu.VMEM((144, LANES), BF16),
            pltpu.VMEM((ATOMS, LANES), BF16),
            pltpu.VMEM((ATOMS, LANES), BF16),
            pltpu.VMEM((ATOMS * 16, 128), F32),
            pltpu.VMEM((4 * NBLK * KWIN, 128), F32),
            pltpu.VMEM((NBLK * KWIN, LANES), F32),
            pltpu.VMEM((5, 512, 256), BF16),
            pltpu.VMEM((LANES, CP), BF16),
            pltpu.VMEM((LANES, CP), BF16),
            pltpu.VMEM((LANES, 128), F32),
            pltpu.VMEM((LANES, 128), F32),
            pltpu.VMEM((NBLK, 256, LANES), BF16),
            pltpu.VMEM((EXT, CP), F32),
            pltpu.VMEM((ATOMS, CP), F32),
            pltpu.VMEM((KEYS, QTOK * CA), F32),
            pltpu.VMEM((HALO, CP), F32),
            pltpu.VMEM((HALO, CP), F32),
            pltpu.VMEM((N_COL, KEYS, QTOK * CA), F32),
            pltpu.VMEM((16, 256), F32),
            pltpu.VMEM((128, TOK * CA), F32),
            pltpu.VMEM((QTOK // 8 * KEYS, 8 * CP), BF16),
            pltpu.VMEM((QTOK // 8 * KEYS, 128), BF16),
            pltpu.VMEM((QTOK // 8 * KEYS, 128), BF16),
            pltpu.VMEM((2, CA, CP), F32),
            pltpu.VMEM((N_COL - 1, CA, CP), F32),
            pltpu.VMEM((N_ROW - 1, CA, CP), F32),
            dma((9,)),
            dma((GROUPS,)),
            dma,
            dma,
            dma((N_COL,)),
            dma,
            dma,
            dma,
            dma((N_COL,)),
            dma,
            dma,
            dma,
            dma((4,)),
            dma((4,)),
            dma,
            dma((N_COL,)),
            dma,
            dma,
            dma((2,)),
            dma((2,)),
            dma((N_COL - 1,)),
            dma((N_COL - 1,)),
            dma((N_ROW - 1,)),
            dma((N_ROW - 1,)),
        ],
        compiler_params=pltpu.CompilerParams(
            collective_id=0, has_side_effects=True, vmem_limit_bytes=VMEM_LIMIT
        ),
        name="band_pass",
    )(start, pair_repr, cot, gain, proj, feats, counts, *weights)


def place_kernel(
    grads_ref,
    corner_ref,
    atom_ref,
    proj_ref,
    pair_grad_ref,
    atom_grad_ref,
    proj_grad_ref,
    zeros,
    held,
    sems,
):
    row = lax.axis_index("row")
    col = lax.axis_index("col")
    odd = row % 2
    half = row // 2
    is_main = col == half
    holder = jnp.where(odd == 0, half - 1, half + 1)
    is_holder = col == holder
    zeros[...] = jnp.zeros_like(zeros)

    def blank(group, first, last, sem):
        return pltpu.make_async_copy(
            zeros.at[:, pl.ds(0, last - first)],
            pair_grad_ref.at[pl.ds(8 * group, 8), pl.ds(first, last - first)],
            sem,
        )

    def pieces(kind, parity):
        copies, loads, stores = [], [], []
        for group in range(GROUPS):
            first, last, source = 0, 0, None
            if kind == "band":
                first = 16 * ((8 * group - 13 + 16) // 16) - 16 + TOK * parity
                first = min(max(first, 0), COLS - KEYS)
                last, source = first + KEYS, (grads_ref.at[group], held.at[group])
            elif kind == "corner" and group // 2 == 5 * parity:
                first = 176 * (1 - parity)
                last = first + 16
                source = (
                    corner_ref.at[pl.ds(8 * (group % 2), 8)],
                    held.at[group, :, pl.ds(0, 16)],
                )
            if source is not None:
                to = pair_grad_ref.at[pl.ds(8 * group, 8), pl.ds(first, last - first)]
                loads.append(pltpu.make_async_copy(*source, sems.at[group, 0]))
                stores.append(pltpu.make_async_copy(source[1], to, sems.at[group, 3]))
            if first > 0:
                copies.append(blank(group, 0, first, sems.at[group, 1]))
            if last < COLS:
                copies.append(blank(group, last, COLS, sems.at[group, 2]))
        return copies, loads, stores

    cases = (
        (is_main & (odd == 0), "band", 0),
        (is_main & (odd == 1), "band", 1),
        (is_holder & (odd == 0), "corner", 0),
        (is_holder & (odd == 1), "corner", 1),
        (jnp.logical_not(is_main | is_holder), "none", 0),
    )
    for when, kind, parity in cases:

        @pl.when(when)
        def _():
            copies, loads, stores = pieces(kind, parity)
            for copy in loads + copies:
                copy.start()
            for load, store in zip(loads, stores):
                load.wait()
                store.start()
            for copy in copies + stores:
                copy.wait()

    atom_grad_ref[...] = atom_ref[...]
    proj_grad_ref[...] = proj_ref[...]


def place(grads, corner, atom_grad, proj_grad):
    vmem = pl.BlockSpec(memory_space=pltpu.VMEM)
    any_spec = pl.BlockSpec(memory_space=pl.ANY)
    return pl.pallas_call(
        place_kernel,
        out_shape=(
            jax.ShapeDtypeStruct((TOK, COLS, CP), BF16),
            jax.ShapeDtypeStruct((ATOMS, CP), BF16),
            jax.ShapeDtypeStruct((CA, CP), F32),
        ),
        in_specs=[any_spec, any_spec, vmem, vmem],
        out_specs=(any_spec, vmem, vmem),
        scratch_shapes=[
            pltpu.VMEM((8, COLS, CP), BF16),
            pltpu.VMEM((GROUPS, 8, KEYS, CP), BF16),
            pltpu.SemaphoreType.DMA((GROUPS, 4)),
        ],
        compiler_params=pltpu.CompilerParams(vmem_limit_bytes=VMEM_LIMIT),
        name="place",
    )(grads, corner, atom_grad, proj_grad)


def shards(
    pair_repr,
    pair_gain,
    proj_weight,
    query_weight,
    key_weight,
    mlp_first,
    mlp_second,
    mlp_third,
    atom_feats,
    token_counts,
    key_start,
    pair_cotangent,
):
    grads, corner, atom_grad, proj_grad = band_pass(
        key_start,
        pair_repr,
        pair_cotangent,
        pair_gain.reshape(1, CP),
        proj_weight.T,
        atom_feats,
        token_counts,
        (query_weight.T, key_weight.T, mlp_first, mlp_second, mlp_third),
    )
    pair_grad, atom_grad, proj_grad = place(grads, corner, atom_grad, proj_grad)
    return pair_grad, atom_grad, proj_grad.T


def solution(mesh):
    placed = (
        P("row", "col", None),
        P(),
        P(),
        P(),
        P(),
        P(),
        P(),
        P(),
        P(("row", "col"), None),
        P("row", None),
        P(("row", "col")),
        P(("row", "col"), None),
    )
    return jax.shard_map(
        shards,
        mesh=mesh,
        in_specs=placed,
        out_specs=(P("row", "col", None), P(("row", "col"), None), P()),
        check_vma=False,
    )
```
